512 devices in a mesh: face: 8 (over x, y_lo), tile: 64 (over z, y_hi, core).
Axes of the slice: x: 4, y: 4 (y_hi: 2, y_lo: 2; y = y_hi * 2 + y_lo), z: 16, core: 2. Of those that a mesh axis runs over, the one named last changes fastest.
Arguments:
- maps: bfloat16 [4, 4, 128, 8192], P(None, None, 'face', 'tile'), may hold values from -8 to 8
- params: float32 [4, 2], replicated, may hold values from 0 to 1
- labels: int32 [4], replicated, may hold values 0 or 1
- edge_flip: int32 [8, 64], replicated, may hold values from 0 to 1
- fine_weight: float32 [3, 4, 16], replicated, may hold values from -1.75 to 1.75
- coarse_weight: float32 [3, 16, 32], replicated, may hold values from -0.875 to 0.875
- feature_weight: float32 [32, 128], replicated, may hold values from -2 to 2
- param_weight: float32 [2, 128], replicated, may hold values from -4 to 4
- out_weight: float32 [128], replicated, may hold values from -1 to 1
Outputs:
- logits: float32 [4], replicated
- saliency: float32 [4, 4, 128, 8192], P(None, None, 'face', 'tile')
- grad_fine: float32 [3, 4, 16], replicated
- grad_coarse: float32 [3, 16, 32], replicated
The draws below stay inside these ranges and needn't reach their ends.
All inputs are finite; a program needn't handle non-finite values.
Results may differ from the reference program's by a relative error of at most 0.0003.
Values sent between devices are 32-bit elements; how exact they have to be, the bound alone decides.
No kernel may reach another device: no remote copies, remote signals or barrier semaphores. Data moves between devices by JAX's collectives and lax.ppermute only.
A program may use at most 64 MiB of HBM per device.

```python
import jax
import jax.numpy as jnp
from jax import lax

BINS = 4
CH0 = 16
CH1 = 32
HIDDEN_UNITS = 128
NPAR = 2
ORDER = 3
MAPS = 4
R_DEV = 16
C_DEV = 128
ROWS = 128
COLS = 8192
FACES = 8
TILES = 64


def draw_maps(key, part):
    shape = (MAPS, BINS, ROWS, COLS)
    rows = (jnp.arange(ROWS, dtype=jnp.float32) + 0.5) / ROWS
    cols = (jnp.arange(COLS, dtype=jnp.float32) + 0.5) / COLS
    base = jnp.clip(jax.random.normal(key, shape, jnp.float32), -3.0, 3.0)
    profile = (0.6 + 1.4 * rows)[:, None] * (1.3 - 0.6 * cols)[None, :]
    values = base * profile
    return values.astype(jnp.bfloat16)


def touch_ends(entries, key, least, largest):
    shape = entries.shape
    index_at = [jax.random.randint(jax.random.fold_in(key, axis), (), 0, shape[axis]) for axis in range(len(shape))]
    entries = entries.at[tuple(index_at)].set(least)
    longest = shape.index(max(shape))
    index_at[longest] = (index_at[longest] + 1) % shape[longest]
    return entries.at[tuple(index_at)].set(largest)


def scatter_about(rng, dims, scale, limit, held_as=jnp.bfloat16):
    result = jax.random.normal(rng, dims, jnp.float32) * scale
    return jnp.minimum(jnp.maximum(result, -limit), limit).astype(held_as)


def setup_inputs(seed: int = 0) -> dict:
    key_list = jax.random.split(jax.random.key(seed), 10)
    maps = draw_maps(jax.random.fold_in(key_list[9], 71), 0)
    params = jnp.clip(jax.random.uniform(key_list[1], (MAPS, NPAR), jnp.float32, 0.0, 1.0), 0.0, 1.0)
    labels = touch_ends((jax.random.randint(key_list[2], (MAPS,), 0, 2) < 1).astype(jnp.int32), jax.random.fold_in(key_list[2], 1), 0, 1)
    edge_flip = touch_ends(jax.random.randint(key_list[3], (FACES, TILES), 0, 2), jax.random.fold_in(key_list[3], 1), 0, 1).astype(jnp.int32)
    fine_weight = scatter_about(key_list[4], (ORDER, BINS, CH0), (ORDER * BINS) ** -0.5, 1.75, jnp.float32)
    coarse_weight = scatter_about(key_list[5], (ORDER, CH0, CH1), (ORDER * CH0) ** -0.5, 0.875, jnp.float32)
    feature_weight = scatter_about(key_list[6], (CH1, HIDDEN_UNITS), (CH1 // 4) ** -0.5, 2.0, jnp.float32)
    param_weight = scatter_about(key_list[7], (NPAR, HIDDEN_UNITS), NPAR ** -0.5, 4.0, jnp.float32)
    out_weight = scatter_about(key_list[8], (HIDDEN_UNITS,), (HIDDEN_UNITS // 4) ** -0.5, 1.0, jnp.float32)
    return {"maps": maps, "params": params, "labels": labels, "edge_flip": edge_flip, "fine_weight": fine_weight, "coarse_weight": coarse_weight, "feature_weight": feature_weight, "param_weight": param_weight, "out_weight": out_weight}


exact = lax.Precision.HIGHEST


def lap(field, edge_flip, block_rows, block_cols):
    nrows = field.shape[-2]
    ncols = field.shape[-1]
    turned = field.reshape(field.shape[:-1] + (ncols // block_cols, block_cols))[..., ::-1].reshape(field.shape)
    rows = jnp.arange(nrows)
    cols = jnp.arange(ncols)
    block = rows // block_rows
    colblock = cols // block_cols
    faces = edge_flip.shape[0]
    top_flags = edge_flip[block][:, colblock] == 1
    bottom_flags = edge_flip[(block + 1) % faces][:, colblock] == 1
    top_mask = (rows % block_rows == 0)[:, None] & top_flags
    bottom_mask = (rows % block_rows == block_rows - 1)[:, None] & bottom_flags
    upper = jnp.where(top_mask, jnp.roll(turned, 1, -2), jnp.roll(field, 1, -2))
    lower = jnp.where(bottom_mask, jnp.roll(turned, -1, -2), jnp.roll(field, -1, -2))
    return -0.25 * (upper + lower + jnp.roll(field, 1, -1) + jnp.roll(field, -1, -1))


def cheb_terms(field, edge_flip, block_rows, block_cols):
    first = lap(field, edge_flip, block_rows, block_cols)
    second = 2.0 * lap(first, edge_flip, block_rows, block_cols) - field
    return jnp.stack([field, first, second])


def cheb_adjoint(parts, edge_flip, block_rows, block_cols):
    inner = lap(parts[2], edge_flip, block_rows, block_cols)
    outer = lap(parts[1] + 2.0 * inner, edge_flip, block_rows, block_cols)
    return parts[0] - parts[2] + outer


def reference(maps, params, labels, edge_flip, fine_weight, coarse_weight, feature_weight, param_weight, out_weight):
    pooled_count = (ROWS // 2) * (COLS // 2)

    def forward_map(single):
        x0 = single.astype(jnp.float32)
        terms0 = cheb_terms(x0, edge_flip, R_DEV, C_DEV)
        pre0 = jnp.einsum("kio,kirc->orc", fine_weight, terms0, precision=exact)
        act0 = jax.nn.softplus(pre0)
        x1 = act0.reshape(CH0, ROWS // 2, 2, COLS // 2, 2).mean(axis=(2, 4))
        terms1 = cheb_terms(x1, edge_flip, R_DEV // 2, C_DEV // 2)
        pre1 = jnp.einsum("kio,kirc->orc", coarse_weight, terms1, precision=exact)
        return terms0, pre0, terms1, pre1

    def feature_map(single):
        pre1 = forward_map(single)[3]
        return jax.nn.softplus(pre1).sum(axis=(1, 2))

    features = lax.map(feature_map, maps) / pooled_count
    hidden = jnp.tanh(jnp.dot(features, feature_weight, precision=exact) + jnp.dot(params, param_weight, precision=exact))
    logits = jnp.dot(hidden, out_weight, precision=exact)
    dlogit = jax.nn.sigmoid(logits) - labels.astype(jnp.float32)
    dhidden = dlogit[:, None] * out_weight[None, :] * (1.0 - hidden * hidden)
    dfeatures = jnp.dot(dhidden, feature_weight.T, precision=exact)

    def backward_map(pair):
        single, dfeat = pair
        terms0, pre0, terms1, pre1 = forward_map(single)
        dpre1 = (dfeat / pooled_count)[:, None, None] * jax.nn.sigmoid(pre1)
        grad_c = jnp.einsum("kirc,orc->kio", terms1, dpre1, precision=exact)
        parts1 = jnp.einsum("kio,orc->kirc", coarse_weight, dpre1, precision=exact)
        dx1 = cheb_adjoint(parts1, edge_flip, R_DEV // 2, C_DEV // 2)
        spread = jnp.broadcast_to(dx1[:, :, None, :, None], (CH0, ROWS // 2, 2, COLS // 2, 2)).reshape(pre0.shape)
        dpre0 = 0.25 * spread * jax.nn.sigmoid(pre0)
        grad_f = jnp.einsum("kirc,orc->kio", terms0, dpre0, precision=exact)
        parts0 = jnp.einsum("kio,orc->kirc", fine_weight, dpre0, precision=exact)
        dx0 = cheb_adjoint(parts0, edge_flip, R_DEV, C_DEV)
        return dx0 * (ROWS * COLS), grad_f, grad_c

    saliency, grad_f, grad_c = lax.map(backward_map, (maps, dfeatures))
    return logits, saliency, grad_f.sum(axis=0), grad_c.sum(axis=0)
```

```python
import jax
import jax.numpy as jnp
from jax import lax
from jax.sharding import PartitionSpec as P

exact = lax.Precision.HIGHEST


def with_halo(block, sides, width):
    for axis, dim in sides:
        count = lax.axis_size(axis)
        forward = [(i, i + 1) for i in range(count - 1)]
        forward.append((count - 1, 0))
        backward = [(target, source) for source, target in forward]
        low = lax.ppermute(
            lax.slice_in_dim(block, block.shape[dim] - width, None, axis=dim), axis, forward
        )
        high = lax.ppermute(lax.slice_in_dim(block, 0, width, axis=dim), axis, backward)
        block = jnp.concatenate([low, block, high], axis=dim)
    return block


def turn_blocks(edge_row, width):
    lead = edge_row.shape[:-1]
    return edge_row.reshape(lead + (-1, width))[..., ::-1].reshape(edge_row.shape)


def face_flags(edge_flip):
    position = lax.axis_index("face")
    faces = edge_flip.shape[0]
    return (edge_flip[position] == 1, edge_flip[(position + 1) % faces] == 1)


def tile_flags(flags):
    tiles = flags[0].shape[0]
    spot = lax.axis_index("tile") % tiles
    return (flags[0][spot], flags[1][spot])


def stencil(padded, flags, width):
    top_flag, bottom_flag = tile_flags(flags)
    left = padded[..., 1:-1, :-2]
    right = padded[..., 1:-1, 2:]
    upper = padded[..., :-2, 1:-1]
    lower = padded[..., 2:, 1:-1]
    top_row = upper[..., 0, :]
    upper = upper.at[..., 0, :].set(jnp.where(top_flag, turn_blocks(top_row, width), top_row))
    bottom_row = lower[..., -1, :]
    lower = lower.at[..., -1, :].set(
        jnp.where(bottom_flag, turn_blocks(bottom_row, width), bottom_row)
    )
    return -0.25 * (upper + lower + left + right)


def fine_apply(field, flags):
    padded = with_halo(field, (("face", 2), ("tile", 3)), 1)
    return stencil(padded, flags, field.shape[-1])


def coarse_apply(field, flags):
    padded = with_halo(field, (("face", 2), ("tile", 3)), 1)
    return stencil(padded, flags, field.shape[-1])


def coarse_terms(field, flags):
    first = coarse_apply(field, flags)
    second = 2.0 * coarse_apply(first, flags) - field
    return (first, second)


def coarse_adjoint(parts, flags):
    inner = coarse_apply(parts[2], flags)
    outer = coarse_apply(parts[1] + 2.0 * inner, flags)
    return parts[0] - parts[2] + outer


def sum_over(rows, axes):
    count = lax.axis_size(axes)
    copies = jnp.broadcast_to(rows[None], (count,) + rows.shape)
    return lax.all_to_all(copies, axes, 0, 0).sum(axis=0)


def on_device(
    maps,
    params,
    labels,
    edge_flip,
    fine_weight,
    coarse_weight,
    feature_weight,
    param_weight,
    out_weight,
):
    flags = face_flags(edge_flip)
    field0 = maps.astype(jnp.float32)
    first0 = fine_apply(field0, flags)
    second0 = 2.0 * fine_apply(first0, flags) - field0
    terms0 = jnp.stack([field0, first0, second0])
    pre0 = jnp.einsum("kio,kbirc->borc", fine_weight, terms0, precision=exact)
    act0 = jax.nn.softplus(pre0)
    nmaps, nchan, nrows, ncols = act0.shape
    field1 = act0.reshape(nmaps, nchan, nrows // 2, 2, ncols // 2, 2).mean(axis=(3, 5))
    first1, second1 = coarse_terms(field1, flags)
    terms1 = jnp.stack([field1, first1, second1])
    pre1 = jnp.einsum("kio,kbirc->borc", coarse_weight, terms1, precision=exact)
    act1 = jax.nn.softplus(pre1)
    pooled_count = nrows // 2 * lax.axis_size("face") * (ncols // 2) * lax.axis_size("tile")
    features = sum_over(act1.sum(axis=(2, 3)).reshape(1, -1), ("face", "tile")).reshape(nmaps, -1)
    features = features / pooled_count
    hidden = jnp.tanh(
        jnp.dot(features, feature_weight, precision=exact)
        + jnp.dot(params, param_weight, precision=exact)
    )
    logits = jnp.dot(hidden, out_weight, precision=exact)
    dlogit = jax.nn.sigmoid(logits) - labels.astype(jnp.float32)
    dhidden = dlogit[:, None] * out_weight[None, :] * (1.0 - hidden * hidden)
    dfeatures = jnp.dot(dhidden, feature_weight.T, precision=exact)
    dpre1 = (dfeatures / pooled_count)[:, :, None, None] * jax.nn.sigmoid(pre1)
    grad_c = jnp.einsum("kbirc,borc->kio", terms1, dpre1, precision=exact)
    parts1 = jnp.einsum("kio,borc->kbirc", coarse_weight, dpre1, precision=exact)
    dfield1 = coarse_adjoint(parts1, flags)
    spread = jnp.broadcast_to(
        dfield1[:, :, :, None, :, None], (nmaps, nchan, nrows // 2, 2, ncols // 2, 2)
    ).reshape(pre0.shape)
    dpre0 = 0.25 * spread * jax.nn.sigmoid(pre0)
    grad_f = jnp.einsum("kbirc,borc->kio", terms0, dpre0, precision=exact)
    parts0 = jnp.einsum("kio,borc->kbirc", fine_weight, dpre0, precision=exact)
    inner0 = fine_apply(parts0[2], flags)
    outer0 = fine_apply(parts0[1] + 2.0 * inner0, flags)
    pixel_count = nrows * lax.axis_size("face") * ncols * lax.axis_size("tile")
    saliency = (parts0[0] - parts0[2] + outer0) * pixel_count
    packed = jnp.concatenate([grad_f.reshape(-1), grad_c.reshape(-1)])
    packed = jnp.pad(packed, (0, -packed.size % 1024)).reshape(-1, 128)
    packed = sum_over(sum_over(packed, "face"), "tile").reshape(-1)
    grad_f, grad_c = (
        packed[: grad_f.size].reshape(grad_f.shape),
        packed[grad_f.size : grad_f.size + grad_c.size].reshape(grad_c.shape),
    )
    return (logits, saliency, grad_f, grad_c)


def solution(mesh):
    in_specs = (P(None, None, "face", "tile"), P(), P(), P(), P(), P(), P(), P(), P())
    out_specs = (P(), P(None, None, "face", "tile"), P(), P())
    return jax.shard_map(
        on_device, mesh=mesh, in_specs=in_specs, out_specs=out_specs, check_vma=False
    )
```

```python
import jax
import jax.numpy as jnp
from jax import lax
from jax.experimental import pallas as pl
from jax.experimental.pallas import tpu as pltpu
from jax.sharding import PartitionSpec as P

exact = lax.Precision.HIGHEST
MAPS, BINS, CH0, CH1, ORDER = 4, 4, 16, 32, 3
ROWS, COLS = 16, 128
CROWS, CCOLS = ROWS // 2, COLS // 2
CI = MAPS * BINS
CA = MAPS * CH0
CB = MAPS * CH1
STRIP = 4
SLOT = 2 * STRIP
PER = 128 // SLOT
UP0 = 12
UP1 = 5
UP2 = 3
PAIRS = [(0, 4), (1, 5), (2, 6), (3, 7), (-3, 8), (-2, 9), (-1, 10)]
WHERE = {row: (q, half) for q, pair in enumerate(PAIRS) for half, row in enumerate(pair)}
bf16, f32 = jnp.bfloat16, jnp.float32


def lanes(count):
    return lax.broadcasted_iota(jnp.int32, (count, 128), 1)


def pick(value, index):
    return jnp.take_along_axis(value, index, axis=1, mode="promise_in_bounds")


def roll(value, shift):
    shift %= 128
    return value if shift == 0 else pltpu.roll(value, shift, 1)


def halves(value):
    high = value.astype(bf16)
    return high, (value - high.astype(f32)).astype(bf16)


def weight_halves(ref, start):
    high, low = halves(ref[...])
    column = lax.broadcasted_iota(jnp.int32, ref.shape, 1)
    return jnp.where(column < start, high.astype(f32), low.astype(f32)).astype(bf16)


def dot(a, b):
    return jnp.dot(a, b, preferred_element_type=f32)


def dot_nt(a, b):
    return lax.dot_general(a, b, (((1,), (1,)), ((), ())), preferred_element_type=f32)


def fine_turns(flags, count):
    lane = lanes(count)
    turns = []
    for side in range(2):
        left, own, right = (flags[3 * side + n] for n in range(3))
        block = jnp.where(own == 1, 127 - lane, lane)
        strip = jnp.where(
            lane < 64,
            jnp.where((lane < SLOT) & (right == 1), SLOT - 1 - lane, lane),
            jnp.where((lane >= 128 - SLOT) & (left == 1), 255 - SLOT - lane, lane),
        )
        turns.append((block, strip))
    return turns


def coarse_turns(flags, count):
    lane = lanes(count)
    turns = []
    for side in range(2):
        left, own, right = (flags[3 * side + n] for n in range(3))
        index = jnp.where((lane < 64) & (own == 1), 63 - lane, lane)
        index = jnp.where((lane >= 64) & (lane < 64 + SLOT) & (right == 1), 127 + SLOT - lane, index)
        index = jnp.where((lane >= 128 - SLOT) & (left == 1), 255 - SLOT - lane, index)
        turns.append(index)
    return turns


def vertical(rows, row, height, top, bottom):
    if row == 0:
        upper = pick(rows[-1], top)
    elif row == height:
        upper = pick(rows[height - 1], bottom)
    else:
        upper = rows[row - 1]
    if row == -1:
        lower = pick(rows[0], top)
    elif row == height - 1:
        lower = pick(rows[height], bottom)
    else:
        lower = rows[row + 1]
    return upper + lower


def fine_lap(block, strip, row, turns, with_strip):
    (top, top_strip), (bottom, bottom_strip) = turns
    lane = lanes(block[row].shape[0])
    first, last = lane == 0, lane == 127
    b_right, s_right = roll(block[row], 1), roll(strip[row], 1)
    b_left, s_left = roll(block[row], -1), roll(strip[row], -1)
    side = jnp.where(first, s_right, b_right) + jnp.where(last, s_left, b_left)
    out = -0.25 * (vertical(block, row, ROWS, top, bottom) + side)
    if not with_strip:
        return out
    side = jnp.where(first, b_right, s_right) + jnp.where(last, b_left, s_left)
    return out, -0.25 * (vertical(strip, row, ROWS, top_strip, bottom_strip) + side)


def coarse_lap(rows, row, turns):
    value = rows[row]
    side = roll(value, 1) + roll(value, -1)
    return -0.25 * (vertical(rows, row, CROWS, turns[0], turns[1]) + side)


def end_index(count, stride=1, width=COLS):
    j = lanes(count) % SLOT
    return jnp.where(j < STRIP, j, width - SLOT + j) * stride


def fine_strip(left, right, place):
    group, slot = place // PER, place % PER
    lane = lanes(left.shape[1])
    return jnp.where(
        lane < 64, roll(right[group], -SLOT * slot), roll(left[group], 128 - SLOT - SLOT * slot)
    )


def coarse_row(block, left, right, slot):
    lane = lanes(block.shape[0])
    strip = jnp.where(
        lane < 96, roll(right, 64 - SLOT * slot), roll(left, 128 - SLOT - SLOT * slot)
    )
    return jnp.where(lane < 64, block, strip)


def groups(count):
    return -(-count // PER)


def put_slots(out_ref, filled, count):
    lane = lanes(filled[0].shape[0])
    for group in range(groups(count)):
        value = filled[group * PER]
        for n in range(group * PER + 1, min(count, group * PER + PER)):
            value = jnp.where(lane // SLOT == n % PER, filled[n], value)
        out_ref[group] = value


def fine_rows(up_ref, own_ref, down_ref):
    rows = {}
    for row in range(-UP0, ROWS + UP0):
        if row < 0:
            rows[row] = up_ref[ROWS + row]
        elif row < ROWS:
            rows[row] = own_ref[row]
        else:
            rows[row] = down_ref[row - ROWS]
    return rows


def ends_kernel(up_ref, own_ref, down_ref, out_ref):
    index = end_index(CI)
    rows = fine_rows(up_ref, own_ref, down_ref)
    put_slots(out_ref, [pick(rows[row], index) for row in sorted(rows)], len(rows))


def fine_kernel(
    flags, up_ref, own_ref, down_ref, left_ref, right_ref, w_ref,
    x1_ref, sig_ref, terms_ref, ends_ref, t_ref,
):
    turns = fine_turns(flags, CI)
    block = fine_rows(up_ref, own_ref, down_ref)
    strip = {row: fine_strip(left_ref, right_ref, row + UP0) for row in block}
    first, first_strip = {}, {}
    for row in range(1 - UP0, ROWS + UP0 - 1):
        first[row], first_strip[row] = fine_lap(block, strip, row, turns, True)
    low, high = -2 * UP1, ROWS + 2 * UP1
    for row in range(low, high):
        second = 2.0 * fine_lap(first, first_strip, row, turns, False) - block[row]
        here = pl.ds((row - low) * 128, 128)
        one, one_low = halves(first[row])
        two, two_low = halves(second)
        for n, part in enumerate((block[row].astype(bf16), one, two, one_low, two_low)):
            t_ref[CI * n : CI * (n + 1), here] = part
        for n, part in enumerate((block[row].astype(bf16), one, two)):
            t_ref[CI * (5 + n) : CI * (6 + n), here] = part
    own = pl.ds(-low * 128, ROWS * 128)
    terms_ref[...] = t_ref[0 : 5 * CI, own]
    weights = weight_halves(w_ref, 5 * CI)
    lane = lanes(CA)
    even = 2 * (lane % 64)
    ends = end_index(CA, 2, CCOLS)
    filled = []
    for crow in range(-UP1, CROWS + UP1):
        place = crow + UP1
        pre = dot(weights, t_ref[:, place * 256 : place * 256 + 256])
        decay = jnp.exp(-jnp.abs(pre))
        act = jnp.maximum(pre, 0.0) + jnp.log(1.0 + decay)
        if -1 <= crow <= CROWS:
            inverse = 1.0 / (1.0 + decay)
            sig = jnp.where(pre >= 0, inverse, decay * inverse)
            sig_ref[2 * (crow + 1)] = sig[:, :128]
            sig_ref[2 * (crow + 1) + 1] = sig[:, 128:]
        both = act[:, :128] + act[:, 128:]
        both = 0.25 * (both + roll(both, -1))
        x1_ref[place] = pick(both, even)
        filled.append(pick(both, ends))
    put_slots(ends_ref, filled, len(filled))


def coarse_kernel(
    flags, x1_ref, left_ref, right_ref, w_ref, feat_ref, sig_ref, ends_ref, gram_ref, t_ref, s_ref
):
    turns = coarse_turns(flags, CA)
    lane = lanes(CA)
    rows = {}
    for row in range(-UP1, CROWS + UP1):
        place = row + UP1
        rows[row] = coarse_row(
            x1_ref[place], left_ref[place // PER], right_ref[place // PER], place % PER
        )
    first = {row: coarse_lap(rows, row, turns) for row in range(1 - UP1, CROWS + UP1 - 1)}
    second = {
        row: 2.0 * coarse_lap(first, row, turns) - rows[row]
        for row in range(-UP2, CROWS + UP2)
    }
    for q, (a, b) in enumerate(PAIRS):
        here = pl.ds(q * 128, 128)
        for k, term in enumerate((rows, first, second)):
            packed = jnp.where(lane < 64, term[a], roll(term[b], 64))
            high, low = halves(packed)
            for m in range(MAPS):
                chans = slice(CH0 * m, CH0 * (m + 1))
                t_ref[m, CH0 * k : CH0 * (k + 1), here] = high[chans]
                t_ref[m, CH0 * (3 + k) : CH0 * (4 + k), here] = low[chans]
                t_ref[m, CH0 * (6 + k) : CH0 * (7 + k), here] = high[chans]
    weights = weight_halves(w_ref, 2 * ORDER * CH0)
    own = 4 * 128
    j = lanes(CH1) % SLOT
    column = jnp.where(j < STRIP, j, CCOLS - SLOT + j)
    index = jnp.where(lanes(CH1) // SLOT % 2 == 0, column, 64 + column)
    sums = []
    for m in range(MAPS):
        pre = dot(weights, t_ref[m])
        decay = jnp.exp(-jnp.abs(pre))
        inverse = 1.0 / (1.0 + decay)
        sig = jnp.where(pre >= 0, inverse, decay * inverse)
        act = jnp.maximum(pre[:, :own], 0.0) + jnp.log(1.0 + decay[:, :own])
        sums.append(sum(act[:, 128 * q : 128 * (q + 1)] for q in range(4)))
        high, low = halves(sig[:, :own])
        s_ref[CH1 * m : CH1 * (m + 1)] = high
        s_ref[CB + CH1 * m : CB + CH1 * (m + 1)] = low
        chans = slice(CH1 * m, CH1 * (m + 1))
        ends = jnp.zeros((CH1, 128), f32)
        for q in range(len(PAIRS)):
            value = sig[:, 128 * q : 128 * (q + 1)]
            sig_ref[q, chans] = value
            ends = jnp.where(lanes(CH1) // (2 * SLOT) == q, pick(value, index), ends)
        ends_ref[chans] = ends
    total = jnp.sum(jnp.concatenate(sums, axis=0).T, axis=0, keepdims=True)
    feat_ref[...] = jnp.broadcast_to(total, feat_ref.shape)
    grams = [jnp.zeros((CH0, 128), f32) for _ in range(ORDER)]
    for m in range(MAPS):
        both = dot_nt(t_ref[m, : 2 * ORDER * CH0, :own], s_ref[...])
        for k in range(ORDER):
            high = both[CH0 * k : CH0 * (k + 1)]
            low = both[CH0 * (3 + k) : CH0 * (4 + k)]
            value = high[:, :CB] + high[:, CB:] + low[:, :CB]
            grams[k] = jnp.where(lanes(CH0) // CH1 == m, value, grams[k])
    for k in range(ORDER):
        gram_ref[k] = grams[k]


def back_kernel(
    flags, feat_ref, shift_ref, labels_ref, fw_ref, out_ref, w1_ref, w0_ref,
    sig1_ref, left_ref, right_ref, gram_ref, sig0_ref, terms_ref,
    logits_ref, grads_ref, g_ref, ends_ref, s_ref, d_ref,
    *, pooled,
):
    features = jnp.sum(feat_ref[...], axis=0, keepdims=True) * (1.0 / pooled)
    row8 = lax.broadcasted_iota(jnp.int32, (8, 128), 0)
    spread = jnp.where(lanes(8) // CH1 == row8, jnp.broadcast_to(features, (8, 128)), 0.0)
    fw = fw_ref[...]
    hidden = jnp.tanh(
        jnp.dot(spread, fw, precision=exact, preferred_element_type=f32) + shift_ref[...]
    )
    logits = jnp.sum(hidden * out_ref[...], axis=1, keepdims=True)
    logits_ref[...] = jnp.broadcast_to(logits, (8, 128))
    decay = jnp.exp(-jnp.abs(logits))
    dlogit = jnp.where(logits >= 0, 1.0, decay) / (1.0 + decay) - labels_ref[...]
    dhidden = dlogit * out_ref[...] * (1.0 - hidden * hidden)
    dhidden = jnp.concatenate(
        [jnp.broadcast_to(dhidden[m : m + 1], (CH1, 128)) for m in range(MAPS)], axis=0
    )
    dcol = jnp.sum(fw * dhidden, axis=1, keepdims=True) * (1.0 / pooled)
    dfull = jnp.broadcast_to(dcol, (CB, 128))
    drow = jnp.broadcast_to(dfull.T[:1], (CH0, 128))
    coarse = []
    for k in range(ORDER):
        value = gram_ref[k] * drow
        value = value + roll(value, 64)
        coarse.append(value + roll(value, 32))
    slabs = len(PAIRS) + 2
    for q in range(slabs):
        value = sig1_ref[q] if q < len(PAIRS) else (left_ref, right_ref)[q - len(PAIRS)][...]
        high, low = halves(value * dfull)
        here = pl.ds(q * 128, 128)
        for m in range(MAPS):
            chans = slice(CH1 * m, CH1 * (m + 1))
            s_ref[m, :CH1, here] = high[chans]
            s_ref[m, CH1 : 2 * CH1, here] = low[chans]
            s_ref[m, 2 * CH1 :, here] = high[chans]
    weights = weight_halves(w1_ref, 2 * CH1)
    parts = [dot(weights, s_ref[m]) for m in range(MAPS)]

    def slab(k, q):
        return jnp.concatenate(
            [part[CH0 * k : CH0 * (k + 1), 128 * q : 128 * (q + 1)] for part in parts], axis=0
        )

    def spread_rows(k, low, high, strips):
        left, right = (slab(k, slabs - 2), slab(k, slabs - 1)) if strips else (None, None)
        packed = [slab(k, q) for q in range(len(PAIRS))]
        rows = {}
        for row in range(low, high):
            q, half = WHERE[row]
            value = roll(packed[q], 64 * half)
            rows[row] = coarse_row(value, left, right, 2 * q + half) if strips else value
        return rows

    turns = coarse_turns(flags, CA)
    g0 = spread_rows(0, -1, CROWS + 1, False)
    g1 = spread_rows(1, 1 - UP2, CROWS + UP2 - 1, True)
    g2 = spread_rows(2, -UP2, CROWS + UP2, True)
    inner = {row: g1[row] + 2.0 * coarse_lap(g2, row, turns) for row in g1}
    doubled = lanes(CA) // 2
    for crow in range(-1, CROWS + 1):
        dx1 = g0[crow] - g2[crow] + coarse_lap(inner, crow, turns)
        dx1 = 0.25 * pick(dx1, doubled)
        for n in (2 * (crow + 1), 2 * (crow + 1) + 1):
            high, low = halves(dx1 * sig0_ref[n])
            here = pl.ds(n * 128, 128)
            d_ref[:CA, here] = high
            d_ref[CA : 2 * CA, here] = low
            d_ref[2 * CA :, here] = high
    both = dot_nt(terms_ref[...], d_ref[: 2 * CA, 2 * 128 : (2 + ROWS) * 128])
    lane = lanes(CI)
    row16 = lax.broadcasted_iota(jnp.int32, (CI, 128), 0)
    same = lane % CA // CH0 == row16 // BINS
    fine = []
    for k in range(ORDER):
        value = jnp.where(same, both[CI * k : CI * (k + 1)], 0.0)
        if k:
            low = both[CI * (2 + k) : CI * (3 + k)]
            value = value + jnp.where(same & (lane < CA), low, 0.0)
        for shift in (64, 32, 16):
            value = value + roll(value, shift)
        for shift in (8, 4):
            value = value + pltpu.roll(value, shift, 0)
        fine.append(value)
    value = jnp.where(row16 // BINS == 0, fine[0], jnp.where(row16 // BINS == 1, fine[1], fine[2]))
    for k in range(ORDER):
        value = jnp.where(lane // CH1 == k, coarse[k], value)
    for n in range(grads_ref.shape[0] // CI):
        grads_ref[CI * n : CI * (n + 1)] = value
    weights = weight_halves(w0_ref, 2 * CA)
    index = end_index(2 * CI)
    filled = []
    for n in range(0, ROWS + 4, 2):
        value = dot(weights, d_ref[:, n * 128 : (n + 2) * 128])
        for step in range(2):
            part = value[:, 128 * step : 128 * (step + 1)]
            g_ref[n + step] = part
            filled.append(pick(part[CI:], index))
    put_slots(ends_ref, filled, len(filled))


def saliency_kernel(flags, g_ref, left_ref, right_ref, out_ref, *, pixels):
    turns = fine_turns(flags, CI)
    g0, g1, g2, s1, s2 = {}, {}, {}, {}, {}
    for row in range(-2, ROWS + 2):
        value = g_ref[row + 2]
        g0[row], g1[row], g2[row] = (value[CI * k : CI * (k + 1)] for k in range(3))
        strip = fine_strip(left_ref, right_ref, row + 2)
        s1[row], s2[row] = strip[:CI], strip[CI:]
    inner, inner_strip = {}, {}
    for row in range(-1, ROWS + 1):
        value, strip = fine_lap(g2, s2, row, turns, True)
        inner[row] = g1[row] + 2.0 * value
        inner_strip[row] = s1[row] + 2.0 * strip
    for row in range(ROWS):
        outer = fine_lap(inner, inner_strip, row, turns, False)
        out_ref[pl.ds(row, CI, stride=ROWS), :] = (g0[row] - g2[row] + outer) * pixels


def again_kernel(in_ref, out_ref):
    value = in_ref[0:CI]
    for n in range(1, in_ref.shape[0] // CI):
        value = value + in_ref[CI * n : CI * (n + 1)]
    for n in range(out_ref.shape[0] // CI):
        out_ref[CI * n : CI * (n + 1)] = value


def last_kernel(in_ref, fine_ref, coarse_ref, tmp_ref):
    value = in_ref[0:CI]
    for n in range(1, in_ref.shape[0] // CI):
        value = value + in_ref[CI * n : CI * (n + 1)]
    for k in range(ORDER):
        coarse_ref[k] = roll(value, -CH1 * k)[:, :CH1]
    tmp_ref[...] = roll(value, -ORDER * CH1)
    for k in range(ORDER):
        fine_ref[k] = tmp_ref[BINS * k : BINS * (k + 1), :CH0]


def call(kernel, outs, *args, smem=0, scratch=()):
    in_specs = [
        pl.BlockSpec(memory_space=pltpu.SMEM if n < smem else pltpu.VMEM) for n in range(len(args))
    ]
    return pl.pallas_call(
        kernel,
        out_shape=outs,
        in_specs=in_specs,
        out_specs=jax.tree.map(lambda _: pl.BlockSpec(memory_space=pltpu.VMEM), outs),
        scratch_shapes=list(scratch),
        compiler_params=pltpu.CompilerParams(vmem_limit_bytes=32 * 2**20),
    )(*args)


def shape(*dims, dtype=f32):
    return jax.ShapeDtypeStruct(dims, dtype)


def both_ways(value, axis):
    count = lax.axis_size(axis)
    forward = [(n, (n + 1) % count) for n in range(count)]
    backward = [(target, source) for source, target in forward]
    return lax.ppermute(value, axis, forward), lax.ppermute(value, axis, backward)


def share(rows, axes):
    return lax.all_to_all(rows, axes, 0, 0, tiled=True)


def on_device(
    maps, params, labels, edge_flip,
    fine_weight, coarse_weight, feature_weight, param_weight, out_weight,
):
    faces, tiles = lax.axis_size("face"), lax.axis_size("tile")
    devices = faces * tiles
    f, t = lax.axis_index("face"), lax.axis_index("tile")
    columns = jnp.stack([(t + tiles - 1) % tiles, t, (t + 1) % tiles])
    flags = jnp.concatenate([edge_flip[f][columns], edge_flip[(f + 1) % faces][columns]])
    eye = jnp.eye(MAPS, dtype=f32)
    fine = jnp.einsum("kio,mn->monki", fine_weight, eye)
    fine = fine.transpose(0, 1, 3, 2, 4).reshape(CA, ORDER * CI)
    fine_forward = jnp.concatenate([fine, fine[:, CI:], fine], axis=1)
    fine_backward = jnp.concatenate([fine.T] * 3, axis=1)
    coarse = coarse_weight.reshape(ORDER * CH0, CH1)
    coarse_forward = jnp.concatenate([coarse.T] * 3, axis=1)
    coarse_backward = jnp.concatenate([coarse] * 3, axis=1)
    features4 = jnp.concatenate([feature_weight] * MAPS, axis=0)
    pad = [(0, 8 - MAPS), (0, 0)]
    shift = jnp.dot(jnp.pad(params, pad), param_weight, precision=exact)
    labels8 = jnp.broadcast_to(jnp.pad(labels.astype(f32)[:, None], pad), (8, 128))

    own = maps.reshape(CI, ROWS, COLS).transpose(1, 0, 2).astype(f32)
    up, down = both_ways(own, "face")
    ends0 = call(ends_kernel, shape(groups(ROWS + 2 * UP0), CI, 128), up, own, down)
    left0, right0 = both_ways(ends0, "tile")
    crows = CROWS + 2 * UP1
    x1, sig0, terms0, ends1 = call(
        fine_kernel,
        (
            shape(crows, CA, 128),
            shape(ROWS + 4, CA, 128),
            shape(5 * CI, ROWS * 128, dtype=bf16),
            shape(groups(crows), CA, 128),
        ),
        flags, up, own, down, left0, right0, fine_forward,
        smem=1,
        scratch=[pltpu.VMEM((8 * CI, 2 * crows * 128), bf16)],
    )
    left1, right1 = both_ways(ends1, "tile")
    feats, sig1, ends2, grams = call(
        coarse_kernel,
        (
            shape(devices, CB),
            shape(len(PAIRS), CB, 128),
            shape(CB, 128),
            shape(ORDER, CH0, 128),
        ),
        flags, x1, left1, right1, coarse_forward,
        smem=1,
        scratch=[
            pltpu.VMEM((MAPS, 3 * ORDER * CH0, len(PAIRS) * 128), bf16),
            pltpu.VMEM((2 * CB, 4 * 128), bf16),
        ],
    )
    left2, right2 = both_ways(ends2, "tile")
    feats = share(feats, ("face", "tile"))
    pooled = CROWS * faces * CCOLS * tiles
    logits, grads, g, ends3 = call(
        lambda *refs: back_kernel(*refs, pooled=pooled),
        (
            shape(8, 128),
            shape(faces * CI, 128),
            shape(ROWS + 4, ORDER * CI, 128),
            shape(groups(ROWS + 4), 2 * CI, 128),
        ),
        flags, feats, shift, labels8, features4, out_weight[None],
        coarse_backward, fine_backward, sig1, left2, right2, grams, sig0, terms0,
        smem=1,
        scratch=[
            pltpu.VMEM((MAPS, 3 * CH1, (len(PAIRS) + 2) * 128), bf16),
            pltpu.VMEM((3 * CA, (ROWS + 4) * 128), bf16),
        ],
    )
    left3, right3 = both_ways(ends3, "tile")
    grads = share(grads, "face")
    grads = call(again_kernel, shape(tiles * CI, 128), grads)
    grads = share(grads, "tile")
    pixels = float(ROWS * faces * COLS * tiles)
    saliency = call(
        lambda *refs: saliency_kernel(*refs, pixels=pixels),
        shape(CI * ROWS, COLS), flags, g, left3, right3,
        smem=1,
    )
    grad_f, grad_c = call(
        last_kernel, (shape(*fine_weight.shape), shape(*coarse_weight.shape)), grads,
        scratch=[pltpu.VMEM((CI, 128), f32)],
    )
    return (logits[:MAPS, 0], saliency.reshape(maps.shape), grad_f, grad_c)


def solution(mesh):
    in_specs = (P(None, None, "face", "tile"), P(), P(), P(), P(), P(), P(), P(), P())
    out_specs = (P(), P(None, None, "face", "tile"), P(), P())
    return jax.shard_map(
        on_device, mesh=mesh, in_specs=in_specs, out_specs=out_specs, check_vma=False
    )
```

```python
import jax
import jax.numpy as jnp
from jax import lax
from jax.experimental import pallas as pl
from jax.experimental.pallas import tpu as pltpu
from jax.sharding import PartitionSpec as P

exact = lax.Precision.HIGHEST
MAPS, BINS, CH0, CH1, ORDER = 4, 4, 16, 32, 3
ROWS, COLS = 16, 128
CROWS, CCOLS = ROWS // 2, COLS // 2
CI = MAPS * BINS
CA = MAPS * CH0
CB = MAPS * CH1
STRIP = 4
SLOT = 2 * STRIP
PER = 128 // SLOT
UP0 = 12
UP1 = 5
UP2 = 3
PAIRS = [(0, 4), (1, 5), (2, 6), (3, 7), (-3, 8), (-2, 9), (-1, 10)]
WHERE = {row: (q, half) for q, pair in enumerate(PAIRS) for half, row in enumerate(pair)}
FACE, TILE = ("x", "y_lo"), ("z", "y_hi", "core")
PLANE = ("x", "y_lo", "y_hi", "core")
bf16, f32 = jnp.bfloat16, jnp.float32


def lanes(count):
    return lax.broadcasted_iota(jnp.int32, (count, 128), 1)


def pick(value, index):
    return jnp.take_along_axis(value, index, axis=1, mode="promise_in_bounds")


def roll(value, shift):
    shift %= 128
    return value if shift == 0 else pltpu.roll(value, shift, 1)


def halves(value):
    high = value.astype(bf16)
    return high, (value - high.astype(f32)).astype(bf16)


def weight_halves(ref, start):
    high, low = halves(ref[...])
    column = lax.broadcasted_iota(jnp.int32, ref.shape, 1)
    return jnp.where(column < start, high.astype(f32), low.astype(f32)).astype(bf16)


def dot(a, b):
    return jnp.dot(a, b, preferred_element_type=f32)


def dot_nt(a, b):
    return lax.dot_general(a, b, (((1,), (1,)), ((), ())), preferred_element_type=f32)


def fine_turns(flags, count):
    lane = lanes(count)
    turns = []
    for side in range(2):
        left, own, right = (flags[3 * side + n] for n in range(3))
        block = jnp.where(own == 1, 127 - lane, lane)
        strip = jnp.where(
            lane < 64,
            jnp.where((lane < SLOT) & (right == 1), SLOT - 1 - lane, lane),
            jnp.where((lane >= 128 - SLOT) & (left == 1), 255 - SLOT - lane, lane),
        )
        turns.append((block, strip))
    return turns


def coarse_turns(flags, count):
    lane = lanes(count)
    turns = []
    for side in range(2):
        left, own, right = (flags[3 * side + n] for n in range(3))
        index = jnp.where((lane < 64) & (own == 1), 63 - lane, lane)
        index = jnp.where((lane >= 64) & (lane < 64 + SLOT) & (right == 1), 127 + SLOT - lane, index)
        index = jnp.where((lane >= 128 - SLOT) & (left == 1), 255 - SLOT - lane, index)
        turns.append(index)
    return turns


def vertical(rows, row, height, top, bottom):
    if row == 0:
        upper = pick(rows[-1], top)
    elif row == height:
        upper = pick(rows[height - 1], bottom)
    else:
        upper = rows[row - 1]
    if row == -1:
        lower = pick(rows[0], top)
    elif row == height - 1:
        lower = pick(rows[height], bottom)
    else:
        lower = rows[row + 1]
    return upper + lower


def fine_lap(block, strip, row, turns, with_strip):
    (top, top_strip), (bottom, bottom_strip) = turns
    lane = lanes(block[row].shape[0])
    first, last = lane == 0, lane == 127
    b_right, s_right = roll(block[row], 1), roll(strip[row], 1)
    b_left, s_left = roll(block[row], -1), roll(strip[row], -1)
    side = jnp.where(first, s_right, b_right) + jnp.where(last, s_left, b_left)
    out = -0.25 * (vertical(block, row, ROWS, top, bottom) + side)
    if not with_strip:
        return out
    side = jnp.where(first, b_right, s_right) + jnp.where(last, b_left, s_left)
    return out, -0.25 * (vertical(strip, row, ROWS, top_strip, bottom_strip) + side)


def coarse_lap(rows, row, turns):
    value = rows[row]
    side = roll(value, 1) + roll(value, -1)
    return -0.25 * (vertical(rows, row, CROWS, turns[0], turns[1]) + side)


def end_index(count, stride=1, width=COLS):
    j = lanes(count) % SLOT
    return jnp.where(j < STRIP, j, width - SLOT + j) * stride


def fine_strip(left, right, place):
    group, slot = place // PER, place % PER
    lane = lanes(left[group].shape[0])
    return jnp.where(
        lane < 64, roll(right[group], -SLOT * slot), roll(left[group], 128 - SLOT - SLOT * slot)
    )


def coarse_row(block, left, right, slot):
    lane = lanes(block.shape[0])
    strip = jnp.where(
        lane < 96, roll(right, 64 - SLOT * slot), roll(left, 128 - SLOT - SLOT * slot)
    )
    return jnp.where(lane < 64, block, strip)


def groups(count):
    return -(-count // PER)


def put_slots(out_ref, filled, count):
    lane = lanes(filled[0].shape[0])
    for group in range(groups(count)):
        value = filled[group * PER]
        for n in range(group * PER + 1, min(count, group * PER + PER)):
            value = jnp.where(lane // SLOT == n % PER, filled[n], value)
        out_ref[group] = value


def before(far, near, odd):
    return jnp.where(odd == 1, near, far)


def after(far, near, odd):
    return jnp.where(odd == 1, far, near)


def fine_rows(far_ref, near_ref, own_ref, odd):
    rows = {}
    for row in range(-UP0, ROWS + UP0):
        if row < 0:
            rows[row] = before(far_ref[UP0 + row], near_ref[UP0 + row], odd)
        elif row < ROWS:
            rows[row] = own_ref[row]
        else:
            rows[row] = after(far_ref[row - ROWS], near_ref[row - ROWS], odd)
    return rows


def rows_kernel(flags, maps_ref, own_ref, far_ref, near_ref, t_ref):
    t_ref[...] = maps_ref[...].astype(f32)
    rows = [t_ref[pl.ds(row, CI, stride=ROWS), :] for row in range(ROWS)]
    for row in range(ROWS):
        own_ref[row] = rows[row]
    for row in range(UP0):
        first, last = rows[row], rows[ROWS - UP0 + row]
        far_ref[row] = before(first, last, flags[6])
        near_ref[row] = after(first, last, flags[6])


def both_strips(far_ref, near_ref, odd):
    count = far_ref.shape[0]
    left = [before(far_ref[n], near_ref[n], odd) for n in range(count)]
    return left, [after(far_ref[n], near_ref[n], odd) for n in range(count)]


def ends_kernel(flags, far_ref, near_ref, own_ref, out_ref):
    index = end_index(CI)
    rows = fine_rows(far_ref, near_ref, own_ref, flags[6])
    put_slots(out_ref, [pick(rows[row], index) for row in sorted(rows)], len(rows))


def fine_kernel(
    flags, far_ref, near_ref, own_ref, far0_ref, near0_ref, w_ref,
    x1_ref, sig_ref, terms_ref, ends_ref, t_ref,
):
    turns = fine_turns(flags, CI)
    block = fine_rows(far_ref, near_ref, own_ref, flags[6])
    left, right = both_strips(far0_ref, near0_ref, flags[7])
    strip = {row: fine_strip(left, right, row + UP0) for row in block}
    first, first_strip = {}, {}
    for row in range(1 - UP0, ROWS + UP0 - 1):
        first[row], first_strip[row] = fine_lap(block, strip, row, turns, True)
    low, high = -2 * UP1, ROWS + 2 * UP1
    for row in range(low, high):
        second = 2.0 * fine_lap(first, first_strip, row, turns, False) - block[row]
        here = pl.ds((row - low) * 128, 128)
        one, one_low = halves(first[row])
        two, two_low = halves(second)
        for n, part in enumerate((block[row].astype(bf16), one, two, one_low, two_low)):
            t_ref[CI * n : CI * (n + 1), here] = part
        for n, part in enumerate((block[row].astype(bf16), one, two)):
            t_ref[CI * (5 + n) : CI * (6 + n), here] = part
    own = pl.ds(-low * 128, ROWS * 128)
    terms_ref[...] = t_ref[0 : 5 * CI, own]
    weights = weight_halves(w_ref, 5 * CI)
    lane = lanes(CA)
    even = 2 * (lane % 64)
    ends = end_index(CA, 2, CCOLS)
    filled = []
    for crow in range(-UP1, CROWS + UP1):
        place = crow + UP1
        pre = dot(weights, t_ref[:, place * 256 : place * 256 + 256])
        decay = jnp.exp(-jnp.abs(pre))
        act = jnp.maximum(pre, 0.0) + jnp.log(1.0 + decay)
        if -1 <= crow <= CROWS:
            inverse = 1.0 / (1.0 + decay)
            sig = jnp.where(pre >= 0, inverse, decay * inverse)
            sig_ref[2 * (crow + 1)] = sig[:, :128]
            sig_ref[2 * (crow + 1) + 1] = sig[:, 128:]
        both = act[:, :128] + act[:, 128:]
        both = 0.25 * (both + roll(both, -1))
        x1_ref[place] = pick(both, even)
        filled.append(pick(both, ends))
    put_slots(ends_ref, filled, len(filled))


def coarse_kernel(
    flags, x1_ref, far_ref, near_ref, w_ref, feat_ref, sig_ref, ends_ref, gram_ref, t_ref, s_ref
):
    turns = coarse_turns(flags, CA)
    lane = lanes(CA)
    left, right = both_strips(far_ref, near_ref, flags[7])
    rows = {}
    for row in range(-UP1, CROWS + UP1):
        place = row + UP1
        rows[row] = coarse_row(
            x1_ref[place], left[place // PER], right[place // PER], place % PER
        )
    first = {row: coarse_lap(rows, row, turns) for row in range(1 - UP1, CROWS + UP1 - 1)}
    second = {
        row: 2.0 * coarse_lap(first, row, turns) - rows[row]
        for row in range(-UP2, CROWS + UP2)
    }
    for q, (a, b) in enumerate(PAIRS):
        here = pl.ds(q * 128, 128)
        for k, term in enumerate((rows, first, second)):
            packed = jnp.where(lane < 64, term[a], roll(term[b], 64))
            high, low = halves(packed)
            for m in range(MAPS):
                chans = slice(CH0 * m, CH0 * (m + 1))
                t_ref[m, CH0 * k : CH0 * (k + 1), here] = high[chans]
                t_ref[m, CH0 * (3 + k) : CH0 * (4 + k), here] = low[chans]
                t_ref[m, CH0 * (6 + k) : CH0 * (7 + k), here] = high[chans]
    weights = weight_halves(w_ref, 2 * ORDER * CH0)
    own = 4 * 128
    j = lanes(CH1) % SLOT
    column = jnp.where(j < STRIP, j, CCOLS - SLOT + j)
    index = jnp.where(lanes(CH1) // SLOT % 2 == 0, column, 64 + column)
    sums = []
    for m in range(MAPS):
        pre = dot(weights, t_ref[m])
        decay = jnp.exp(-jnp.abs(pre))
        inverse = 1.0 / (1.0 + decay)
        sig = jnp.where(pre >= 0, inverse, decay * inverse)
        act = jnp.maximum(pre[:, :own], 0.0) + jnp.log(1.0 + decay[:, :own])
        sums.append(sum(act[:, 128 * q : 128 * (q + 1)] for q in range(4)))
        high, low = halves(sig[:, :own])
        s_ref[CH1 * m : CH1 * (m + 1)] = high
        s_ref[CB + CH1 * m : CB + CH1 * (m + 1)] = low
        chans = slice(CH1 * m, CH1 * (m + 1))
        ends = jnp.zeros((CH1, 128), f32)
        for q in range(len(PAIRS)):
            value = sig[:, 128 * q : 128 * (q + 1)]
            sig_ref[q, chans] = value
            ends = jnp.where(lanes(CH1) // (2 * SLOT) == q, pick(value, index), ends)
        ends_ref[chans] = ends
    total = jnp.sum(jnp.concatenate(sums, axis=0).T, axis=0, keepdims=True)
    feat_ref[...] = jnp.broadcast_to(total, feat_ref.shape)
    grams = [jnp.zeros((CH0, 128), f32) for _ in range(ORDER)]
    for m in range(MAPS):
        both = dot_nt(t_ref[m, : 2 * ORDER * CH0, :own], s_ref[...])
        for k in range(ORDER):
            high = both[CH0 * k : CH0 * (k + 1)]
            low = both[CH0 * (3 + k) : CH0 * (4 + k)]
            value = high[:, :CB] + high[:, CB:] + low[:, :CB]
            grams[k] = jnp.where(lanes(CH0) // CH1 == m, value, grams[k])
    for k in range(ORDER):
        gram_ref[k] = grams[k]


def back_kernel(
    flags, feat_ref, shift_ref, labels_ref, fw_ref, out_ref, w1_ref, w0_ref,
    sig1_ref, far_ref, near_ref, gram_ref, sig0_ref, terms_ref,
    logits_ref, grads_ref, g_ref, ends_ref, s_ref, d_ref,
    *, pooled,
):
    features = jnp.sum(feat_ref[...], axis=0, keepdims=True) * (1.0 / pooled)
    row8 = lax.broadcasted_iota(jnp.int32, (8, 128), 0)
    spread = jnp.where(lanes(8) // CH1 == row8, jnp.broadcast_to(features, (8, 128)), 0.0)
    fw = fw_ref[...]
    hidden = jnp.tanh(
        jnp.dot(spread, fw, precision=exact, preferred_element_type=f32) + shift_ref[...]
    )
    logits = jnp.sum(hidden * out_ref[...], axis=1, keepdims=True)
    logits_ref[...] = jnp.broadcast_to(logits, (8, 128))
    decay = jnp.exp(-jnp.abs(logits))
    dlogit = jnp.where(logits >= 0, 1.0, decay) / (1.0 + decay) - labels_ref[...]
    dhidden = dlogit * out_ref[...] * (1.0 - hidden * hidden)
    dhidden = jnp.concatenate(
        [jnp.broadcast_to(dhidden[m : m + 1], (CH1, 128)) for m in range(MAPS)], axis=0
    )
    dcol = jnp.sum(fw * dhidden, axis=1, keepdims=True) * (1.0 / pooled)
    dfull = jnp.broadcast_to(dcol, (CB, 128))
    drow = jnp.broadcast_to(dfull.T[:1], (CH0, 128))
    coarse = []
    for k in range(ORDER):
        value = gram_ref[k] * drow
        value = value + roll(value, 64)
        coarse.append(value + roll(value, 32))
    slabs = len(PAIRS) + 2
    for q in range(slabs):
        if q < len(PAIRS):
            value = sig1_ref[q]
        else:
            value = (before, after)[q - len(PAIRS)](far_ref[...], near_ref[...], flags[7])
        high, low = halves(value * dfull)
        here = pl.ds(q * 128, 128)
        for m in range(MAPS):
            chans = slice(CH1 * m, CH1 * (m + 1))
            s_ref[m, :CH1, here] = high[chans]
            s_ref[m, CH1 : 2 * CH1, here] = low[chans]
            s_ref[m, 2 * CH1 :, here] = high[chans]
    weights = weight_halves(w1_ref, 2 * CH1)
    parts = [dot(weights, s_ref[m]) for m in range(MAPS)]

    def slab(k, q):
        return jnp.concatenate(
            [part[CH0 * k : CH0 * (k + 1), 128 * q : 128 * (q + 1)] for part in parts], axis=0
        )

    def spread_rows(k, low, high, strips):
        left, right = (slab(k, slabs - 2), slab(k, slabs - 1)) if strips else (None, None)
        packed = [slab(k, q) for q in range(len(PAIRS))]
        rows = {}
        for row in range(low, high):
            q, half = WHERE[row]
            value = roll(packed[q], 64 * half)
            rows[row] = coarse_row(value, left, right, 2 * q + half) if strips else value
        return rows

    turns = coarse_turns(flags, CA)
    g0 = spread_rows(0, -1, CROWS + 1, False)
    g1 = spread_rows(1, 1 - UP2, CROWS + UP2 - 1, True)
    g2 = spread_rows(2, -UP2, CROWS + UP2, True)
    inner = {row: g1[row] + 2.0 * coarse_lap(g2, row, turns) for row in g1}
    doubled = lanes(CA) // 2
    for crow in range(-1, CROWS + 1):
        dx1 = g0[crow] - g2[crow] + coarse_lap(inner, crow, turns)
        dx1 = 0.25 * pick(dx1, doubled)
        for n in (2 * (crow + 1), 2 * (crow + 1) + 1):
            high, low = halves(dx1 * sig0_ref[n])
            here = pl.ds(n * 128, 128)
            d_ref[:CA, here] = high
            d_ref[CA : 2 * CA, here] = low
            d_ref[2 * CA :, here] = high
    both = dot_nt(terms_ref[...], d_ref[: 2 * CA, 2 * 128 : (2 + ROWS) * 128])
    lane = lanes(CI)
    row16 = lax.broadcasted_iota(jnp.int32, (CI, 128), 0)
    same = lane % CA // CH0 == row16 // BINS
    fine = []
    for k in range(ORDER):
        value = jnp.where(same, both[CI * k : CI * (k + 1)], 0.0)
        if k:
            low = both[CI * (2 + k) : CI * (3 + k)]
            value = value + jnp.where(same & (lane < CA), low, 0.0)
        for shift in (64, 32, 16):
            value = value + roll(value, shift)
        for shift in (8, 4):
            value = value + pltpu.roll(value, shift, 0)
        fine.append(value)
    value = jnp.where(row16 // BINS == 0, fine[0], jnp.where(row16 // BINS == 1, fine[1], fine[2]))
    for k in range(ORDER):
        value = jnp.where(lane // CH1 == k, coarse[k], value)
    for n in range(grads_ref.shape[0] // CI):
        grads_ref[CI * n : CI * (n + 1)] = value
    weights = weight_halves(w0_ref, 2 * CA)
    index = end_index(2 * CI)
    filled = []
    for n in range(0, ROWS + 4, 2):
        value = dot(weights, d_ref[:, n * 128 : (n + 2) * 128])
        for step in range(2):
            part = value[:, 128 * step : 128 * (step + 1)]
            g_ref[n + step] = part
            filled.append(pick(part[CI:], index))
    put_slots(ends_ref, filled, len(filled))


def saliency_kernel(flags, g_ref, far_ref, near_ref, out_ref, *, pixels):
    turns = fine_turns(flags, CI)
    left, right = both_strips(far_ref, near_ref, flags[7])
    g0, g1, g2, s1, s2 = {}, {}, {}, {}, {}
    for row in range(-2, ROWS + 2):
        value = g_ref[row + 2]
        g0[row], g1[row], g2[row] = (value[CI * k : CI * (k + 1)] for k in range(3))
        strip = fine_strip(left, right, row + 2)
        s1[row], s2[row] = strip[:CI], strip[CI:]
    inner, inner_strip = {}, {}
    for row in range(-1, ROWS + 1):
        value, strip = fine_lap(g2, s2, row, turns, True)
        inner[row] = g1[row] + 2.0 * value
        inner_strip[row] = s1[row] + 2.0 * strip
    for row in range(ROWS):
        outer = fine_lap(inner, inner_strip, row, turns, False)
        out_ref[pl.ds(row, CI, stride=ROWS), :] = (g0[row] - g2[row] + outer) * pixels


def again_kernel(in_ref, out_ref):
    value = in_ref[0:CI]
    for n in range(1, in_ref.shape[0] // CI):
        value = value + in_ref[CI * n : CI * (n + 1)]
    for n in range(out_ref.shape[0] // CI):
        out_ref[CI * n : CI * (n + 1)] = value


def row_again_kernel(in_ref, out_ref):
    out_ref[...] = jnp.broadcast_to(jnp.sum(in_ref[...], axis=0, keepdims=True), out_ref.shape)


def last_kernel(in_ref, fine_ref, coarse_ref, tmp_ref):
    value = in_ref[0:CI]
    for n in range(1, in_ref.shape[0] // CI):
        value = value + in_ref[CI * n : CI * (n + 1)]
    for k in range(ORDER):
        coarse_ref[k] = roll(value, -CH1 * k)[:, :CH1]
    tmp_ref[...] = roll(value, -ORDER * CH1)
    for k in range(ORDER):
        fine_ref[k] = tmp_ref[BINS * k : BINS * (k + 1), :CH0]


def call(kernel, outs, *args, smem=0, scratch=()):
    in_specs = [
        pl.BlockSpec(memory_space=pltpu.SMEM if n < smem else pltpu.VMEM) for n in range(len(args))
    ]
    return pl.pallas_call(
        kernel,
        out_shape=outs,
        in_specs=in_specs,
        out_specs=jax.tree.map(lambda _: pl.BlockSpec(memory_space=pltpu.VMEM), outs),
        scratch_shapes=list(scratch),
        compiler_params=pltpu.CompilerParams(vmem_limit_bytes=32 * 2**20),
    )(*args)


def shape(*dims, dtype=f32):
    return jax.ShapeDtypeStruct(dims, dtype)


def exchange(axis, far_value, near_value):
    count = lax.axis_size(axis)
    far = [(n, (n + (1 if n % 2 else count - 1)) % count) for n in range(count)]
    near = [(n, n + (1 if n % 2 == 0 else -1)) for n in range(count)]
    return lax.ppermute(far_value, axis, far), lax.ppermute(near_value, axis, near)


def share(rows, axes):
    return lax.all_to_all(rows, axes, 0, 0, tiled=True)


def on_device(
    maps, params, labels, edge_flip,
    fine_weight, coarse_weight, feature_weight, param_weight, out_weight,
):
    faces, tiles = lax.axis_size(FACE), lax.axis_size(TILE)
    f, t = lax.axis_index(FACE), lax.axis_index(TILE)
    columns = jnp.stack([(t + tiles - 1) % tiles, t, (t + 1) % tiles])
    flags = jnp.concatenate(
        [edge_flip[f][columns], edge_flip[(f + 1) % faces][columns], jnp.stack([f % 2, t % 2])]
    )
    eye = jnp.eye(MAPS, dtype=f32)
    fine = jnp.einsum("kio,mn->monki", fine_weight, eye)
    fine = fine.transpose(0, 1, 3, 2, 4).reshape(CA, ORDER * CI)
    fine_forward = jnp.concatenate([fine, fine[:, CI:], fine], axis=1)
    fine_backward = jnp.concatenate([fine.T] * 3, axis=1)
    coarse = coarse_weight.reshape(ORDER * CH0, CH1)
    coarse_forward = jnp.concatenate([coarse.T] * 3, axis=1)
    coarse_backward = jnp.concatenate([coarse] * 3, axis=1)
    features4 = jnp.concatenate([feature_weight] * MAPS, axis=0)
    pad = [(0, 8 - MAPS), (0, 0)]
    shift = jnp.dot(jnp.pad(params, pad), param_weight, precision=exact)
    labels8 = jnp.broadcast_to(jnp.pad(labels.astype(f32)[:, None], pad), (8, 128))

    trade = shape(UP0, CI, COLS)
    own, far, near = call(
        rows_kernel, (shape(ROWS, CI, COLS), trade, trade), flags, maps.reshape(CI * ROWS, COLS),
        smem=1,
        scratch=[pltpu.VMEM((CI * ROWS, COLS), f32)],
    )
    far, near = exchange(FACE, far, near)
    ends0 = call(ends_kernel, shape(groups(ROWS + 2 * UP0), CI, 128), flags, far, near, own, smem=1)
    far0, near0 = exchange(TILE, ends0, ends0)
    crows = CROWS + 2 * UP1
    x1, sig0, terms0, ends1 = call(
        fine_kernel,
        (
            shape(crows, CA, 128),
            shape(ROWS + 4, CA, 128),
            shape(5 * CI, ROWS * 128, dtype=bf16),
            shape(groups(crows), CA, 128),
        ),
        flags, far, near, own, far0, near0, fine_forward,
        smem=1,
        scratch=[pltpu.VMEM((8 * CI, 2 * crows * 128), bf16)],
    )
    far1, near1 = exchange(TILE, ends1, ends1)
    feats, sig1, ends2, grams = call(
        coarse_kernel,
        (
            shape(lax.axis_size(PLANE), CB),
            shape(len(PAIRS), CB, 128),
            shape(CB, 128),
            shape(ORDER, CH0, 128),
        ),
        flags, x1, far1, near1, coarse_forward,
        smem=1,
        scratch=[
            pltpu.VMEM((MAPS, 3 * ORDER * CH0, len(PAIRS) * 128), bf16),
            pltpu.VMEM((2 * CB, 4 * 128), bf16),
        ],
    )
    far2, near2 = exchange(TILE, ends2, ends2)
    feats = share(feats, PLANE)
    feats = call(row_again_kernel, shape(lax.axis_size("z"), CB), feats)
    feats = share(feats, "z")
    pooled = CROWS * faces * CCOLS * tiles
    logits, grads, g, ends3 = call(
        lambda *refs: back_kernel(*refs, pooled=pooled),
        (
            shape(8, 128),
            shape(lax.axis_size(PLANE) * CI, 128),
            shape(ROWS + 4, ORDER * CI, 128),
            shape(groups(ROWS + 4), 2 * CI, 128),
        ),
        flags, feats, shift, labels8, features4, out_weight[None],
        coarse_backward, fine_backward, sig1, far2, near2, grams, sig0, terms0,
        smem=1,
        scratch=[
            pltpu.VMEM((MAPS, 3 * CH1, (len(PAIRS) + 2) * 128), bf16),
            pltpu.VMEM((3 * CA, (ROWS + 4) * 128), bf16),
        ],
    )
    far3, near3 = exchange(TILE, ends3, ends3)
    grads = share(grads, PLANE)
    grads = call(again_kernel, shape(lax.axis_size("z") * CI, 128), grads)
    grads = share(grads, "z")
    pixels = float(ROWS * faces * COLS * tiles)
    saliency = call(
        lambda *refs: saliency_kernel(*refs, pixels=pixels),
        shape(CI * ROWS, COLS), flags, g, far3, near3,
        smem=1,
    )
    grad_f, grad_c = call(
        last_kernel, (shape(*fine_weight.shape), shape(*coarse_weight.shape)), grads,
        scratch=[pltpu.VMEM((CI, 128), f32)],
    )
    return (logits[:MAPS, 0], saliency.reshape(maps.shape), grad_f, grad_c)


def solution(mesh):
    faces, tiles = mesh.devices.shape
    sizes = (faces // 2, 2, tiles // 4, 2, 2)
    fine_mesh = jax.sharding.Mesh(mesh.devices.reshape(sizes), ("x", "y_lo", "z", "y_hi", "core"))
    tiled = P(None, None, FACE, TILE)
    return jax.shard_map(
        on_device,
        mesh=fine_mesh,
        in_specs=(tiled, P(), P(), P(), P(), P(), P(), P(), P()),
        out_specs=(P(), tiled, P(), P()),
        check_vma=False,
    )
```

```python
import jax
import jax.numpy as jnp
from jax import lax
from jax.experimental import pallas as pl
from jax.experimental.pallas import tpu as pltpu
from jax.sharding import PartitionSpec as P

exact = lax.Precision.HIGHEST
MAPS, BINS, CH0, CH1, ORDER = 4, 4, 16, 32, 3
ROWS, COLS = 16, 128
CROWS, CCOLS = ROWS // 2, COLS // 2
CI = MAPS * BINS
CA = MAPS * CH0
CB = MAPS * CH1
STRIP = 4
SLOT = 2 * STRIP
PER = 128 // SLOT
UP0 = 12
UP1 = 5
UP2 = 3
PAIRS = [(0, 4), (1, 5), (2, 6), (3, 7), (-3, 8), (-2, 9), (-1, 10)]
SLABS = len(PAIRS) + 2
OWN = 4
WHERE = {row: (q, half) for q, pair in enumerate(PAIRS) for half, row in enumerate(pair)}
FACE, TILE = ("x", "y_lo"), ("z", "y_hi", "core")
PLANE = ("x", "y_lo", "y_hi", "core")
FIRST, SECOND = ("z", "core"), ("x", "y_lo", "y_hi")
bf16, f32 = jnp.bfloat16, jnp.float32


def lanes(count):
    return lax.broadcasted_iota(jnp.int32, (count, 128), 1)


def pick(value, index):
    return jnp.take_along_axis(value, index, axis=1, mode="promise_in_bounds")


def roll(value, shift):
    shift %= 128
    return value if shift == 0 else pltpu.roll(value, shift, 1)


def halves(value):
    high = value.astype(bf16)
    return high, (value - high.astype(f32)).astype(bf16)


def weight_halves(ref, start):
    high, low = halves(ref[...])
    column = lax.broadcasted_iota(jnp.int32, ref.shape, 1)
    return jnp.where(column < start, high.astype(f32), low.astype(f32)).astype(bf16)


def dot(a, b):
    return jnp.dot(a, b, preferred_element_type=f32)


def dot_nt(a, b):
    return lax.dot_general(a, b, (((1,), (1,)), ((), ())), preferred_element_type=f32)


class Place:
    def __init__(self, flips=None):
        self.face, self.tile = lax.axis_index(FACE), lax.axis_index(TILE)
        self.odd_face, self.odd_tile = self.face % 2, self.tile % 2
        self.flips = flips

    def flags(self, side):
        faces, tiles = self.flips.shape
        face = (self.face + side) % faces
        return [self.flips[face, (self.tile + step) % tiles] for step in (tiles - 1, 0, 1)]


def fine_turns(place, count):
    lane = lanes(count)
    turns = []
    for side in range(2):
        left, own, right = place.flags(side)
        block = jnp.where(own == 1, 127 - lane, lane)
        strip = jnp.where(
            lane < 64,
            jnp.where((lane < SLOT) & (right == 1), SLOT - 1 - lane, lane),
            jnp.where((lane >= 128 - SLOT) & (left == 1), 255 - SLOT - lane, lane),
        )
        turns.append((block, strip))
    return turns


def coarse_turns(place, count):
    lane = lanes(count)
    turns = []
    for side in range(2):
        left, own, right = place.flags(side)
        index = jnp.where((lane < 64) & (own == 1), 63 - lane, lane)
        index = jnp.where((lane >= 64) & (lane < 64 + SLOT) & (right == 1), 127 + SLOT - lane, index)
        index = jnp.where((lane >= 128 - SLOT) & (left == 1), 255 - SLOT - lane, index)
        turns.append(index)
    return turns


def vertical(rows, row, height, top, bottom):
    if row == 0:
        upper = pick(rows[-1], top)
    elif row == height:
        upper = pick(rows[height - 1], bottom)
    else:
        upper = rows[row - 1]
    if row == -1:
        lower = pick(rows[0], top)
    elif row == height - 1:
        lower = pick(rows[height], bottom)
    else:
        lower = rows[row + 1]
    return upper + lower


def fine_lap(block, strip, row, turns, with_strip):
    (top, top_strip), (bottom, bottom_strip) = turns
    lane = lanes(block[row].shape[0])
    first, last = lane == 0, lane == 127
    b_right, s_right = roll(block[row], 1), roll(strip[row], 1)
    b_left, s_left = roll(block[row], -1), roll(strip[row], -1)
    side = jnp.where(first, s_right, b_right) + jnp.where(last, s_left, b_left)
    out = -0.25 * (vertical(block, row, ROWS, top, bottom) + side)
    if not with_strip:
        return out
    side = jnp.where(first, b_right, s_right) + jnp.where(last, b_left, s_left)
    return out, -0.25 * (vertical(strip, row, ROWS, top_strip, bottom_strip) + side)


def coarse_lap(rows, row, turns):
    value = rows[row]
    side = roll(value, 1) + roll(value, -1)
    return -0.25 * (vertical(rows, row, CROWS, turns[0], turns[1]) + side)


def end_index(count, stride=1, width=COLS):
    j = lanes(count) % SLOT
    return jnp.where(j < STRIP, j, width - SLOT + j) * stride


def fine_strip(left, right, place):
    group, slot = place // PER, place % PER
    lane = lanes(left[group].shape[0])
    return jnp.where(
        lane < 64, roll(right[group], -SLOT * slot), roll(left[group], 128 - SLOT - SLOT * slot)
    )


def coarse_row(block, left, right, slot):
    lane = lanes(block.shape[0])
    strip = jnp.where(
        lane < 96, roll(right, 64 - SLOT * slot), roll(left, 128 - SLOT - SLOT * slot)
    )
    return jnp.where(lane < 64, block, strip)


def groups(count):
    return -(-count // PER)


def put_slots(out_refs, filled, count):
    lane = lanes(filled[0].shape[0])
    for group in range(groups(count)):
        value = filled[group * PER]
        for n in range(group * PER + 1, min(count, group * PER + PER)):
            value = jnp.where(lane // SLOT == n % PER, filled[n], value)
        for out_ref in out_refs:
            out_ref[group] = value


def before(far, near, odd):
    return jnp.where(odd == 1, near, far)


def after(far, near, odd):
    return jnp.where(odd == 1, far, near)


def fine_rows(far_ref, near_ref, own_ref, odd):
    rows = {}
    for row in range(-UP0, ROWS + UP0):
        if row < 0:
            rows[row] = before(far_ref[UP0 + row], near_ref[UP0 + row], odd)
        elif row < ROWS:
            rows[row] = own_ref[row]
        else:
            rows[row] = after(far_ref[row - ROWS], near_ref[row - ROWS], odd)
    return rows


def rows_kernel(maps_ref, own_ref, far_ref, near_ref, t_ref):
    here = Place()
    t_ref[...] = maps_ref[...].astype(f32)
    rows = [t_ref[pl.ds(row, CI, stride=ROWS), :] for row in range(ROWS)]
    for row in range(ROWS):
        own_ref[row] = rows[row]
    for row in range(UP0):
        first, last = rows[row], rows[ROWS - UP0 + row]
        far_ref[row] = before(first, last, here.odd_face)
        near_ref[row] = after(first, last, here.odd_face)


def both_strips(far_ref, near_ref, odd):
    count = far_ref.shape[0]
    left = [before(far_ref[n], near_ref[n], odd) for n in range(count)]
    return left, [after(far_ref[n], near_ref[n], odd) for n in range(count)]


def ends_kernel(far_ref, near_ref, own_ref, *out_refs):
    index = end_index(CI)
    rows = fine_rows(far_ref, near_ref, own_ref, Place().odd_face)
    put_slots(out_refs, [pick(rows[row], index) for row in sorted(rows)], len(rows))


def fine_kernel(
    flips, far_ref, near_ref, own_ref, far0_ref, near0_ref, w_ref,
    x1_ref, sig_ref, terms_ref, ends_ref, ends_copy_ref, t_ref,
):
    here = Place(flips)
    turns = fine_turns(here, CI)
    block = fine_rows(far_ref, near_ref, own_ref, here.odd_face)
    left, right = both_strips(far0_ref, near0_ref, here.odd_tile)
    strip = {row: fine_strip(left, right, row + UP0) for row in block}
    first, first_strip = {}, {}
    for row in range(1 - UP0, ROWS + UP0 - 1):
        first[row], first_strip[row] = fine_lap(block, strip, row, turns, True)
    low, high = -2 * UP1, ROWS + 2 * UP1
    for row in range(low, high):
        second = 2.0 * fine_lap(first, first_strip, row, turns, False) - block[row]
        at = pl.ds((row - low) * 128, 128)
        one, one_low = halves(first[row])
        two, two_low = halves(second)
        for n, part in enumerate((block[row].astype(bf16), one, two, one_low, two_low)):
            t_ref[CI * n : CI * (n + 1), at] = part
        for n, part in enumerate((block[row].astype(bf16), one, two)):
            t_ref[CI * (5 + n) : CI * (6 + n), at] = part
    own = pl.ds(-low * 128, ROWS * 128)
    terms_ref[...] = t_ref[0 : 5 * CI, own]
    weights = weight_halves(w_ref, 5 * CI)
    lane = lanes(CA)
    even = 2 * (lane % 64)
    ends = end_index(CA, 2, CCOLS)
    filled = []
    for crow in range(-UP1, CROWS + UP1):
        place = crow + UP1
        pre = dot(weights, t_ref[:, place * 256 : place * 256 + 256])
        decay = jnp.exp(-jnp.abs(pre))
        act = jnp.maximum(pre, 0.0) + jnp.log(1.0 + decay)
        if -1 <= crow <= CROWS:
            inverse = 1.0 / (1.0 + decay)
            sig = jnp.where(pre >= 0, inverse, decay * inverse)
            sig_ref[2 * (crow + 1)] = sig[:, :128]
            sig_ref[2 * (crow + 1) + 1] = sig[:, 128:]
        both = act[:, :128] + act[:, 128:]
        both = 0.25 * (both + roll(both, -1))
        x1_ref[place] = pick(both, even)
        filled.append(pick(both, ends))
    put_slots((ends_ref, ends_copy_ref), filled, len(filled))


def coarse_kernel(
    flips, x1_ref, far_ref, near_ref, w_ref, feat_ref, sig_ref, t_ref
):
    here = Place(flips)
    turns = coarse_turns(here, CA)
    lane = lanes(CA)
    left, right = both_strips(far_ref, near_ref, here.odd_tile)
    rows = {}
    for row in range(-UP1, CROWS + UP1):
        place = row + UP1
        rows[row] = coarse_row(
            x1_ref[place], left[place // PER], right[place // PER], place % PER
        )
    first = {row: coarse_lap(rows, row, turns) for row in range(1 - UP1, CROWS + UP1 - 1)}
    second = {
        row: 2.0 * coarse_lap(first, row, turns) - rows[row]
        for row in range(-UP2, CROWS + UP2)
    }
    for q, (a, b) in enumerate(PAIRS):
        at = pl.ds(q * 128, 128)
        for k, term in enumerate((rows, first, second)):
            packed = jnp.where(lane < 64, term[a], roll(term[b], 64))
            high, low = halves(packed)
            for m in range(MAPS):
                chans = slice(CH0 * m, CH0 * (m + 1))
                t_ref[m, CH0 * k : CH0 * (k + 1), at] = high[chans]
                t_ref[m, CH0 * (3 + k) : CH0 * (4 + k), at] = low[chans]
                t_ref[m, CH0 * (6 + k) : CH0 * (7 + k), at] = high[chans]
    weights = weight_halves(w_ref, 2 * ORDER * CH0)
    own = OWN * 128
    sums = []
    for m in range(MAPS):
        pre = dot(weights, t_ref[m])
        decay = jnp.exp(-jnp.abs(pre))
        inverse = 1.0 / (1.0 + decay)
        sig = jnp.where(pre >= 0, inverse, decay * inverse)
        act = jnp.maximum(pre[:, :own], 0.0) + jnp.log(1.0 + decay[:, :own])
        sums.append(sum(act[:, 128 * q : 128 * (q + 1)] for q in range(OWN)))
        for q in range(len(PAIRS)):
            sig_ref[q, CH1 * m : CH1 * (m + 1)] = sig[:, 128 * q : 128 * (q + 1)]
    total = jnp.sum(jnp.concatenate(sums, axis=0).T, axis=0, keepdims=True)
    feat_ref[...] = jnp.broadcast_to(total, feat_ref.shape)


def gram_kernel(sig_ref, t_ref, ends_ref, ends_copy_ref, gram_ref, s_ref):
    j = lanes(CB) % SLOT
    column = jnp.where(j < STRIP, j, CCOLS - SLOT + j)
    index = jnp.where(lanes(CB) // SLOT % 2 == 0, column, 64 + column)
    ends = jnp.zeros((CB, 128), f32)
    for q in range(len(PAIRS)):
        value = sig_ref[q]
        ends = jnp.where(lanes(CB) // (2 * SLOT) == q, pick(value, index), ends)
        if q < OWN:
            s_ref[:CB, 128 * q : 128 * (q + 1)], s_ref[CB:, 128 * q : 128 * (q + 1)] = halves(value)
    ends_ref[...] = ends
    ends_copy_ref[...] = ends
    grams = [jnp.zeros((CH0, 128), f32) for _ in range(ORDER)]
    for m in range(MAPS):
        both = dot_nt(t_ref[m, : 2 * ORDER * CH0, : OWN * 128], s_ref[...])
        for k in range(ORDER):
            high = both[CH0 * k : CH0 * (k + 1)]
            low = both[CH0 * (3 + k) : CH0 * (4 + k)]
            value = high[:, :CB] + high[:, CB:] + low[:, :CB]
            grams[k] = jnp.where(lanes(CH0) // CH1 == m, value, grams[k])
    for k in range(ORDER):
        gram_ref[k] = grams[k]


def split_kernel(
    sig1_ref, far_ref, near_ref, shift_ref, labels_ref, out_ref, s_ref, head_ref
):
    here = Place()
    for q in range(SLABS):
        if q < len(PAIRS):
            value = sig1_ref[q]
        else:
            value = (before, after)[q - len(PAIRS)](far_ref[...], near_ref[...], here.odd_tile)
        high, low = halves(value)
        at = pl.ds(q * 128, 128)
        for m in range(MAPS):
            chans = slice(CH1 * m, CH1 * (m + 1))
            s_ref[m, :CH1, at] = high[chans]
            s_ref[m, CH1 : 2 * CH1, at] = low[chans]
            s_ref[m, 2 * CH1 :, at] = high[chans]
    head_ref[0] = shift_ref[...]
    head_ref[1] = labels_ref[...]
    head_ref[2] = jnp.broadcast_to(out_ref[...], (8, 128))


def back_kernel(
    flips, feat_ref, head_ref, fw_ref, w1_ref, s_ref, gram_ref, sig0_ref, terms_ref,
    logits_ref, grads_ref, d_ref,
    *, pooled,
):
    here = Place(flips)
    features = jnp.sum(feat_ref[...], axis=0, keepdims=True) * (1.0 / pooled)
    row8 = lax.broadcasted_iota(jnp.int32, (8, 128), 0)
    spread = jnp.where(lanes(8) // CH1 == row8, jnp.broadcast_to(features, (8, 128)), 0.0)
    fw = fw_ref[...]
    shift, labels, out = head_ref[0], head_ref[1], head_ref[2]
    hidden = jnp.tanh(
        jnp.dot(spread, fw, precision=exact, preferred_element_type=f32) + shift
    )
    logits = jnp.sum(hidden * out, axis=1, keepdims=True)
    logits_ref[...] = jnp.broadcast_to(logits, (8, 128))
    decay = jnp.exp(-jnp.abs(logits))
    dlogit = jnp.where(logits >= 0, 1.0, decay) / (1.0 + decay) - labels
    dhidden = dlogit * out * (1.0 - hidden * hidden)
    dhidden = jnp.concatenate(
        [jnp.broadcast_to(dhidden[m : m + 1], (CH1, 128)) for m in range(MAPS)], axis=0
    )
    dcol = jnp.sum(fw * dhidden, axis=1, keepdims=True) * (1.0 / pooled)
    dfull = jnp.broadcast_to(dcol, (CB, 128))
    drow = jnp.broadcast_to(dfull.T[:1], (CH0, 128))
    coarse = []
    for k in range(ORDER):
        value = gram_ref[k] * drow
        value = value + roll(value, 64)
        coarse.append(value + roll(value, 32))
    weighted = w1_ref[...] * jnp.broadcast_to(drow[:1], w1_ref.shape)
    lane = lanes(w1_ref.shape[0])
    parts = []
    for m in range(MAPS):
        weights = jnp.where(lane // CH1 == m, weighted, 0.0)
        weights = weights + roll(weights, 64)
        high, low = halves(weights + roll(weights, 32))
        weights = jnp.where(lane < 2 * CH1, high.astype(f32), low.astype(f32)).astype(bf16)
        parts.append(dot(weights[:, : 3 * CH1], s_ref[m]))

    def slab(k, q):
        return jnp.concatenate(
            [part[CH0 * k : CH0 * (k + 1), 128 * q : 128 * (q + 1)] for part in parts], axis=0
        )

    def spread_rows(k, low, high, strips):
        left, right = (slab(k, SLABS - 2), slab(k, SLABS - 1)) if strips else (None, None)
        packed = [slab(k, q) for q in range(len(PAIRS))]
        rows = {}
        for row in range(low, high):
            q, half = WHERE[row]
            value = roll(packed[q], 64 * half)
            rows[row] = coarse_row(value, left, right, 2 * q + half) if strips else value
        return rows

    turns = coarse_turns(here, CA)
    g0 = spread_rows(0, -1, CROWS + 1, False)
    g1 = spread_rows(1, 1 - UP2, CROWS + UP2 - 1, True)
    g2 = spread_rows(2, -UP2, CROWS + UP2, True)
    inner = {row: g1[row] + 2.0 * coarse_lap(g2, row, turns) for row in g1}
    doubled = lanes(CA) // 2
    for crow in range(-1, CROWS + 1):
        dx1 = g0[crow] - g2[crow] + coarse_lap(inner, crow, turns)
        dx1 = 0.25 * pick(dx1, doubled)
        for n in (2 * (crow + 1), 2 * (crow + 1) + 1):
            high, low = halves(dx1 * sig0_ref[n])
            at = pl.ds(n * 128, 128)
            d_ref[:CA, at] = high
            d_ref[CA : 2 * CA, at] = low
            d_ref[2 * CA :, at] = high
    both = dot_nt(terms_ref[...], d_ref[: 2 * CA, 2 * 128 : (2 + ROWS) * 128])
    lane = lanes(CI)
    row16 = lax.broadcasted_iota(jnp.int32, (CI, 128), 0)
    same = lane % CA // CH0 == row16 // BINS
    fine = []
    for k in range(ORDER):
        value = jnp.where(same, both[CI * k : CI * (k + 1)], 0.0)
        if k:
            low = both[CI * (2 + k) : CI * (3 + k)]
            value = value + jnp.where(same & (lane < CA), low, 0.0)
        for shift in (64, 32, 16):
            value = value + roll(value, shift)
        for shift in (8, 4):
            value = value + pltpu.roll(value, shift, 0)
        fine.append(value)
    value = jnp.where(row16 // BINS == 0, fine[0], jnp.where(row16 // BINS == 1, fine[1], fine[2]))
    for k in range(ORDER):
        value = jnp.where(lane // CH1 == k, coarse[k], value)
    for n in range(grads_ref.shape[0] // CI):
        grads_ref[CI * n : CI * (n + 1)] = value


def terms_kernel(d_ref, w0_ref, g_ref, ends_ref, ends_copy_ref):
    weights = weight_halves(w0_ref, 2 * CA)
    index = end_index(2 * CI)
    filled = []
    for n in range(0, ROWS + 4, 2):
        value = dot(weights, d_ref[:, n * 128 : (n + 2) * 128])
        for step in range(2):
            part = value[:, 128 * step : 128 * (step + 1)]
            g_ref[n + step] = part
            filled.append(pick(part[CI:], index))
    put_slots((ends_ref, ends_copy_ref), filled, len(filled))


def saliency_kernel(flips, g_ref, far_ref, near_ref, out_ref, *, pixels):
    here = Place(flips)
    turns = fine_turns(here, CI)
    left, right = both_strips(far_ref, near_ref, here.odd_tile)
    g0, g1, g2, s1, s2 = {}, {}, {}, {}, {}
    for row in range(-2, ROWS + 2):
        value = g_ref[row + 2]
        g0[row], g1[row], g2[row] = (value[CI * k : CI * (k + 1)] for k in range(3))
        strip = fine_strip(left, right, row + 2)
        s1[row], s2[row] = strip[:CI], strip[CI:]
    inner, inner_strip = {}, {}
    for row in range(-1, ROWS + 1):
        value, strip = fine_lap(g2, s2, row, turns, True)
        inner[row] = g1[row] + 2.0 * value
        inner_strip[row] = s1[row] + 2.0 * strip
    for row in range(ROWS):
        outer = fine_lap(inner, inner_strip, row, turns, False)
        out_ref[pl.ds(row, CI, stride=ROWS), :] = (g0[row] - g2[row] + outer) * pixels


def again_kernel(in_ref, out_ref):
    value = in_ref[0:CI]
    for n in range(1, in_ref.shape[0] // CI):
        value = value + in_ref[CI * n : CI * (n + 1)]
    for n in range(out_ref.shape[0] // CI):
        out_ref[CI * n : CI * (n + 1)] = value


def row_again_kernel(in_ref, out_ref):
    out_ref[...] = jnp.broadcast_to(jnp.sum(in_ref[...], axis=0, keepdims=True), out_ref.shape)


def last_kernel(in_ref, fine_ref, coarse_ref, tmp_ref):
    value = in_ref[0:CI]
    for n in range(1, in_ref.shape[0] // CI):
        value = value + in_ref[CI * n : CI * (n + 1)]
    for k in range(ORDER):
        coarse_ref[k] = roll(value, -CH1 * k)[:, :CH1]
    tmp_ref[...] = roll(value, -ORDER * CH1)
    for k in range(ORDER):
        fine_ref[k] = tmp_ref[BINS * k : BINS * (k + 1), :CH0]


def call(kernel, outs, *args, smem=0, scratch=()):
    in_specs = [
        pl.BlockSpec(memory_space=pltpu.SMEM if n < smem else pltpu.VMEM) for n in range(len(args))
    ]
    return pl.pallas_call(
        kernel,
        out_shape=outs,
        in_specs=in_specs,
        out_specs=jax.tree.map(lambda _: pl.BlockSpec(memory_space=pltpu.VMEM), outs),
        scratch_shapes=list(scratch),
        compiler_params=pltpu.CompilerParams(vmem_limit_bytes=32 * 2**20),
    )(*args)


def shape(*dims, dtype=f32):
    return jax.ShapeDtypeStruct(dims, dtype)


def exchange(axis, far_value, near_value):
    count = lax.axis_size(axis)
    far = [(n, (n + (1 if n % 2 else count - 1)) % count) for n in range(count)]
    near = [(n, n + (1 if n % 2 == 0 else -1)) for n in range(count)]
    return lax.ppermute(far_value, axis, far), lax.ppermute(near_value, axis, near)


def share(rows, axes):
    return lax.all_to_all(rows, axes, 0, 0, tiled=True)


def on_device(
    maps, params, labels, edge_flip,
    fine_weight, coarse_weight, feature_weight, param_weight, out_weight,
):
    faces, tiles = lax.axis_size(FACE), lax.axis_size(TILE)
    eye = jnp.eye(MAPS, dtype=f32)
    fine = jnp.einsum("kio,mn->monki", fine_weight, eye)
    fine = fine.transpose(0, 1, 3, 2, 4).reshape(CA, ORDER * CI)
    fine_forward = jnp.concatenate([fine, fine[:, CI:], fine], axis=1)
    fine_backward = jnp.concatenate([fine.T] * 3, axis=1)
    coarse = coarse_weight.reshape(ORDER * CH0, CH1)
    coarse_forward = jnp.concatenate([coarse.T] * 3, axis=1)
    coarse_backward = jnp.concatenate([coarse] * MAPS, axis=1)
    features4 = jnp.concatenate([feature_weight] * MAPS, axis=0)
    pad = [(0, 8 - MAPS), (0, 0)]
    shift = jnp.dot(jnp.pad(params, pad), param_weight, precision=exact)
    labels8 = jnp.broadcast_to(jnp.pad(labels.astype(f32)[:, None], pad), (8, 128))

    trade = shape(UP0, CI, COLS)
    own, far, near = call(
        rows_kernel, (shape(ROWS, CI, COLS), trade, trade), maps.reshape(CI * ROWS, COLS),
        scratch=[pltpu.VMEM((CI * ROWS, COLS), f32)],
    )
    far, near = exchange(FACE, far, near)
    trade = shape(groups(ROWS + 2 * UP0), CI, 128)
    far0, near0 = call(ends_kernel, (trade, trade), far, near, own)
    far0, near0 = exchange(TILE, far0, near0)
    crows = CROWS + 2 * UP1
    trade = shape(groups(crows), CA, 128)
    x1, sig0, terms0, far1, near1 = call(
        fine_kernel,
        (
            shape(crows, CA, 128),
            shape(ROWS + 4, CA, 128),
            shape(5 * CI, ROWS * 128, dtype=bf16),
            trade,
            trade,
        ),
        edge_flip, far, near, own, far0, near0, fine_forward,
        smem=1,
        scratch=[pltpu.VMEM((8 * CI, 2 * crows * 128), bf16)],
    )
    far1, near1 = exchange(TILE, far1, near1)
    feats, sig1, terms1 = call(
        coarse_kernel,
        (
            shape(lax.axis_size(FIRST), CB),
            shape(len(PAIRS), CB, 128),
            shape(MAPS, 3 * ORDER * CH0, len(PAIRS) * 128, dtype=bf16),
        ),
        edge_flip, x1, far1, near1, coarse_forward,
        smem=1,
    )
    feats = share(feats, FIRST)
    feats = call(row_again_kernel, shape(lax.axis_size(SECOND), CB), feats)
    trade = shape(CB, 128)
    far2, near2, grams = call(
        gram_kernel, (trade, trade, shape(ORDER, CH0, 128)), sig1, terms1,
        scratch=[pltpu.VMEM((2 * CB, OWN * 128), bf16)],
    )
    feats = share(feats, SECOND)
    far2, near2 = exchange(TILE, far2, near2)
    pooled = CROWS * faces * CCOLS * tiles
    split1, head = call(
        split_kernel,
        (shape(MAPS, 3 * CH1, SLABS * 128, dtype=bf16), shape(3, 8, 128)),
        sig1, far2, near2, shift, labels8, out_weight[None],
    )
    logits, grads, dpre0 = call(
        lambda *refs: back_kernel(*refs, pooled=pooled),
        (
            shape(8, 128),
            shape(lax.axis_size(PLANE) * CI, 128),
            shape(3 * CA, (ROWS + 4) * 128, dtype=bf16),
        ),
        edge_flip, feats, head, features4, coarse_backward, split1, grams, sig0, terms0,
        smem=1,
    )
    grads = share(grads, PLANE)
    trade = shape(groups(ROWS + 4), 2 * CI, 128)
    g, far3, near3 = call(
        terms_kernel, (shape(ROWS + 4, ORDER * CI, 128), trade, trade), dpre0, fine_backward
    )
    far3, near3 = exchange(TILE, far3, near3)
    grads = call(again_kernel, shape(lax.axis_size("z") * CI, 128), grads)
    grads = share(grads, "z")
    pixels = float(ROWS * faces * COLS * tiles)
    saliency = call(
        lambda *refs: saliency_kernel(*refs, pixels=pixels),
        shape(CI * ROWS, COLS), edge_flip, g, far3, near3,
        smem=1,
    )
    grad_f, grad_c = call(
        last_kernel, (shape(*fine_weight.shape), shape(*coarse_weight.shape)), grads,
        scratch=[pltpu.VMEM((CI, 128), f32)],
    )
    return (logits[:MAPS, 0], saliency.reshape(maps.shape), grad_f, grad_c)


def solution(mesh):
    faces, tiles = mesh.devices.shape
    sizes = (faces // 2, 2, tiles // 4, 2, 2)
    fine_mesh = jax.sharding.Mesh(mesh.devices.reshape(sizes), ("x", "y_lo", "z", "y_hi", "core"))
    tiled = P(None, None, FACE, TILE)
    return jax.shard_map(
        on_device,
        mesh=fine_mesh,
        in_specs=(tiled, P(), P(), P(), P(), P(), P(), P(), P()),
        out_specs=(P(), tiled, P(), P()),
        check_vma=False,
    )
```

```python
import jax
import jax.numpy as jnp
from jax import lax
from jax.experimental import pallas as pl
from jax.experimental.pallas import tpu as pltpu
from jax.sharding import PartitionSpec as P

exact = lax.Precision.HIGHEST
MAPS, BINS, CH0, CH1, ORDER = 4, 4, 16, 32, 3
ROWS, COLS = 16, 128
CROWS, CCOLS = ROWS // 2, COLS // 2
CI = MAPS * BINS
CA = MAPS * CH0
CB = MAPS * CH1
STRIP = 2
SLOT = 2 * STRIP
PER = 128 // SLOT
UP0 = 12
UP1 = 5
UP2 = 3
PAIRS = [(0, 4), (1, 5), (2, 6), (3, 7), (-3, 8), (-2, 9), (-1, 10)]
OWN = 4
WHERE = {row: (q, half) for q, pair in enumerate(PAIRS) for half, row in enumerate(pair)}
FACE, TILE = ("x", "y_lo"), ("z", "y_hi", "core")
PLANE = ("x", "y_lo", "y_hi", "core")
FIRST, SECOND = ("z", "core"), ("x", "y_lo", "y_hi")
bf16, f32 = jnp.bfloat16, jnp.float32


def lanes(count):
    return lax.broadcasted_iota(jnp.int32, (count, 128), 1)


def pick(value, index):
    return jnp.take_along_axis(value, index, axis=1, mode="promise_in_bounds")


def roll(value, shift):
    shift %= 128
    return value if shift == 0 else pltpu.roll(value, shift, 1)


def halves(value):
    high = value.astype(bf16)
    return high, (value - high.astype(f32)).astype(bf16)


def weight_halves(ref, start):
    high, low = halves(ref[...])
    column = lax.broadcasted_iota(jnp.int32, ref.shape, 1)
    return jnp.where(column < start, high.astype(f32), low.astype(f32)).astype(bf16)


def dot(a, b):
    return jnp.dot(a, b, preferred_element_type=f32)


def dot_nt(a, b):
    return lax.dot_general(a, b, (((1,), (1,)), ((), ())), preferred_element_type=f32)


class Place:
    def __init__(self, flips=None):
        self.face, self.tile = lax.axis_index(FACE), lax.axis_index(TILE)
        self.odd_face, self.odd_tile = self.face % 2, self.tile % 2
        self.flips = flips

    def flags(self, side):
        faces, tiles = self.flips.shape
        face = (self.face + side) % faces
        return [self.flips[face, (self.tile + step) % tiles] for step in (tiles - 1, 0, 1)]


def fine_turns(place, count):
    lane = lanes(count)
    turns = []
    for side in range(2):
        left, own, right = place.flags(side)
        block = jnp.where(own == 1, 127 - lane, lane)
        strip = jnp.where(
            lane < 64,
            jnp.where((lane < SLOT) & (right == 1), SLOT - 1 - lane, lane),
            jnp.where((lane >= 128 - SLOT) & (left == 1), 255 - SLOT - lane, lane),
        )
        turns.append((block, strip))
    return turns


def coarse_turns(place, count):
    lane = lanes(count)
    turns = []
    for side in range(2):
        left, own, right = place.flags(side)
        index = jnp.where((lane < 64) & (own == 1), 63 - lane, lane)
        index = jnp.where((lane >= 64) & (lane < 64 + SLOT) & (right == 1), 127 + SLOT - lane, index)
        index = jnp.where((lane >= 128 - SLOT) & (left == 1), 255 - SLOT - lane, index)
        turns.append(index)
    return turns


def vertical(rows, row, height, top, bottom):
    if row == 0:
        upper = pick(rows[-1], top)
    elif row == height:
        upper = pick(rows[height - 1], bottom)
    else:
        upper = rows[row - 1]
    if row == -1:
        lower = pick(rows[0], top)
    elif row == height - 1:
        lower = pick(rows[height], bottom)
    else:
        lower = rows[row + 1]
    return upper + lower


def fine_lap(block, strip, row, turns, with_strip):
    (top, top_strip), (bottom, bottom_strip) = turns
    lane = lanes(block[row].shape[0])
    first, last = lane == 0, lane == 127
    b_right, s_right = roll(block[row], 1), roll(strip[row], 1)
    b_left, s_left = roll(block[row], -1), roll(strip[row], -1)
    side = jnp.where(first, s_right, b_right) + jnp.where(last, s_left, b_left)
    out = -0.25 * (vertical(block, row, ROWS, top, bottom) + side)
    if not with_strip:
        return out
    side = jnp.where(first, b_right, s_right) + jnp.where(last, b_left, s_left)
    return out, -0.25 * (vertical(strip, row, ROWS, top_strip, bottom_strip) + side)


def coarse_laps(rows, low, high, turns, around, ref):
    count = rows[low].shape[0]
    for n, row in enumerate(range(low, high)):
        side_by_side(ref, slice(count * n, count * (n + 1)), rows[row])
    sides = dot(ref[0 : count * (high - low)], around)
    return {
        row: sides[count * n : count * (n + 1)] - 0.25 * vertical(rows, row, CROWS, *turns)
        for n, row in enumerate(range(low, high))
    }


def grid(rows, columns):
    return (lax.broadcasted_iota(jnp.int32, (rows, columns), axis) for axis in range(2))


def ring(length, copies=1):
    i, j = grid(length * copies, length)
    step = (i - j + length) % length
    return jnp.where((step == 1) | (step == length - 1), -0.25, 0.0).astype(bf16)


def side_by_side(ref, at, value):
    high, low = halves(value)
    width = value.shape[1]
    ref[at, :width], ref[at, width:] = high, low


def end_index(count, stride=1, width=COLS):
    j = lanes(count) % SLOT
    return jnp.where(j < STRIP, j, width - SLOT + j) * stride


def fine_strip(left, right, place):
    group, slot = place // PER, place % PER
    lane = lanes(left[group].shape[0])
    return jnp.where(
        lane < 64, roll(right[group], -SLOT * slot), roll(left[group], 128 - SLOT - SLOT * slot)
    )


def coarse_row(block, left, right, slot):
    lane = lanes(block.shape[0])
    strip = jnp.where(
        lane < 96, roll(right, 64 - SLOT * slot), roll(left, 128 - SLOT - SLOT * slot)
    )
    return jnp.where(lane < 64, block, strip)


def groups(count):
    return -(-count // PER)


def put_slots(out_refs, filled, count):
    lane = lanes(filled[0].shape[0])
    for group in range(groups(count)):
        value = filled[group * PER]
        for n in range(group * PER + 1, min(count, group * PER + PER)):
            value = jnp.where(lane // SLOT == n % PER, filled[n], value)
        for out_ref in out_refs:
            out_ref[group] = value


def before(far, near, odd):
    return jnp.where(odd == 1, near, far)


def after(far, near, odd):
    return jnp.where(odd == 1, far, near)


def fine_rows(far_ref, near_ref, own_ref, odd):
    rows = {}
    for row in range(-UP0, ROWS + UP0):
        if row < 0:
            rows[row] = before(far_ref[UP0 + row], near_ref[UP0 + row], odd)
        elif row < ROWS:
            rows[row] = own_ref[row]
        else:
            rows[row] = after(far_ref[row - ROWS], near_ref[row - ROWS], odd)
    return rows


def rows_kernel(maps_ref, own_ref, far_ref, near_ref, t_ref):
    here = Place()
    t_ref[...] = maps_ref[...].astype(f32)
    rows = [t_ref[pl.ds(row, CI, stride=ROWS), :] for row in range(ROWS)]
    for row in range(ROWS):
        own_ref[row] = rows[row]
    for row in range(UP0):
        first, last = rows[row], rows[ROWS - UP0 + row]
        far_ref[row] = before(first, last, here.odd_face)
        near_ref[row] = after(first, last, here.odd_face)


def both_strips(far_ref, near_ref, odd):
    count = far_ref.shape[0]
    left = [before(far_ref[n], near_ref[n], odd) for n in range(count)]
    return left, [after(far_ref[n], near_ref[n], odd) for n in range(count)]


def ends_kernel(far_ref, near_ref, own_ref, *out_refs):
    index = end_index(CI)
    rows = fine_rows(far_ref, near_ref, own_ref, Place().odd_face)
    put_slots(out_refs, [pick(rows[row], index) for row in sorted(rows)], len(rows))


def fine_kernel(
    flips, far_ref, near_ref, own_ref, far0_ref, near0_ref, w_ref,
    x1_ref, sig_ref, terms_ref, ends_ref, ends_copy_ref, t_ref, x_ref, y_ref, a_ref,
):
    here = Place(flips)
    turns = fine_turns(here, CI)
    block = fine_rows(far_ref, near_ref, own_ref, here.odd_face)
    left, right = both_strips(far0_ref, near0_ref, here.odd_tile)
    strip = {row: fine_strip(left, right, row + UP0) for row in block}
    around = ring(256)
    for n, row in enumerate(sorted(block)):
        x_ref[CI * n : CI * (n + 1), :128] = block[row].astype(bf16)
        x_ref[CI * n : CI * (n + 1), 128:] = strip[row].astype(bf16)
    sides = dot(x_ref[...], around)
    (top, top_strip), (bottom, bottom_strip) = turns
    first, split = {}, {}
    for n, row in enumerate(range(1 - UP0, ROWS + UP0 - 1)):
        side = sides[CI * (n + 1) : CI * (n + 2)]
        first[row] = side[:, :128] - 0.25 * vertical(block, row, ROWS, top, bottom)
        other = side[:, 128:] - 0.25 * vertical(strip, row, ROWS, top_strip, bottom_strip)
        split[row] = halves(first[row])
        at = slice(CI * n, CI * (n + 1))
        y_ref[at, :128], y_ref[at, 256:384] = split[row]
        y_ref[at, 128:256], y_ref[at, 384:] = halves(other)
    around = around[:, :128]
    sides = dot(y_ref[:, :256], around) + dot(y_ref[:, 256:], around)
    low, high = -2 * UP1, ROWS + 2 * UP1
    for n, row in enumerate(range(low, high)):
        lap = sides[CI * (n + 1) : CI * (n + 2)] - 0.25 * vertical(first, row, ROWS, top, bottom)
        at = pl.ds(n * 128, 128)
        zero = block[row].astype(bf16)
        one, one_low = split[row]
        two, two_low = halves(2.0 * lap - block[row])
        for k, part in enumerate((zero, one, two, one_low, two_low, zero, one, two)):
            t_ref[CI * k : CI * (k + 1), at] = part
    own = pl.ds(-low * 128, ROWS * 128)
    terms_ref[...] = t_ref[0 : 5 * CI, own]
    weights = weight_halves(w_ref, 5 * CI)
    for crow in range(-UP1, CROWS + UP1):
        place = crow + UP1
        pre = dot(weights, t_ref[:, place * 256 : place * 256 + 256])
        decay = jnp.exp(-jnp.abs(pre))
        act = jnp.maximum(pre, 0.0) + jnp.log(1.0 + decay)
        if -1 <= crow <= CROWS:
            inverse = 1.0 / (1.0 + decay)
            sig = jnp.where(pre >= 0, inverse, decay * inverse)
            sig_ref[2 * (crow + 1)] = sig[:, :128]
            sig_ref[2 * (crow + 1) + 1] = sig[:, 128:]
        side_by_side(a_ref, slice(CA * place, CA * (place + 1)), act[:, :128] + act[:, 128:])
    i, j = grid(256, 256)
    slot = j % SLOT
    end = jnp.where(slot < STRIP, slot, CCOLS - SLOT + slot)
    column = jnp.where(j < 128, j, end)
    means = dot(a_ref[...], jnp.where(i % 128 // 2 == column, 0.25, 0.0).astype(bf16))
    filled = []
    for place in range(CROWS + 2 * UP1):
        value = means[CA * place : CA * (place + 1)]
        x1_ref[place] = value[:, :128]
        filled.append(value[:, 128:])
    put_slots((ends_ref, ends_copy_ref), filled, len(filled))


def coarse_kernel(
    flips, x1_ref, far_ref, near_ref, w_ref, feat_ref, sig_ref, t_ref, z_ref
):
    here = Place(flips)
    turns = coarse_turns(here, CA)
    lane = lanes(CA)
    left, right = both_strips(far_ref, near_ref, here.odd_tile)
    rows = {}
    for row in range(-UP1, CROWS + UP1):
        place = row + UP1
        rows[row] = coarse_row(
            x1_ref[place], left[place // PER], right[place // PER], place % PER
        )
    around = ring(128, 2)
    first = coarse_laps(rows, 1 - UP1, CROWS + UP1 - 1, turns, around, z_ref)
    second = coarse_laps(first, -UP2, CROWS + UP2, turns, around, z_ref)
    second = {row: 2.0 * second[row] - rows[row] for row in second}
    for q, (a, b) in enumerate(PAIRS):
        at = pl.ds(q * 128, 128)
        for k, term in enumerate((rows, first, second)):
            packed = jnp.where(lane < 64, term[a], roll(term[b], 64))
            high, low = halves(packed)
            for m in range(MAPS):
                chans = slice(CH0 * m, CH0 * (m + 1))
                t_ref[m, CH0 * k : CH0 * (k + 1), at] = high[chans]
                t_ref[m, CH0 * (3 + k) : CH0 * (4 + k), at] = low[chans]
                t_ref[m, CH0 * (6 + k) : CH0 * (7 + k), at] = high[chans]
    weights = weight_halves(w_ref, 2 * ORDER * CH0)
    own = OWN * 128
    sums = []
    for m in range(MAPS):
        pre = dot(weights, t_ref[m])
        decay = jnp.exp(-jnp.abs(pre))
        inverse = 1.0 / (1.0 + decay)
        sig = jnp.where(pre >= 0, inverse, decay * inverse)
        act = jnp.maximum(pre[:, :own], 0.0) + jnp.log(1.0 + decay[:, :own])
        sums.append(sum(act[:, 128 * q : 128 * (q + 1)] for q in range(OWN)))
        for q in range(len(PAIRS)):
            sig_ref[q, CH1 * m : CH1 * (m + 1)] = sig[:, 128 * q : 128 * (q + 1)]
    total = jnp.sum(jnp.concatenate(sums, axis=0).T, axis=0, keepdims=True)
    feat_ref[...] = jnp.broadcast_to(total, feat_ref.shape)


def gram_kernel(sig_ref, t_ref, ends_ref, ends_copy_ref, gram_ref, s_ref):
    j = lanes(CB) % SLOT
    column = jnp.where(j < STRIP, j, CCOLS - SLOT + j)
    index = jnp.where(lanes(CB) // SLOT % 2 == 0, column, 64 + column)
    ends = jnp.zeros((CB, 128), f32)
    for q in range(len(PAIRS)):
        value = sig_ref[q]
        ends = jnp.where(lanes(CB) // (2 * SLOT) == q, pick(value, index), ends)
        if q < OWN:
            s_ref[:CB, 128 * q : 128 * (q + 1)], s_ref[CB:, 128 * q : 128 * (q + 1)] = halves(value)
    ends_ref[...] = ends
    ends_copy_ref[...] = ends
    grams = [jnp.zeros((CH0, 128), f32) for _ in range(ORDER)]
    for m in range(MAPS):
        both = dot_nt(t_ref[m, : 2 * ORDER * CH0, : OWN * 128], s_ref[...])
        for k in range(ORDER):
            high = both[CH0 * k : CH0 * (k + 1)]
            low = both[CH0 * (3 + k) : CH0 * (4 + k)]
            value = high[:, :CB] + high[:, CB:] + low[:, :CB]
            grams[k] = jnp.where(lanes(CH0) // CH1 == m, value, grams[k])
    for k in range(ORDER):
        gram_ref[k] = grams[k]


def split_kernel(
    sig1_ref, far_ref, near_ref, shift_ref, labels_ref, out_ref, s_ref, head_ref
):
    here = Place()
    left = before(far_ref[...], near_ref[...], here.odd_tile)
    right = after(far_ref[...], near_ref[...], here.odd_tile)
    for n, row in enumerate(range(-UP2, CROWS + UP2)):
        q, half = WHERE[row]
        value = coarse_row(roll(sig1_ref[q], 64 * half), left, right, 2 * q + half)
        high, low = halves(value)
        at = pl.ds(n * 128, 128)
        for m in range(MAPS):
            chans = slice(CH1 * m, CH1 * (m + 1))
            s_ref[m, :CH1, at] = high[chans]
            s_ref[m, CH1 : 2 * CH1, at] = low[chans]
            s_ref[m, 2 * CH1 :, at] = high[chans]
    head_ref[0] = shift_ref[...]
    head_ref[1] = labels_ref[...]
    head_ref[2] = jnp.broadcast_to(out_ref[...], (8, 128))


def back_kernel(
    flips, feat_ref, head_ref, fw_ref, w1_ref, s_ref, gram_ref, sig0_ref, terms_ref,
    logits_ref, grads_ref, d_ref, z_ref,
    *, pooled,
):
    here = Place(flips)
    features = jnp.sum(feat_ref[...], axis=0, keepdims=True) * (1.0 / pooled)
    row8 = lax.broadcasted_iota(jnp.int32, (8, 128), 0)
    apart = jnp.where(lanes(8) // CH1 == row8, jnp.broadcast_to(features, (8, 128)), 0.0)
    fw = fw_ref[...]
    shift, labels, out = head_ref[0], head_ref[1], head_ref[2]
    hidden = jnp.tanh(
        jnp.dot(apart, fw, precision=exact, preferred_element_type=f32) + shift
    )
    logits = jnp.sum(hidden * out, axis=1, keepdims=True)
    logits_ref[...] = jnp.broadcast_to(logits, (8, 128))
    decay = jnp.exp(-jnp.abs(logits))
    dlogit = jnp.where(logits >= 0, 1.0, decay) / (1.0 + decay) - labels
    dhidden = dlogit * out * (1.0 - hidden * hidden)
    dhidden = jnp.concatenate(
        [jnp.broadcast_to(dhidden[m : m + 1], (CH1, 128)) for m in range(MAPS)], axis=0
    )
    dcol = jnp.sum(fw * dhidden, axis=1, keepdims=True) * (1.0 / pooled)
    dfull = jnp.broadcast_to(dcol, (CB, 128))
    drow = jnp.broadcast_to(dfull.T[:1], (CH0, 128))
    coarse = []
    for k in range(ORDER):
        value = gram_ref[k] * drow
        value = value + roll(value, 64)
        coarse.append(value + roll(value, 32))
    weighted = w1_ref[...] * jnp.broadcast_to(drow[:1], w1_ref.shape)
    lane = lanes(w1_ref.shape[0])
    parts = []
    for m in range(MAPS):
        weights = jnp.where(lane // CH1 == m, weighted, 0.0)
        weights = weights + roll(weights, 64)
        high, low = halves(weights + roll(weights, 32))
        weights = jnp.where(lane < 2 * CH1, high.astype(f32), low.astype(f32)).astype(bf16)
        parts.append(dot(weights[:, : 3 * CH1], s_ref[m]))

    def term(k, low, high):
        rows = {}
        for row in range(low, high):
            at = slice(128 * (row + UP2), 128 * (row + UP2 + 1))
            rows[row] = jnp.concatenate([part[CH0 * k : CH0 * (k + 1), at] for part in parts], axis=0)
        return rows

    turns = coarse_turns(here, CA)
    around = ring(128, 2)
    g0 = term(0, -1, CROWS + 1)
    g1 = term(1, 1 - UP2, CROWS + UP2 - 1)
    g2 = term(2, -UP2, CROWS + UP2)
    inner = coarse_laps(g2, 1 - UP2, CROWS + UP2 - 1, turns, around, z_ref)
    inner = {row: g1[row] + 2.0 * inner[row] for row in g1}
    outer = coarse_laps(inner, -1, CROWS + 1, turns, around, z_ref)
    for n, crow in enumerate(range(-1, CROWS + 1)):
        at = slice(CA * n, CA * (n + 1))
        side_by_side(z_ref, at, g0[crow] - g2[crow] + outer[crow])
    i, j = grid(256, 128)
    doubled = jnp.where(i % 128 == j // 2, 0.25, 0.0).astype(bf16)
    spread = dot(z_ref[0 : CA * (CROWS + 2)], doubled)
    for n in range(ROWS + 4):
        value = spread[CA * (n // 2) : CA * (n // 2 + 1)]
        high, low = halves(value * sig0_ref[n])
        at = pl.ds(n * 128, 128)
        d_ref[:CA, at] = high
        d_ref[CA : 2 * CA, at] = low
        d_ref[2 * CA :, at] = high
    both = dot_nt(terms_ref[...], d_ref[: 2 * CA, 2 * 128 : (2 + ROWS) * 128])
    lane = lanes(CI)
    row16 = lax.broadcasted_iota(jnp.int32, (CI, 128), 0)
    same = lane % CA // CH0 == row16 // BINS
    fine = []
    for k in range(ORDER):
        value = jnp.where(same, both[CI * k : CI * (k + 1)], 0.0)
        if k:
            low = both[CI * (2 + k) : CI * (3 + k)]
            value = value + jnp.where(same & (lane < CA), low, 0.0)
        for shift in (64, 32, 16):
            value = value + roll(value, shift)
        for shift in (8, 4):
            value = value + pltpu.roll(value, shift, 0)
        fine.append(value)
    value = jnp.where(row16 // BINS == 0, fine[0], jnp.where(row16 // BINS == 1, fine[1], fine[2]))
    for k in range(ORDER):
        value = jnp.where(lane // CH1 == k, coarse[k], value)
    for n in range(grads_ref.shape[0] // CI):
        grads_ref[CI * n : CI * (n + 1)] = value


def terms_kernel(d_ref, w0_ref, g_ref, ends_ref, ends_copy_ref):
    weights = weight_halves(w0_ref, 2 * CA)
    index = end_index(2 * CI)
    filled = []
    for n in range(0, ROWS + 4, 2):
        value = dot(weights, d_ref[:, n * 128 : (n + 2) * 128])
        for step in range(2):
            part = value[:, 128 * step : 128 * (step + 1)]
            g_ref[n + step] = part
            filled.append(pick(part[CI:], index))
    put_slots((ends_ref, ends_copy_ref), filled, len(filled))


def saliency_kernel(flips, g_ref, far_ref, near_ref, out_ref, *, pixels):
    here = Place(flips)
    turns = fine_turns(here, CI)
    left, right = both_strips(far_ref, near_ref, here.odd_tile)
    g0, g1, g2, s1, s2 = {}, {}, {}, {}, {}
    for row in range(-2, ROWS + 2):
        value = g_ref[row + 2]
        g0[row], g1[row], g2[row] = (value[CI * k : CI * (k + 1)] for k in range(3))
        strip = fine_strip(left, right, row + 2)
        s1[row], s2[row] = strip[:CI], strip[CI:]
    inner, inner_strip = {}, {}
    for row in range(-1, ROWS + 1):
        value, strip = fine_lap(g2, s2, row, turns, True)
        inner[row] = g1[row] + 2.0 * value
        inner_strip[row] = s1[row] + 2.0 * strip
    for row in range(ROWS):
        outer = fine_lap(inner, inner_strip, row, turns, False)
        out_ref[pl.ds(row, CI, stride=ROWS), :] = (g0[row] - g2[row] + outer) * pixels


def again_kernel(in_ref, out_ref):
    value = in_ref[0:CI]
    for n in range(1, in_ref.shape[0] // CI):
        value = value + in_ref[CI * n : CI * (n + 1)]
    for n in range(out_ref.shape[0] // CI):
        out_ref[CI * n : CI * (n + 1)] = value


def row_again_kernel(in_ref, out_ref):
    out_ref[...] = jnp.broadcast_to(jnp.sum(in_ref[...], axis=0, keepdims=True), out_ref.shape)


def last_kernel(in_ref, fine_ref, coarse_ref, tmp_ref):
    value = in_ref[0:CI]
    for n in range(1, in_ref.shape[0] // CI):
        value = value + in_ref[CI * n : CI * (n + 1)]
    for k in range(ORDER):
        coarse_ref[k] = roll(value, -CH1 * k)[:, :CH1]
    tmp_ref[...] = roll(value, -ORDER * CH1)
    for k in range(ORDER):
        fine_ref[k] = tmp_ref[BINS * k : BINS * (k + 1), :CH0]


def call(kernel, outs, *args, smem=0, scratch=()):
    in_specs = [
        pl.BlockSpec(memory_space=pltpu.SMEM if n < smem else pltpu.VMEM) for n in range(len(args))
    ]
    return pl.pallas_call(
        kernel,
        out_shape=outs,
        in_specs=in_specs,
        out_specs=jax.tree.map(lambda _: pl.BlockSpec(memory_space=pltpu.VMEM), outs),
        scratch_shapes=list(scratch),
        compiler_params=pltpu.CompilerParams(vmem_limit_bytes=32 * 2**20),
    )(*args)


def shape(*dims, dtype=f32):
    return jax.ShapeDtypeStruct(dims, dtype)


def exchange(axis, far_value, near_value):
    count = lax.axis_size(axis)
    far = [(n, (n + (1 if n % 2 else count - 1)) % count) for n in range(count)]
    near = [(n, n + (1 if n % 2 == 0 else -1)) for n in range(count)]
    return lax.ppermute(far_value, axis, far), lax.ppermute(near_value, axis, near)


def share(rows, axes):
    return lax.all_to_all(rows, axes, 0, 0, tiled=True)


def on_device(
    maps, params, labels, edge_flip,
    fine_weight, coarse_weight, feature_weight, param_weight, out_weight,
):
    faces, tiles = lax.axis_size(FACE), lax.axis_size(TILE)
    eye = jnp.eye(MAPS, dtype=f32)
    fine = jnp.einsum("kio,mn->monki", fine_weight, eye)
    fine = fine.transpose(0, 1, 3, 2, 4).reshape(CA, ORDER * CI)
    fine_forward = jnp.concatenate([fine, fine[:, CI:], fine], axis=1)
    fine_backward = jnp.concatenate([fine.T] * 3, axis=1)
    coarse = coarse_weight.reshape(ORDER * CH0, CH1)
    coarse_forward = jnp.concatenate([coarse.T] * 3, axis=1)
    coarse_backward = jnp.concatenate([coarse] * MAPS, axis=1)
    features4 = jnp.concatenate([feature_weight] * MAPS, axis=0)
    pad = [(0, 8 - MAPS), (0, 0)]
    shift = jnp.dot(jnp.pad(params, pad), param_weight, precision=exact)
    labels8 = jnp.broadcast_to(jnp.pad(labels.astype(f32)[:, None], pad), (8, 128))

    trade = shape(UP0, CI, COLS)
    own, far, near = call(
        rows_kernel, (shape(ROWS, CI, COLS), trade, trade), maps.reshape(CI * ROWS, COLS),
        scratch=[pltpu.VMEM((CI * ROWS, COLS), f32)],
    )
    far, near = exchange(FACE, far, near)
    trade = shape(groups(ROWS + 2 * UP0), CI, 128)
    far0, near0 = call(ends_kernel, (trade, trade), far, near, own)
    far0, near0 = exchange(TILE, far0, near0)
    crows = CROWS + 2 * UP1
    trade = shape(groups(crows), CA, 128)
    x1, sig0, terms0, far1, near1 = call(
        fine_kernel,
        (
            shape(crows, CA, 128),
            shape(ROWS + 4, CA, 128),
            shape(5 * CI, ROWS * 128, dtype=bf16),
            trade,
            trade,
        ),
        edge_flip, far, near, own, far0, near0, fine_forward,
        smem=1,
        scratch=[
            pltpu.VMEM((8 * CI, 2 * crows * 128), bf16),
            pltpu.VMEM(((ROWS + 2 * UP0) * CI, 256), bf16),
            pltpu.VMEM(((ROWS + 2 * UP0 - 2) * CI, 512), bf16),
            pltpu.VMEM((crows * CA, 256), bf16),
        ],
    )
    far1, near1 = exchange(TILE, far1, near1)
    feats, sig1, terms1 = call(
        coarse_kernel,
        (
            shape(lax.axis_size(FIRST), CB),
            shape(len(PAIRS), CB, 128),
            shape(MAPS, 3 * ORDER * CH0, len(PAIRS) * 128, dtype=bf16),
        ),
        edge_flip, x1, far1, near1, coarse_forward,
        smem=1,
        scratch=[pltpu.VMEM((crows * CA, 256), bf16)],
    )
    feats = share(feats, FIRST)
    feats = call(row_again_kernel, shape(lax.axis_size(SECOND), CB), feats)
    trade = shape(CB, 128)
    far2, near2, grams = call(
        gram_kernel, (trade, trade, shape(ORDER, CH0, 128)), sig1, terms1,
        scratch=[pltpu.VMEM((2 * CB, OWN * 128), bf16)],
    )
    feats = share(feats, SECOND)
    far2, near2 = exchange(TILE, far2, near2)
    pooled = CROWS * faces * CCOLS * tiles
    split1, head = call(
        split_kernel,
        (shape(MAPS, 3 * CH1, (CROWS + 2 * UP2) * 128, dtype=bf16), shape(3, 8, 128)),
        sig1, far2, near2, shift, labels8, out_weight[None],
    )
    logits, grads, dpre0 = call(
        lambda *refs: back_kernel(*refs, pooled=pooled),
        (
            shape(8, 128),
            shape(lax.axis_size(PLANE) * CI, 128),
            shape(3 * CA, (ROWS + 4) * 128, dtype=bf16),
        ),
        edge_flip, feats, head, features4, coarse_backward, split1, grams, sig0, terms0,
        smem=1,
        scratch=[pltpu.VMEM(((CROWS + 2 * UP2) * CA, 256), bf16)],
    )
    grads = share(grads, PLANE)
    trade = shape(groups(ROWS + 4), 2 * CI, 128)
    g, far3, near3 = call(
        terms_kernel, (shape(ROWS + 4, ORDER * CI, 128), trade, trade), dpre0, fine_backward
    )
    far3, near3 = exchange(TILE, far3, near3)
    grads = call(again_kernel, shape(lax.axis_size("z") * CI, 128), grads)
    grads = share(grads, "z")
    pixels = float(ROWS * faces * COLS * tiles)
    saliency = call(
        lambda *refs: saliency_kernel(*refs, pixels=pixels),
        shape(CI * ROWS, COLS), edge_flip, g, far3, near3,
        smem=1,
    )
    grad_f, grad_c = call(
        last_kernel, (shape(*fine_weight.shape), shape(*coarse_weight.shape)), grads,
        scratch=[pltpu.VMEM((CI, 128), f32)],
    )
    return (logits[:MAPS, 0], saliency.reshape(maps.shape), grad_f, grad_c)


def solution(mesh):
    faces, tiles = mesh.devices.shape
    sizes = (faces // 2, 2, tiles // 4, 2, 2)
    fine_mesh = jax.sharding.Mesh(mesh.devices.reshape(sizes), ("x", "y_lo", "z", "y_hi", "core"))
    tiled = P(None, None, FACE, TILE)
    return jax.shard_map(
        on_device,
        mesh=fine_mesh,
        in_specs=(tiled, P(), P(), P(), P(), P(), P(), P(), P()),
        out_specs=(P(), tiled, P(), P()),
        check_vma=False,
    )
```

```python
import jax
import jax.numpy as jnp
from jax import lax
from jax.experimental import pallas as pl
from jax.experimental.pallas import tpu as pltpu
from jax.sharding import PartitionSpec as P

exact = lax.Precision.HIGHEST
MAPS, BINS, CH0, CH1, ORDER = 4, 4, 16, 32, 3
ROWS, COLS = 16, 128
CROWS, CCOLS = ROWS // 2, COLS // 2
CI = MAPS * BINS
CA = MAPS * CH0
CB = MAPS * CH1
STRIP = 2
SLOT = 2 * STRIP
PER = 128 // SLOT
UP0 = 12
UP1 = 5
UP2 = 3
PAIRS = [(0, 4), (1, 5), (2, 6), (3, 7), (-3, 8), (-2, 9), (-1, 10)]
OWN = 4
WHERE = {row: (q, half) for q, pair in enumerate(PAIRS) for half, row in enumerate(pair)}
FACE, TILE = ("x", "y_lo"), ("z", "y_hi", "core")
PLANE = ("x", "y_lo", "y_hi", "core")
FIRST, SECOND = ("z", "core"), ("x", "y_lo", "y_hi")
bf16, f32 = jnp.bfloat16, jnp.float32


def lanes(count):
    return lax.broadcasted_iota(jnp.int32, (count, 128), 1)


def pick(value, index):
    return jnp.take_along_axis(value, index, axis=1, mode="promise_in_bounds")


def roll(value, shift):
    shift %= 128
    return value if shift == 0 else pltpu.roll(value, shift, 1)


def halves(value):
    high = value.astype(bf16)
    return high, (value - high.astype(f32)).astype(bf16)


def weight_halves(ref, start):
    high, low = halves(ref[...])
    column = lax.broadcasted_iota(jnp.int32, ref.shape, 1)
    return jnp.where(column < start, high.astype(f32), low.astype(f32)).astype(bf16)


def dot(a, b):
    return jnp.dot(a, b, preferred_element_type=f32)


def dot_nt(a, b):
    return lax.dot_general(a, b, (((1,), (1,)), ((), ())), preferred_element_type=f32)


class Place:
    def __init__(self, flips=None):
        self.face, self.tile = lax.axis_index(FACE), lax.axis_index(TILE)
        self.odd_face, self.odd_tile = self.face % 2, self.tile % 2
        self.flips = flips

    def flags(self, side):
        faces, tiles = self.flips.shape
        face = (self.face + side) % faces
        return [self.flips[face, (self.tile + step) % tiles] for step in (tiles - 1, 0, 1)]


def fine_turns(place, count):
    lane = lanes(count)
    turns = []
    for side in range(2):
        left, own, right = place.flags(side)
        block = jnp.where(own == 1, 127 - lane, lane)
        strip = jnp.where(
            lane < 64,
            jnp.where((lane < SLOT) & (right == 1), SLOT - 1 - lane, lane),
            jnp.where((lane >= 128 - SLOT) & (left == 1), 255 - SLOT - lane, lane),
        )
        turns.append((block, strip))
    return turns


def coarse_turns(place, count):
    lane = lanes(count)
    turns = []
    for side in range(2):
        left, own, right = place.flags(side)
        index = jnp.where((lane < 64) & (own == 1), 63 - lane, lane)
        index = jnp.where((lane >= 64) & (lane < 64 + SLOT) & (right == 1), 127 + SLOT - lane, index)
        index = jnp.where((lane >= 128 - SLOT) & (left == 1), 255 - SLOT - lane, index)
        turns.append(index)
    return turns


def vertical(rows, row, height, top, bottom):
    if row == 0:
        upper = pick(rows[-1], top)
    elif row == height:
        upper = pick(rows[height - 1], bottom)
    else:
        upper = rows[row - 1]
    if row == -1:
        lower = pick(rows[0], top)
    elif row == height - 1:
        lower = pick(rows[height], bottom)
    else:
        lower = rows[row + 1]
    return upper + lower


def fine_lap(block, strip, row, turns, with_strip):
    (top, top_strip), (bottom, bottom_strip) = turns
    lane = lanes(block[row].shape[0])
    first, last = lane == 0, lane == 127
    b_right, s_right = roll(block[row], 1), roll(strip[row], 1)
    b_left, s_left = roll(block[row], -1), roll(strip[row], -1)
    side = jnp.where(first, s_right, b_right) + jnp.where(last, s_left, b_left)
    out = -0.25 * (vertical(block, row, ROWS, top, bottom) + side)
    if not with_strip:
        return out
    side = jnp.where(first, b_right, s_right) + jnp.where(last, b_left, s_left)
    return out, -0.25 * (vertical(strip, row, ROWS, top_strip, bottom_strip) + side)


def coarse_laps(rows, low, high, turns, around, ref):
    count = rows[low].shape[0]
    for n, row in enumerate(range(low, high)):
        side_by_side(ref, slice(count * n, count * (n + 1)), rows[row])
    sides = dot(ref[0 : count * (high - low)], around)
    return {
        row: sides[count * n : count * (n + 1)] - 0.25 * vertical(rows, row, CROWS, *turns)
        for n, row in enumerate(range(low, high))
    }


def grid(rows, columns):
    return (lax.broadcasted_iota(jnp.int32, (rows, columns), axis) for axis in range(2))


def ring(length, copies=1):
    i, j = grid(length * copies, length)
    step = (i - j + length) % length
    return jnp.where((step == 1) | (step == length - 1), -0.25, 0.0).astype(bf16)


def side_by_side(ref, at, value):
    high, low = halves(value)
    width = value.shape[1]
    ref[at, :width], ref[at, width:] = high, low


def end_index(count, stride=1, width=COLS):
    j = lanes(count) % SLOT
    return jnp.where(j < STRIP, j, width - SLOT + j) * stride


def fine_strip(left, right, place):
    group, slot = place // PER, place % PER
    lane = lanes(left[group].shape[0])
    return jnp.where(
        lane < 64, roll(right[group], -SLOT * slot), roll(left[group], 128 - SLOT - SLOT * slot)
    )


def coarse_row(block, left, right, slot):
    lane = lanes(block.shape[0])
    strip = jnp.where(
        lane < 96, roll(right, 64 - SLOT * slot), roll(left, 128 - SLOT - SLOT * slot)
    )
    return jnp.where(lane < 64, block, strip)


def groups(count):
    return -(-count // PER)


def put_slots(out_refs, filled, count):
    lane = lanes(filled[0].shape[0])
    for group in range(groups(count)):
        value = filled[group * PER]
        for n in range(group * PER + 1, min(count, group * PER + PER)):
            value = jnp.where(lane // SLOT == n % PER, filled[n], value)
        for out_ref in out_refs:
            out_ref[group] = value


def before(far, near, odd):
    return jnp.where(odd == 1, near, far)


def after(far, near, odd):
    return jnp.where(odd == 1, far, near)


def fine_rows(far_ref, near_ref, own_ref, odd):
    rows = {}
    for row in range(-UP0, ROWS + UP0):
        if row < 0:
            rows[row] = before(far_ref[UP0 + row], near_ref[UP0 + row], odd)
        elif row < ROWS:
            rows[row] = own_ref[row]
        else:
            rows[row] = after(far_ref[row - ROWS], near_ref[row - ROWS], odd)
    return rows


def rows_kernel(maps_ref, own_ref, far_ref, near_ref, t_ref):
    here = Place()
    t_ref[...] = maps_ref[...].astype(f32)
    rows = [t_ref[pl.ds(row, CI, stride=ROWS), :] for row in range(ROWS)]
    for row in range(ROWS):
        own_ref[row] = rows[row]
    for row in range(UP0):
        first, last = rows[row], rows[ROWS - UP0 + row]
        far_ref[row] = before(first, last, here.odd_face)
        near_ref[row] = after(first, last, here.odd_face)


def both_strips(far_ref, near_ref, odd):
    count = far_ref.shape[0]
    left = [before(far_ref[n], near_ref[n], odd) for n in range(count)]
    return left, [after(far_ref[n], near_ref[n], odd) for n in range(count)]


def ends_kernel(far_ref, near_ref, own_ref, *out_refs):
    index = end_index(CI)
    rows = fine_rows(far_ref, near_ref, own_ref, Place().odd_face)
    put_slots(out_refs, [pick(rows[row], index) for row in sorted(rows)], len(rows))


def fine_kernel(
    flips, far_ref, near_ref, own_ref, far0_ref, near0_ref, w_ref,
    x1_ref, sig_ref, terms_ref, ends_ref, ends_copy_ref, t_ref, x_ref, y_ref, a_ref,
):
    here = Place(flips)
    turns = fine_turns(here, CI)
    block = fine_rows(far_ref, near_ref, own_ref, here.odd_face)
    left, right = both_strips(far0_ref, near0_ref, here.odd_tile)
    strip = {row: fine_strip(left, right, row + UP0) for row in block}
    around = ring(256)
    for n, row in enumerate(sorted(block)):
        x_ref[CI * n : CI * (n + 1), :128] = block[row].astype(bf16)
        x_ref[CI * n : CI * (n + 1), 128:] = strip[row].astype(bf16)
    sides = dot(x_ref[...], around)
    (top, top_strip), (bottom, bottom_strip) = turns
    first, split = {}, {}
    for n, row in enumerate(range(1 - UP0, ROWS + UP0 - 1)):
        side = sides[CI * (n + 1) : CI * (n + 2)]
        first[row] = side[:, :128] - 0.25 * vertical(block, row, ROWS, top, bottom)
        other = side[:, 128:] - 0.25 * vertical(strip, row, ROWS, top_strip, bottom_strip)
        split[row] = halves(first[row])
        at = slice(CI * n, CI * (n + 1))
        y_ref[at, :128], y_ref[at, 256:384] = split[row]
        y_ref[at, 128:256], y_ref[at, 384:] = halves(other)
    around = around[:, :128]
    sides = dot(y_ref[:, :256], around) + dot(y_ref[:, 256:], around)
    low, high = -2 * UP1, ROWS + 2 * UP1
    for n, row in enumerate(range(low, high)):
        lap = sides[CI * (n + 1) : CI * (n + 2)] - 0.25 * vertical(first, row, ROWS, top, bottom)
        at = pl.ds(n * 128, 128)
        zero = block[row].astype(bf16)
        one, one_low = split[row]
        two, two_low = halves(2.0 * lap - block[row])
        for k, part in enumerate((zero, one, two, one_low, two_low, zero, one, two)):
            t_ref[CI * k : CI * (k + 1), at] = part
    own = pl.ds(-low * 128, ROWS * 128)
    terms_ref[...] = t_ref[0 : 5 * CI, own]
    weights = weight_halves(w_ref, 5 * CI)
    for crow in range(-UP1, CROWS + UP1):
        place = crow + UP1
        pre = dot(weights, t_ref[:, place * 256 : place * 256 + 256])
        decay = jnp.exp(-jnp.abs(pre))
        act = jnp.maximum(pre, 0.0) + jnp.log(1.0 + decay)
        if -1 <= crow <= CROWS:
            inverse = 1.0 / (1.0 + decay)
            sig = jnp.where(pre >= 0, inverse, decay * inverse)
            sig_ref[2 * (crow + 1)] = sig[:, :128]
            sig_ref[2 * (crow + 1) + 1] = sig[:, 128:]
        side_by_side(a_ref, slice(CA * place, CA * (place + 1)), act[:, :128] + act[:, 128:])
    i, j = grid(256, 256)
    slot = j % SLOT
    end = jnp.where(slot < STRIP, slot, CCOLS - SLOT + slot)
    column = jnp.where(j < 128, j, end)
    means = dot(a_ref[...], jnp.where(i % 128 // 2 == column, 0.25, 0.0).astype(bf16))
    filled = []
    for place in range(CROWS + 2 * UP1):
        value = means[CA * place : CA * (place + 1)]
        x1_ref[place] = value[:, :128]
        filled.append(value[:, 128:])
    put_slots((ends_ref, ends_copy_ref), filled, len(filled))


def coarse_kernel(
    flips, x1_ref, far_ref, near_ref, w_ref, feat_ref, sig_ref, t_ref, z_ref
):
    here = Place(flips)
    turns = coarse_turns(here, CA)
    lane = lanes(CA)
    left, right = both_strips(far_ref, near_ref, here.odd_tile)
    rows = {}
    for row in range(-UP1, CROWS + UP1):
        place = row + UP1
        rows[row] = coarse_row(
            x1_ref[place], left[place // PER], right[place // PER], place % PER
        )
    around = ring(128, 2)
    first = coarse_laps(rows, 1 - UP1, CROWS + UP1 - 1, turns, around, z_ref)
    second = coarse_laps(first, -UP2, CROWS + UP2, turns, around, z_ref)
    second = {row: 2.0 * second[row] - rows[row] for row in second}
    for q, (a, b) in enumerate(PAIRS):
        at = pl.ds(q * 128, 128)
        for k, term in enumerate((rows, first, second)):
            packed = jnp.where(lane < 64, term[a], roll(term[b], 64))
            high, low = halves(packed)
            for m in range(MAPS):
                chans = slice(CH0 * m, CH0 * (m + 1))
                t_ref[m, CH0 * k : CH0 * (k + 1), at] = high[chans]
                t_ref[m, CH0 * (3 + k) : CH0 * (4 + k), at] = low[chans]
                t_ref[m, CH0 * (6 + k) : CH0 * (7 + k), at] = high[chans]
    weights = weight_halves(w_ref, 2 * ORDER * CH0)
    own = OWN * 128
    sums = []
    for m in range(MAPS):
        pre = dot(weights, t_ref[m])
        decay = jnp.exp(-jnp.abs(pre))
        inverse = 1.0 / (1.0 + decay)
        sig = jnp.where(pre >= 0, inverse, decay * inverse)
        act = jnp.maximum(pre[:, :own], 0.0) + jnp.log(1.0 + decay[:, :own])
        sums.append(sum(act[:, 128 * q : 128 * (q + 1)] for q in range(OWN)))
        for q in range(len(PAIRS)):
            sig_ref[q, CH1 * m : CH1 * (m + 1)] = sig[:, 128 * q : 128 * (q + 1)]
    total = jnp.sum(jnp.concatenate(sums, axis=0).T, axis=0, keepdims=True)
    feat_ref[...] = jnp.broadcast_to(total, feat_ref.shape)


def gram_kernel(sig_ref, t_ref, ends_ref, ends_copy_ref, gram_ref, s_ref):
    j = lanes(CB) % SLOT
    column = jnp.where(j < STRIP, j, CCOLS - SLOT + j)
    index = jnp.where(lanes(CB) // SLOT % 2 == 0, column, 64 + column)
    ends = jnp.zeros((CB, 128), f32)
    for q in range(len(PAIRS)):
        value = sig_ref[q]
        ends = jnp.where(lanes(CB) // (2 * SLOT) == q, pick(value, index), ends)
        if q < OWN:
            s_ref[:CB, 128 * q : 128 * (q + 1)], s_ref[CB:, 128 * q : 128 * (q + 1)] = halves(value)
    ends_ref[...] = ends
    ends_copy_ref[...] = ends
    grams = [jnp.zeros((CH0, 128), f32) for _ in range(ORDER)]
    for m in range(MAPS):
        both = dot_nt(t_ref[m, : 2 * ORDER * CH0, : OWN * 128], s_ref[...])
        for k in range(ORDER):
            high = both[CH0 * k : CH0 * (k + 1)]
            low = both[CH0 * (3 + k) : CH0 * (4 + k)]
            value = high[:, :CB] + high[:, CB:] + low[:, :CB]
            grams[k] = jnp.where(lanes(CH0) // CH1 == m, value, grams[k])
    for k in range(ORDER):
        gram_ref[k] = grams[k]


def split_kernel(
    sig1_ref, far_ref, near_ref, shift_ref, labels_ref, out_ref, s_ref, head_ref
):
    here = Place()
    left = before(far_ref[...], near_ref[...], here.odd_tile)
    right = after(far_ref[...], near_ref[...], here.odd_tile)
    for n, row in enumerate(range(-UP2, CROWS + UP2)):
        q, half = WHERE[row]
        value = coarse_row(roll(sig1_ref[q], 64 * half), left, right, 2 * q + half)
        high, low = halves(value)
        at = pl.ds(n * 128, 128)
        for m in range(MAPS):
            chans = slice(CH1 * m, CH1 * (m + 1))
            s_ref[m, :CH1, at] = high[chans]
            s_ref[m, CH1:, at] = low[chans]
    head_ref[0] = shift_ref[...]
    head_ref[1] = labels_ref[...]
    head_ref[2] = jnp.broadcast_to(out_ref[...], (8, 128))


def back_kernel(
    flips, feat_ref, head_ref, fw_ref, w1_ref, s_ref, gram_ref, sig0_ref, terms_ref,
    logits_ref, grads_ref, d_ref, z_ref,
    *, pooled,
):
    here = Place(flips)
    features = jnp.sum(feat_ref[...], axis=0, keepdims=True) * (1.0 / pooled)
    row8 = lax.broadcasted_iota(jnp.int32, (8, 128), 0)
    apart = jnp.where(lanes(8) // CH1 == row8, jnp.broadcast_to(features, (8, 128)), 0.0)
    fw = fw_ref[...]
    shift, labels, out = head_ref[0], head_ref[1], head_ref[2]
    hidden = jnp.tanh(
        jnp.dot(apart, fw, precision=exact, preferred_element_type=f32) + shift
    )
    logits = jnp.sum(hidden * out, axis=1, keepdims=True)
    logits_ref[...] = jnp.broadcast_to(logits, (8, 128))
    decay = jnp.exp(-jnp.abs(logits))
    dlogit = jnp.where(logits >= 0, 1.0, decay) / (1.0 + decay) - labels
    dhidden = dlogit * out * (1.0 - hidden * hidden)
    dhidden = jnp.concatenate(
        [jnp.broadcast_to(dhidden[m : m + 1], (CH1, 128)) for m in range(MAPS)], axis=0
    )
    dcol = jnp.sum(fw * dhidden, axis=1, keepdims=True) * (1.0 / pooled)
    dfull = jnp.broadcast_to(dcol, (CB, 128))
    drow = jnp.broadcast_to(dfull.T[:1], (CH0, 128))
    coarse = []
    for k in range(ORDER):
        value = gram_ref[k] * drow
        value = value + roll(value, 64)
        coarse.append(value + roll(value, 32))
    weighted = w1_ref[...] * jnp.broadcast_to(drow[:1], w1_ref.shape)
    lane = lanes(w1_ref.shape[0])
    parts = []
    for m in range(MAPS):
        weights = jnp.where(lane // CH1 == m, weighted, 0.0)
        weights = weights + roll(weights, 64)
        high, low = halves(weights + roll(weights, 32))
        parts.append(dot(high[:, : 2 * CH1], s_ref[m]) + dot(low[:, :CH1], s_ref[m, :CH1]))

    def term(k, low, high):
        rows = {}
        for row in range(low, high):
            at = slice(128 * (row + UP2), 128 * (row + UP2 + 1))
            rows[row] = jnp.concatenate([part[CH0 * k : CH0 * (k + 1), at] for part in parts], axis=0)
        return rows

    turns = coarse_turns(here, CA)
    around = ring(128, 2)
    g0 = term(0, -1, CROWS + 1)
    g1 = term(1, 1 - UP2, CROWS + UP2 - 1)
    g2 = term(2, -UP2, CROWS + UP2)
    inner = coarse_laps(g2, 1 - UP2, CROWS + UP2 - 1, turns, around, z_ref)
    inner = {row: g1[row] + 2.0 * inner[row] for row in g1}
    outer = coarse_laps(inner, -1, CROWS + 1, turns, around, z_ref)
    for n, crow in enumerate(range(-1, CROWS + 1)):
        at = slice(CA * n, CA * (n + 1))
        side_by_side(z_ref, at, g0[crow] - g2[crow] + outer[crow])
    i, j = grid(256, 128)
    doubled = jnp.where(i % 128 == j // 2, 0.25, 0.0).astype(bf16)
    spread = dot(z_ref[0 : CA * (CROWS + 2)], doubled)
    for n in range(ROWS + 4):
        value = spread[CA * (n // 2) : CA * (n // 2 + 1)]
        high, low = halves(value * sig0_ref[n])
        at = pl.ds(n * 128, 128)
        d_ref[:CA, at] = high
        d_ref[CA : 2 * CA, at] = low
        d_ref[2 * CA :, at] = high
    both = dot_nt(terms_ref[...], d_ref[: 2 * CA, 2 * 128 : (2 + ROWS) * 128])
    lane = lanes(CI)
    row16 = lax.broadcasted_iota(jnp.int32, (CI, 128), 0)
    same = lane % CA // CH0 == row16 // BINS
    fine = []
    for k in range(ORDER):
        value = jnp.where(same, both[CI * k : CI * (k + 1)], 0.0)
        if k:
            low = both[CI * (2 + k) : CI * (3 + k)]
            value = value + jnp.where(same & (lane < CA), low, 0.0)
        for shift in (64, 32, 16):
            value = value + roll(value, shift)
        for shift in (8, 4):
            value = value + pltpu.roll(value, shift, 0)
        fine.append(value)
    value = jnp.where(row16 // BINS == 0, fine[0], jnp.where(row16 // BINS == 1, fine[1], fine[2]))
    for k in range(ORDER):
        value = jnp.where(lane // CH1 == k, coarse[k], value)
    for n in range(grads_ref.shape[0] // CI):
        grads_ref[CI * n : CI * (n + 1)] = value


def terms_kernel(d_ref, w0_ref, g_ref, ends_ref, ends_copy_ref):
    weights = weight_halves(w0_ref, 2 * CA)
    index = end_index(2 * CI)
    filled = []
    for n in range(0, ROWS + 4, 2):
        value = dot(weights, d_ref[:, n * 128 : (n + 2) * 128])
        for step in range(2):
            part = value[:, 128 * step : 128 * (step + 1)]
            g_ref[n + step] = part
            filled.append(pick(part[CI:], index))
    put_slots((ends_ref, ends_copy_ref), filled, len(filled))


def saliency_kernel(flips, g_ref, far_ref, near_ref, out_ref, *, pixels):
    here = Place(flips)
    turns = fine_turns(here, CI)
    left, right = both_strips(far_ref, near_ref, here.odd_tile)
    g0, g1, g2, s1, s2 = {}, {}, {}, {}, {}
    for row in range(-2, ROWS + 2):
        value = g_ref[row + 2]
        g0[row], g1[row], g2[row] = (value[CI * k : CI * (k + 1)] for k in range(3))
        strip = fine_strip(left, right, row + 2)
        s1[row], s2[row] = strip[:CI], strip[CI:]
    inner, inner_strip = {}, {}
    for row in range(-1, ROWS + 1):
        value, strip = fine_lap(g2, s2, row, turns, True)
        inner[row] = g1[row] + 2.0 * value
        inner_strip[row] = s1[row] + 2.0 * strip
    for row in range(ROWS):
        outer = fine_lap(inner, inner_strip, row, turns, False)
        out_ref[pl.ds(row, CI, stride=ROWS), :] = (g0[row] - g2[row] + outer) * pixels


def again_kernel(in_ref, out_ref):
    value = in_ref[0:CI]
    for n in range(1, in_ref.shape[0] // CI):
        value = value + in_ref[CI * n : CI * (n + 1)]
    for n in range(out_ref.shape[0] // CI):
        out_ref[CI * n : CI * (n + 1)] = value


def row_again_kernel(in_ref, out_ref):
    out_ref[...] = jnp.broadcast_to(jnp.sum(in_ref[...], axis=0, keepdims=True), out_ref.shape)


def last_kernel(in_ref, fine_ref, coarse_ref, tmp_ref):
    value = in_ref[0:CI]
    for n in range(1, in_ref.shape[0] // CI):
        value = value + in_ref[CI * n : CI * (n + 1)]
    for k in range(ORDER):
        coarse_ref[k] = roll(value, -CH1 * k)[:, :CH1]
    tmp_ref[...] = roll(value, -ORDER * CH1)
    for k in range(ORDER):
        fine_ref[k] = tmp_ref[BINS * k : BINS * (k + 1), :CH0]


def call(kernel, outs, *args, smem=0, scratch=()):
    in_specs = [
        pl.BlockSpec(memory_space=pltpu.SMEM if n < smem else pltpu.VMEM) for n in range(len(args))
    ]
    return pl.pallas_call(
        kernel,
        out_shape=outs,
        in_specs=in_specs,
        out_specs=jax.tree.map(lambda _: pl.BlockSpec(memory_space=pltpu.VMEM), outs),
        scratch_shapes=list(scratch),
        compiler_params=pltpu.CompilerParams(vmem_limit_bytes=32 * 2**20),
    )(*args)


def shape(*dims, dtype=f32):
    return jax.ShapeDtypeStruct(dims, dtype)


def exchange(axis, far_value, near_value):
    count = lax.axis_size(axis)
    far = [(n, (n + (1 if n % 2 else count - 1)) % count) for n in range(count)]
    near = [(n, n + (1 if n % 2 == 0 else -1)) for n in range(count)]
    return lax.ppermute(far_value, axis, far), lax.ppermute(near_value, axis, near)


def share(rows, axes):
    return lax.all_to_all(rows, axes, 0, 0, tiled=True)


def on_device(
    maps, params, labels, edge_flip,
    fine_weight, coarse_weight, feature_weight, param_weight, out_weight,
):
    faces, tiles = lax.axis_size(FACE), lax.axis_size(TILE)
    eye = jnp.eye(MAPS, dtype=f32)
    fine = jnp.einsum("kio,mn->monki", fine_weight, eye)
    fine = fine.transpose(0, 1, 3, 2, 4).reshape(CA, ORDER * CI)
    fine_forward = jnp.concatenate([fine, fine[:, CI:], fine], axis=1)
    fine_backward = jnp.concatenate([fine.T] * 3, axis=1)
    coarse = coarse_weight.reshape(ORDER * CH0, CH1)
    coarse_forward = jnp.concatenate([coarse.T] * 3, axis=1)
    coarse_backward = jnp.concatenate([coarse] * MAPS, axis=1)
    features4 = jnp.concatenate([feature_weight] * MAPS, axis=0)
    pad = [(0, 8 - MAPS), (0, 0)]
    shift = jnp.dot(jnp.pad(params, pad), param_weight, precision=exact)
    labels8 = jnp.broadcast_to(jnp.pad(labels.astype(f32)[:, None], pad), (8, 128))

    trade = shape(UP0, CI, COLS)
    own, far, near = call(
        rows_kernel, (shape(ROWS, CI, COLS), trade, trade), maps.reshape(CI * ROWS, COLS),
        scratch=[pltpu.VMEM((CI * ROWS, COLS), f32)],
    )
    far, near = exchange(FACE, far, near)
    trade = shape(groups(ROWS + 2 * UP0), CI, 128)
    far0, near0 = call(ends_kernel, (trade, trade), far, near, own)
    far0, near0 = exchange(TILE, far0, near0)
    crows = CROWS + 2 * UP1
    trade = shape(groups(crows), CA, 128)
    x1, sig0, terms0, far1, near1 = call(
        fine_kernel,
        (
            shape(crows, CA, 128),
            shape(ROWS + 4, CA, 128),
            shape(5 * CI, ROWS * 128, dtype=bf16),
            trade,
            trade,
        ),
        edge_flip, far, near, own, far0, near0, fine_forward,
        smem=1,
        scratch=[
            pltpu.VMEM((8 * CI, 2 * crows * 128), bf16),
            pltpu.VMEM(((ROWS + 2 * UP0) * CI, 256), bf16),
            pltpu.VMEM(((ROWS + 2 * UP0 - 2) * CI, 512), bf16),
            pltpu.VMEM((crows * CA, 256), bf16),
        ],
    )
    far1, near1 = exchange(TILE, far1, near1)
    feats, sig1, terms1 = call(
        coarse_kernel,
        (
            shape(lax.axis_size(FIRST), CB),
            shape(len(PAIRS), CB, 128),
            shape(MAPS, 3 * ORDER * CH0, len(PAIRS) * 128, dtype=bf16),
        ),
        edge_flip, x1, far1, near1, coarse_forward,
        smem=1,
        scratch=[pltpu.VMEM((crows * CA, 256), bf16)],
    )
    feats = share(feats, FIRST)
    feats = call(row_again_kernel, shape(lax.axis_size(SECOND), CB), feats)
    trade = shape(CB, 128)
    far2, near2, grams = call(
        gram_kernel, (trade, trade, shape(ORDER, CH0, 128)), sig1, terms1,
        scratch=[pltpu.VMEM((2 * CB, OWN * 128), bf16)],
    )
    feats = share(feats, SECOND)
    far2, near2 = exchange(TILE, far2, near2)
    pooled = CROWS * faces * CCOLS * tiles
    split1, head = call(
        split_kernel,
        (shape(MAPS, 2 * CH1, (CROWS + 2 * UP2) * 128, dtype=bf16), shape(3, 8, 128)),
        sig1, far2, near2, shift, labels8, out_weight[None],
    )
    logits, grads, dpre0 = call(
        lambda *refs: back_kernel(*refs, pooled=pooled),
        (
            shape(8, 128),
            shape(lax.axis_size(PLANE) * CI, 128),
            shape(3 * CA, (ROWS + 4) * 128, dtype=bf16),
        ),
        edge_flip, feats, head, features4, coarse_backward, split1, grams, sig0, terms0,
        smem=1,
        scratch=[pltpu.VMEM(((CROWS + 2 * UP2) * CA, 256), bf16)],
    )
    grads = share(grads, PLANE)
    trade = shape(groups(ROWS + 4), 2 * CI, 128)
    g, far3, near3 = call(
        terms_kernel, (shape(ROWS + 4, ORDER * CI, 128), trade, trade), dpre0, fine_backward
    )
    far3, near3 = exchange(TILE, far3, near3)
    grads = call(again_kernel, shape(lax.axis_size("z") * CI, 128), grads)
    grads = share(grads, "z")
    pixels = float(ROWS * faces * COLS * tiles)
    saliency = call(
        lambda *refs: saliency_kernel(*refs, pixels=pixels),
        shape(CI * ROWS, COLS), edge_flip, g, far3, near3,
        smem=1,
    )
    grad_f, grad_c = call(
        last_kernel, (shape(*fine_weight.shape), shape(*coarse_weight.shape)), grads,
        scratch=[pltpu.VMEM((CI, 128), f32)],
    )
    return (logits[:MAPS, 0], saliency.reshape(maps.shape), grad_f, grad_c)


def solution(mesh):
    faces, tiles = mesh.devices.shape
    sizes = (faces // 2, 2, tiles // 4, 2, 2)
    fine_mesh = jax.sharding.Mesh(mesh.devices.reshape(sizes), ("x", "y_lo", "z", "y_hi", "core"))
    tiled = P(None, None, FACE, TILE)
    return jax.shard_map(
        on_device,
        mesh=fine_mesh,
        in_specs=(tiled, P(), P(), P(), P(), P(), P(), P(), P()),
        out_specs=(P(), tiled, P(), P()),
        check_vma=False,
    )
```

```python
import jax
import jax.numpy as jnp
from jax import lax
from jax.experimental import pallas as pl
from jax.experimental.pallas import tpu as pltpu
from jax.sharding import PartitionSpec as P

exact = lax.Precision.HIGHEST
MAPS, BINS, CH0, CH1, ORDER = 4, 4, 16, 32, 3
ROWS, COLS = 16, 128
CROWS, CCOLS = ROWS // 2, COLS // 2
CI = MAPS * BINS
CA = MAPS * CH0
CB = MAPS * CH1
STRIP = 2
SLOT = 2 * STRIP
PER = 128 // SLOT
UP0 = 12
UP1 = 5
UP2 = 3
PAIRS = [(0, 4), (1, 5), (2, 6), (3, 7), (-3, 8), (-2, 9), (-1, 10)]
OWN = 4
WHERE = {row: (q, half) for q, pair in enumerate(PAIRS) for half, row in enumerate(pair)}
FACE, TILE = ("x", "y_lo"), ("z", "y_hi", "core")
PLANE = ("x", "y_lo", "y_hi", "core")
FIRST, SECOND = ("z", "core"), ("x", "y_lo", "y_hi")
bf16, f32 = jnp.bfloat16, jnp.float32


def lanes(count):
    return lax.broadcasted_iota(jnp.int32, (count, 128), 1)


def pick(value, index):
    return jnp.take_along_axis(value, index, axis=1, mode="promise_in_bounds")


def roll(value, shift):
    shift %= 128
    return value if shift == 0 else pltpu.roll(value, shift, 1)


def halves(value):
    high = value.astype(bf16)
    return high, (value - high.astype(f32)).astype(bf16)


def dot(a, b):
    return jnp.dot(a, b, preferred_element_type=f32)


def dot_halves(weights, high, low):
    both = dot(jnp.concatenate(halves(weights), axis=0), high)
    count = weights.shape[0]
    return both[:count] + both[count:] + dot(weights.astype(bf16), low)


def dot_nt(a, b):
    return lax.dot_general(a, b, (((1,), (1,)), ((), ())), preferred_element_type=f32)


class Place:
    def __init__(self, flips=None):
        self.face, self.tile = lax.axis_index(FACE), lax.axis_index(TILE)
        self.odd_face, self.odd_tile = self.face % 2, self.tile % 2
        self.flips = flips

    def flags(self, side):
        faces, tiles = self.flips.shape
        face = (self.face + side) % faces
        return [self.flips[face, (self.tile + step) % tiles] for step in (tiles - 1, 0, 1)]


def fine_turns(place, count):
    lane = lanes(count)
    turns = []
    for side in range(2):
        left, own, right = place.flags(side)
        block = jnp.where(own == 1, 127 - lane, lane)
        strip = jnp.where(
            lane < 64,
            jnp.where((lane < SLOT) & (right == 1), SLOT - 1 - lane, lane),
            jnp.where((lane >= 128 - SLOT) & (left == 1), 255 - SLOT - lane, lane),
        )
        turns.append((block, strip))
    return turns


def coarse_turns(place, count):
    lane = lanes(count)
    turns = []
    for side in range(2):
        left, own, right = place.flags(side)
        index = jnp.where((lane < 64) & (own == 1), 63 - lane, lane)
        index = jnp.where((lane >= 64) & (lane < 64 + SLOT) & (right == 1), 127 + SLOT - lane, index)
        index = jnp.where((lane >= 128 - SLOT) & (left == 1), 255 - SLOT - lane, index)
        turns.append(index)
    return turns


def vertical(rows, row, height, top, bottom):
    if row == 0:
        upper = pick(rows[-1], top)
    elif row == height:
        upper = pick(rows[height - 1], bottom)
    else:
        upper = rows[row - 1]
    if row == -1:
        lower = pick(rows[0], top)
    elif row == height - 1:
        lower = pick(rows[height], bottom)
    else:
        lower = rows[row + 1]
    return upper + lower


def fine_lap(block, strip, row, turns, with_strip):
    (top, top_strip), (bottom, bottom_strip) = turns
    lane = lanes(block[row].shape[0])
    first, last = lane == 0, lane == 127
    b_right, s_right = roll(block[row], 1), roll(strip[row], 1)
    b_left, s_left = roll(block[row], -1), roll(strip[row], -1)
    side = jnp.where(first, s_right, b_right) + jnp.where(last, s_left, b_left)
    out = -0.25 * (vertical(block, row, ROWS, top, bottom) + side)
    if not with_strip:
        return out
    side = jnp.where(first, b_right, s_right) + jnp.where(last, b_left, s_left)
    return out, -0.25 * (vertical(strip, row, ROWS, top_strip, bottom_strip) + side)


def coarse_laps(rows, low, high, turns, around, ref):
    count = rows[low].shape[0]
    for n, row in enumerate(range(low, high)):
        side_by_side(ref, slice(count * n, count * (n + 1)), rows[row])
    sides = dot(ref[0 : count * (high - low)], around)
    return {
        row: sides[count * n : count * (n + 1)] - 0.25 * vertical(rows, row, CROWS, *turns)
        for n, row in enumerate(range(low, high))
    }


def grid(rows, columns):
    return (lax.broadcasted_iota(jnp.int32, (rows, columns), axis) for axis in range(2))


def ring(length, copies=1):
    i, j = grid(length * copies, length)
    step = (i - j + length) % length
    return jnp.where((step == 1) | (step == length - 1), -0.25, 0.0).astype(bf16)


def side_by_side(ref, at, value):
    high, low = halves(value)
    width = value.shape[1]
    ref[at, :width], ref[at, width:] = high, low


def end_index(count, stride=1, width=COLS):
    j = lanes(count) % SLOT
    return jnp.where(j < STRIP, j, width - SLOT + j) * stride


def fine_strip(left, right, place):
    group, slot = place // PER, place % PER
    lane = lanes(left[group].shape[0])
    return jnp.where(
        lane < 64, roll(right[group], -SLOT * slot), roll(left[group], 128 - SLOT - SLOT * slot)
    )


def coarse_row(block, left, right, slot):
    lane = lanes(block.shape[0])
    strip = jnp.where(
        lane < 96, roll(right, 64 - SLOT * slot), roll(left, 128 - SLOT - SLOT * slot)
    )
    return jnp.where(lane < 64, block, strip)


def groups(count):
    return -(-count // PER)


def put_slots(out_refs, filled, count):
    lane = lanes(filled[0].shape[0])
    for group in range(groups(count)):
        value = filled[group * PER]
        for n in range(group * PER + 1, min(count, group * PER + PER)):
            value = jnp.where(lane // SLOT == n % PER, filled[n], value)
        for out_ref in out_refs:
            out_ref[group] = value


def before(far, near, odd):
    return jnp.where(odd == 1, near, far)


def after(far, near, odd):
    return jnp.where(odd == 1, far, near)


def fine_rows(far_ref, near_ref, own_ref, odd):
    rows = {}
    for row in range(-UP0, ROWS + UP0):
        if row < 0:
            rows[row] = before(far_ref[UP0 + row], near_ref[UP0 + row], odd)
        elif row < ROWS:
            rows[row] = own_ref[row]
        else:
            rows[row] = after(far_ref[row - ROWS], near_ref[row - ROWS], odd)
    return rows


def rows_kernel(maps_ref, own_ref, far_ref, near_ref, t_ref):
    here = Place()
    t_ref[...] = maps_ref[...].astype(f32)
    rows = [t_ref[pl.ds(row, CI, stride=ROWS), :] for row in range(ROWS)]
    for row in range(ROWS):
        own_ref[row] = rows[row]
    for row in range(UP0):
        first, last = rows[row], rows[ROWS - UP0 + row]
        far_ref[row] = before(first, last, here.odd_face)
        near_ref[row] = after(first, last, here.odd_face)


def both_strips(far_ref, near_ref, odd):
    count = far_ref.shape[0]
    left = [before(far_ref[n], near_ref[n], odd) for n in range(count)]
    return left, [after(far_ref[n], near_ref[n], odd) for n in range(count)]


def ends_kernel(far_ref, near_ref, own_ref, *out_refs):
    index = end_index(CI)
    rows = fine_rows(far_ref, near_ref, own_ref, Place().odd_face)
    put_slots(out_refs, [pick(rows[row], index) for row in sorted(rows)], len(rows))


def fine_kernel(
    flips, far_ref, near_ref, own_ref, far0_ref, near0_ref, w_ref,
    x1_ref, sig_ref, terms_ref, ends_ref, ends_copy_ref, t_ref, x_ref, y_ref, a_ref,
):
    here = Place(flips)
    turns = fine_turns(here, CI)
    block = fine_rows(far_ref, near_ref, own_ref, here.odd_face)
    left, right = both_strips(far0_ref, near0_ref, here.odd_tile)
    strip = {row: fine_strip(left, right, row + UP0) for row in block}
    around = ring(256)
    for n, row in enumerate(sorted(block)):
        x_ref[CI * n : CI * (n + 1), :128] = block[row].astype(bf16)
        x_ref[CI * n : CI * (n + 1), 128:] = strip[row].astype(bf16)
    sides = dot(x_ref[...], around)
    (top, top_strip), (bottom, bottom_strip) = turns
    first, split = {}, {}
    for n, row in enumerate(range(1 - UP0, ROWS + UP0 - 1)):
        side = sides[CI * (n + 1) : CI * (n + 2)]
        first[row] = side[:, :128] - 0.25 * vertical(block, row, ROWS, top, bottom)
        other = side[:, 128:] - 0.25 * vertical(strip, row, ROWS, top_strip, bottom_strip)
        split[row] = halves(first[row])
        at = slice(CI * n, CI * (n + 1))
        y_ref[at, :128], y_ref[at, 256:384] = split[row]
        y_ref[at, 128:256], y_ref[at, 384:] = halves(other)
    around = around[:, :128]
    sides = dot(y_ref[:, :256], around) + dot(y_ref[:, 256:], around)
    low, high = -2 * UP1, ROWS + 2 * UP1
    for n, row in enumerate(range(low, high)):
        lap = sides[CI * (n + 1) : CI * (n + 2)] - 0.25 * vertical(first, row, ROWS, top, bottom)
        at = pl.ds(n * 128, 128)
        zero = block[row].astype(bf16)
        one, one_low = split[row]
        two, two_low = halves(2.0 * lap - block[row])
        for k, part in enumerate((zero, one, two, jnp.zeros_like(zero), one_low, two_low)):
            t_ref[CI * k : CI * (k + 1), at] = part
    own = pl.ds(-low * 128, ROWS * 128)
    terms_ref[: 3 * CI] = t_ref[: 3 * CI, own]
    terms_ref[3 * CI :] = t_ref[4 * CI :, own]
    weights = w_ref[...]
    for crow in range(-UP1, CROWS + UP1):
        place = crow + UP1
        at = slice(256 * place, 256 * (place + 1))
        pre = dot_halves(weights, t_ref[: 3 * CI, at], t_ref[3 * CI :, at])
        decay = jnp.exp(-jnp.abs(pre))
        act = jnp.maximum(pre, 0.0) + jnp.log(1.0 + decay)
        if -1 <= crow <= CROWS:
            inverse = 1.0 / (1.0 + decay)
            sig = jnp.where(pre >= 0, inverse, decay * inverse)
            sig_ref[2 * (crow + 1)] = sig[:, :128]
            sig_ref[2 * (crow + 1) + 1] = sig[:, 128:]
        side_by_side(a_ref, slice(CA * place, CA * (place + 1)), act[:, :128] + act[:, 128:])
    i, j = grid(256, 256)
    slot = j % SLOT
    end = jnp.where(slot < STRIP, slot, CCOLS - SLOT + slot)
    column = jnp.where(j < 128, j, end)
    means = dot(a_ref[...], jnp.where(i % 128 // 2 == column, 0.25, 0.0).astype(bf16))
    filled = []
    for place in range(CROWS + 2 * UP1):
        value = means[CA * place : CA * (place + 1)]
        x1_ref[place] = value[:, :128]
        filled.append(value[:, 128:])
    put_slots((ends_ref, ends_copy_ref), filled, len(filled))


def coarse_kernel(
    flips, x1_ref, far_ref, near_ref, w_ref, feat_ref, sig_ref, t_ref, z_ref
):
    here = Place(flips)
    turns = coarse_turns(here, CA)
    lane = lanes(CA)
    left, right = both_strips(far_ref, near_ref, here.odd_tile)
    rows = {}
    for row in range(-UP1, CROWS + UP1):
        place = row + UP1
        rows[row] = coarse_row(
            x1_ref[place], left[place // PER], right[place // PER], place % PER
        )
    around = ring(128, 2)
    first = coarse_laps(rows, 1 - UP1, CROWS + UP1 - 1, turns, around, z_ref)
    second = coarse_laps(first, -UP2, CROWS + UP2, turns, around, z_ref)
    second = {row: 2.0 * second[row] - rows[row] for row in second}
    for q, (a, b) in enumerate(PAIRS):
        at = pl.ds(q * 128, 128)
        for k, term in enumerate((rows, first, second)):
            packed = jnp.where(lane < 64, term[a], roll(term[b], 64))
            high, low = halves(packed)
            for m in range(MAPS):
                chans = slice(CH0 * m, CH0 * (m + 1))
                t_ref[m, CH0 * k : CH0 * (k + 1), at] = high[chans]
                t_ref[m, CH0 * (3 + k) : CH0 * (4 + k), at] = low[chans]
    weights = w_ref[...].T
    own = OWN * 128
    sums = []
    for m in range(MAPS):
        pre = dot_halves(weights, t_ref[m, : ORDER * CH0], t_ref[m, ORDER * CH0 :])
        decay = jnp.exp(-jnp.abs(pre))
        inverse = 1.0 / (1.0 + decay)
        sig = jnp.where(pre >= 0, inverse, decay * inverse)
        act = jnp.maximum(pre[:, :own], 0.0) + jnp.log(1.0 + decay[:, :own])
        sums.append(sum(act[:, 128 * q : 128 * (q + 1)] for q in range(OWN)))
        for q in range(len(PAIRS)):
            sig_ref[q, CH1 * m : CH1 * (m + 1)] = sig[:, 128 * q : 128 * (q + 1)]
    total = jnp.sum(jnp.concatenate(sums, axis=0).T, axis=0, keepdims=True)
    feat_ref[...] = jnp.broadcast_to(total, feat_ref.shape)


def gram_kernel(sig_ref, t_ref, ends_ref, ends_copy_ref, gram_ref, s_ref):
    j = lanes(CB) % SLOT
    column = jnp.where(j < STRIP, j, CCOLS - SLOT + j)
    index = jnp.where(lanes(CB) // SLOT % 2 == 0, column, 64 + column)
    ends = jnp.zeros((CB, 128), f32)
    for q in range(len(PAIRS)):
        value = sig_ref[q]
        ends = jnp.where(lanes(CB) // (2 * SLOT) == q, pick(value, index), ends)
        if q < OWN:
            s_ref[:CB, 128 * q : 128 * (q + 1)], s_ref[CB:, 128 * q : 128 * (q + 1)] = halves(value)
    ends_ref[...] = ends
    ends_copy_ref[...] = ends
    grams = [jnp.zeros((CH0, 128), f32) for _ in range(ORDER)]
    for m in range(MAPS):
        both = dot_nt(t_ref[m, :, : OWN * 128], s_ref[...])
        for k in range(ORDER):
            high = both[CH0 * k : CH0 * (k + 1)]
            low = both[CH0 * (3 + k) : CH0 * (4 + k)]
            value = high[:, :CB] + high[:, CB:] + low[:, :CB]
            grams[k] = jnp.where(lanes(CH0) // CH1 == m, value, grams[k])
    for k in range(ORDER):
        gram_ref[k] = grams[k]


def split_kernel(
    sig1_ref, far_ref, near_ref, shift_ref, labels_ref, out_ref, s_ref, head_ref
):
    here = Place()
    left = before(far_ref[...], near_ref[...], here.odd_tile)
    right = after(far_ref[...], near_ref[...], here.odd_tile)
    for n, row in enumerate(range(-UP2, CROWS + UP2)):
        q, half = WHERE[row]
        value = coarse_row(roll(sig1_ref[q], 64 * half), left, right, 2 * q + half)
        high, low = halves(value)
        at = pl.ds(n * 128, 128)
        for m in range(MAPS):
            chans = slice(CH1 * m, CH1 * (m + 1))
            s_ref[m, :CH1, at] = high[chans]
            s_ref[m, CH1:, at] = low[chans]
    head_ref[0] = shift_ref[...]
    head_ref[1] = labels_ref[...]
    head_ref[2] = jnp.broadcast_to(out_ref[...], (8, 128))


def back_kernel(
    flips, feat_ref, head_ref, fw_ref, w1_ref, s_ref, gram_ref, sig0_ref, terms_ref,
    logits_ref, grads_ref, d_ref, z_ref,
    *, pooled,
):
    here = Place(flips)
    features = jnp.sum(feat_ref[...], axis=0, keepdims=True) * (1.0 / pooled)
    row8 = lax.broadcasted_iota(jnp.int32, (8, 128), 0)
    apart = jnp.where(lanes(8) // CH1 == row8, jnp.broadcast_to(features, (8, 128)), 0.0)
    fw = jnp.concatenate([fw_ref[...]] * MAPS, axis=0)
    shift, labels, out = head_ref[0], head_ref[1], head_ref[2]
    hidden = jnp.tanh(
        jnp.dot(apart, fw, precision=exact, preferred_element_type=f32) + shift
    )
    logits = jnp.sum(hidden * out, axis=1, keepdims=True)
    logits_ref[...] = jnp.broadcast_to(logits, (8, 128))
    decay = jnp.exp(-jnp.abs(logits))
    dlogit = jnp.where(logits >= 0, 1.0, decay) / (1.0 + decay) - labels
    dhidden = dlogit * out * (1.0 - hidden * hidden)
    dhidden = jnp.concatenate(
        [jnp.broadcast_to(dhidden[m : m + 1], (CH1, 128)) for m in range(MAPS)], axis=0
    )
    dcol = jnp.sum(fw * dhidden, axis=1, keepdims=True) * (1.0 / pooled)
    dfull = jnp.broadcast_to(dcol, (CB, 128))
    drow = jnp.broadcast_to(dfull.T[:1], (CH0, 128))
    coarse = []
    for k in range(ORDER):
        value = gram_ref[k] * drow
        value = value + roll(value, 64)
        coarse.append(value + roll(value, 32))
    weighted = w1_ref[...] * jnp.broadcast_to(drow[:1], w1_ref.shape)
    lane = lanes(w1_ref.shape[0])
    parts = []
    for m in range(MAPS):
        weights = jnp.where(lane // CH1 == m, weighted, 0.0)
        weights = weights + roll(weights, 64)
        high, low = halves(weights + roll(weights, 32))
        parts.append(dot(high[:, : 2 * CH1], s_ref[m]) + dot(low[:, :CH1], s_ref[m, :CH1]))

    def term(k, low, high):
        rows = {}
        for row in range(low, high):
            at = slice(128 * (row + UP2), 128 * (row + UP2 + 1))
            rows[row] = jnp.concatenate([part[CH0 * k : CH0 * (k + 1), at] for part in parts], axis=0)
        return rows

    turns = coarse_turns(here, CA)
    around = ring(128, 2)
    g0 = term(0, -1, CROWS + 1)
    g1 = term(1, 1 - UP2, CROWS + UP2 - 1)
    g2 = term(2, -UP2, CROWS + UP2)
    inner = coarse_laps(g2, 1 - UP2, CROWS + UP2 - 1, turns, around, z_ref)
    inner = {row: g1[row] + 2.0 * inner[row] for row in g1}
    outer = coarse_laps(inner, -1, CROWS + 1, turns, around, z_ref)
    for n, crow in enumerate(range(-1, CROWS + 1)):
        at = slice(CA * n, CA * (n + 1))
        side_by_side(z_ref, at, g0[crow] - g2[crow] + outer[crow])
    i, j = grid(256, 128)
    doubled = jnp.where(i % 128 == j // 2, 0.25, 0.0).astype(bf16)
    spread = dot(z_ref[0 : CA * (CROWS + 2)], doubled)
    for n in range(ROWS + 4):
        value = spread[CA * (n // 2) : CA * (n // 2 + 1)]
        high, low = halves(value * sig0_ref[n])
        at = pl.ds(n * 128, 128)
        d_ref[:CA, at] = high
        d_ref[CA:, at] = low
    both = dot_nt(terms_ref[...], d_ref[:, 2 * 128 : (2 + ROWS) * 128])
    lane = lanes(CI)
    row16 = lax.broadcasted_iota(jnp.int32, (CI, 128), 0)
    same = lane % CA // CH0 == row16 // BINS
    fine = []
    for k in range(ORDER):
        value = jnp.where(same, both[CI * k : CI * (k + 1)], 0.0)
        if k:
            low = both[CI * (2 + k) : CI * (3 + k)]
            value = value + jnp.where(same & (lane < CA), low, 0.0)
        for shift in (64, 32, 16):
            value = value + roll(value, shift)
        for shift in (8, 4):
            value = value + pltpu.roll(value, shift, 0)
        fine.append(value)
    value = jnp.where(row16 // BINS == 0, fine[0], jnp.where(row16 // BINS == 1, fine[1], fine[2]))
    for k in range(ORDER):
        value = jnp.where(lane // CH1 == k, coarse[k], value)
    for n in range(grads_ref.shape[0] // CI):
        grads_ref[CI * n : CI * (n + 1)] = value


def terms_kernel(d_ref, w0_ref, g_ref, ends_ref, ends_copy_ref):
    weights = w0_ref[...]
    index = end_index(2 * CI)
    filled = []
    for n in range(0, ROWS + 4, 2):
        at = slice(128 * n, 128 * (n + 2))
        value = dot_halves(weights, d_ref[:CA, at], d_ref[CA:, at])
        for step in range(2):
            part = value[:, 128 * step : 128 * (step + 1)]
            g_ref[n + step] = part
            filled.append(pick(part[CI:], index))
    put_slots((ends_ref, ends_copy_ref), filled, len(filled))


def saliency_kernel(flips, g_ref, far_ref, near_ref, out_ref, *, pixels):
    here = Place(flips)
    turns = fine_turns(here, CI)
    left, right = both_strips(far_ref, near_ref, here.odd_tile)
    g0, g1, g2, s1, s2 = {}, {}, {}, {}, {}
    for row in range(-2, ROWS + 2):
        value = g_ref[row + 2]
        g0[row], g1[row], g2[row] = (value[CI * k : CI * (k + 1)] for k in range(3))
        strip = fine_strip(left, right, row + 2)
        s1[row], s2[row] = strip[:CI], strip[CI:]
    inner, inner_strip = {}, {}
    for row in range(-1, ROWS + 1):
        value, strip = fine_lap(g2, s2, row, turns, True)
        inner[row] = g1[row] + 2.0 * value
        inner_strip[row] = s1[row] + 2.0 * strip
    for row in range(ROWS):
        outer = fine_lap(inner, inner_strip, row, turns, False)
        out_ref[pl.ds(row, CI, stride=ROWS), :] = (g0[row] - g2[row] + outer) * pixels


def again_kernel(in_ref, out_ref):
    value = in_ref[0:CI]
    for n in range(1, in_ref.shape[0] // CI):
        value = value + in_ref[CI * n : CI * (n + 1)]
    for n in range(out_ref.shape[0] // CI):
        out_ref[CI * n : CI * (n + 1)] = value


def row_again_kernel(in_ref, out_ref):
    out_ref[...] = jnp.broadcast_to(jnp.sum(in_ref[...], axis=0, keepdims=True), out_ref.shape)


def last_kernel(in_ref, fine_ref, coarse_ref, tmp_ref):
    value = in_ref[0:CI]
    for n in range(1, in_ref.shape[0] // CI):
        value = value + in_ref[CI * n : CI * (n + 1)]
    for k in range(ORDER):
        coarse_ref[k] = roll(value, -CH1 * k)[:, :CH1]
    tmp_ref[...] = roll(value, -ORDER * CH1)
    for k in range(ORDER):
        fine_ref[k] = tmp_ref[BINS * k : BINS * (k + 1), :CH0]


def call(kernel, outs, *args, smem=0, scratch=()):
    in_specs = [
        pl.BlockSpec(memory_space=pltpu.SMEM if n < smem else pltpu.VMEM) for n in range(len(args))
    ]
    return pl.pallas_call(
        kernel,
        out_shape=outs,
        in_specs=in_specs,
        out_specs=jax.tree.map(lambda _: pl.BlockSpec(memory_space=pltpu.VMEM), outs),
        scratch_shapes=list(scratch),
        compiler_params=pltpu.CompilerParams(vmem_limit_bytes=32 * 2**20),
    )(*args)


def shape(*dims, dtype=f32):
    return jax.ShapeDtypeStruct(dims, dtype)


def exchange(axis, far_value, near_value):
    count = lax.axis_size(axis)
    far = [(n, (n + (1 if n % 2 else count - 1)) % count) for n in range(count)]
    near = [(n, n + (1 if n % 2 == 0 else -1)) for n in range(count)]
    return lax.ppermute(far_value, axis, far), lax.ppermute(near_value, axis, near)


def share(rows, axes):
    return lax.all_to_all(rows, axes, 0, 0, tiled=True)


def on_device(
    maps, params, labels, edge_flip,
    fine_weight, coarse_weight, feature_weight, param_weight, out_weight,
):
    faces, tiles = lax.axis_size(FACE), lax.axis_size(TILE)
    eye = jnp.eye(MAPS, dtype=f32)
    fine = jnp.einsum("kio,mn->monki", fine_weight, eye)
    fine = fine.transpose(0, 1, 3, 2, 4).reshape(CA, ORDER * CI)
    coarse = coarse_weight.reshape(ORDER * CH0, CH1)
    coarse_backward = jnp.concatenate([coarse] * MAPS, axis=1)
    pad = [(0, 8 - MAPS), (0, 0)]
    shift = jnp.dot(jnp.pad(params, pad), param_weight, precision=exact)
    labels8 = jnp.broadcast_to(jnp.pad(labels.astype(f32)[:, None], pad), (8, 128))

    trade = shape(UP0, CI, COLS)
    own, far, near = call(
        rows_kernel, (shape(ROWS, CI, COLS), trade, trade), maps.reshape(CI * ROWS, COLS),
        scratch=[pltpu.VMEM((CI * ROWS, COLS), f32)],
    )
    far, near = exchange(FACE, far, near)
    trade = shape(groups(ROWS + 2 * UP0), CI, 128)
    far0, near0 = call(ends_kernel, (trade, trade), far, near, own)
    far0, near0 = exchange(TILE, far0, near0)
    crows = CROWS + 2 * UP1
    trade = shape(groups(crows), CA, 128)
    x1, sig0, terms0, far1, near1 = call(
        fine_kernel,
        (
            shape(crows, CA, 128),
            shape(ROWS + 4, CA, 128),
            shape(5 * CI, ROWS * 128, dtype=bf16),
            trade,
            trade,
        ),
        edge_flip, far, near, own, far0, near0, fine,
        smem=1,
        scratch=[
            pltpu.VMEM((6 * CI, 2 * crows * 128), bf16),
            pltpu.VMEM(((ROWS + 2 * UP0) * CI, 256), bf16),
            pltpu.VMEM(((ROWS + 2 * UP0 - 2) * CI, 512), bf16),
            pltpu.VMEM((crows * CA, 256), bf16),
        ],
    )
    far1, near1 = exchange(TILE, far1, near1)
    feats, sig1, terms1 = call(
        coarse_kernel,
        (
            shape(lax.axis_size(FIRST), CB),
            shape(len(PAIRS), CB, 128),
            shape(MAPS, 2 * ORDER * CH0, len(PAIRS) * 128, dtype=bf16),
        ),
        edge_flip, x1, far1, near1, coarse,
        smem=1,
        scratch=[pltpu.VMEM((crows * CA, 256), bf16)],
    )
    feats = share(feats, FIRST)
    feats = call(row_again_kernel, shape(lax.axis_size(SECOND), CB), feats)
    trade = shape(CB, 128)
    far2, near2, grams = call(
        gram_kernel, (trade, trade, shape(ORDER, CH0, 128)), sig1, terms1,
        scratch=[pltpu.VMEM((2 * CB, OWN * 128), bf16)],
    )
    feats = share(feats, SECOND)
    far2, near2 = exchange(TILE, far2, near2)
    pooled = CROWS * faces * CCOLS * tiles
    split1, head = call(
        split_kernel,
        (shape(MAPS, 2 * CH1, (CROWS + 2 * UP2) * 128, dtype=bf16), shape(3, 8, 128)),
        sig1, far2, near2, shift, labels8, out_weight[None],
    )
    logits, grads, dpre0 = call(
        lambda *refs: back_kernel(*refs, pooled=pooled),
        (
            shape(8, 128),
            shape(lax.axis_size(PLANE) * CI, 128),
            shape(2 * CA, (ROWS + 4) * 128, dtype=bf16),
        ),
        edge_flip, feats, head, feature_weight, coarse_backward, split1, grams, sig0, terms0,
        smem=1,
        scratch=[pltpu.VMEM(((CROWS + 2 * UP2) * CA, 256), bf16)],
    )
    grads = share(grads, PLANE)
    trade = shape(groups(ROWS + 4), 2 * CI, 128)
    g, far3, near3 = call(
        terms_kernel, (shape(ROWS + 4, ORDER * CI, 128), trade, trade), dpre0, fine.T
    )
    far3, near3 = exchange(TILE, far3, near3)
    grads = call(again_kernel, shape(lax.axis_size("z") * CI, 128), grads)
    grads = share(grads, "z")
    pixels = float(ROWS * faces * COLS * tiles)
    saliency = call(
        lambda *refs: saliency_kernel(*refs, pixels=pixels),
        shape(CI * ROWS, COLS), edge_flip, g, far3, near3,
        smem=1,
    )
    grad_f, grad_c = call(
        last_kernel, (shape(*fine_weight.shape), shape(*coarse_weight.shape)), grads,
        scratch=[pltpu.VMEM((CI, 128), f32)],
    )
    return (logits[:MAPS, 0], saliency.reshape(maps.shape), grad_f, grad_c)


def solution(mesh):
    faces, tiles = mesh.devices.shape
    sizes = (faces // 2, 2, tiles // 4, 2, 2)
    fine_mesh = jax.sharding.Mesh(mesh.devices.reshape(sizes), ("x", "y_lo", "z", "y_hi", "core"))
    tiled = P(None, None, FACE, TILE)
    return jax.shard_map(
        on_device,
        mesh=fine_mesh,
        in_specs=(tiled, P(), P(), P(), P(), P(), P(), P(), P()),
        out_specs=(P(), tiled, P(), P()),
        check_vma=False,
    )
```

```python
import jax
import jax.numpy as jnp
from jax import lax
from jax.experimental import pallas as pl
from jax.experimental.pallas import tpu as pltpu
from jax.sharding import PartitionSpec as P

exact = lax.Precision.HIGHEST
MAPS, BINS, CH0, CH1, ORDER = 4, 4, 16, 32, 3
ROWS, COLS = 16, 128
CROWS, CCOLS = ROWS // 2, COLS // 2
CI = MAPS * BINS
CA = MAPS * CH0
CB = MAPS * CH1
STRIP = 2
SLOT = 2 * STRIP
PER = 128 // SLOT
UP0 = 12
UP1 = 5
UP2 = 3
PAIRS = [(0, 4), (1, 5), (2, 6), (3, 7), (-3, 8), (-2, 9), (-1, 10)]
OWN = 4
WHERE = {row: (q, half) for q, pair in enumerate(PAIRS) for half, row in enumerate(pair)}
FACE, TILE = ("x", "y_lo"), ("z", "y_hi", "core")
PLANE = ("x", "y_lo", "y_hi", "core")
FIRST, SECOND = ("z", "core"), ("x", "y_lo", "y_hi")
bf16, f32 = jnp.bfloat16, jnp.float32


def lanes(count):
    return lax.broadcasted_iota(jnp.int32, (count, 128), 1)


def pick(value, index):
    return jnp.take_along_axis(value, index, axis=1, mode="promise_in_bounds")


def roll(value, shift):
    shift %= 128
    return value if shift == 0 else pltpu.roll(value, shift, 1)


def halves(value):
    high = value.astype(bf16)
    return high, (value - high.astype(f32)).astype(bf16)


def dot(a, b):
    return jnp.dot(a, b, preferred_element_type=f32)


def dot_halves(weights, high, low):
    both = dot(jnp.concatenate(halves(weights), axis=0), high)
    count = weights.shape[0]
    return both[:count] + both[count:] + dot(weights.astype(bf16), low)


def dot_nt(a, b):
    return lax.dot_general(a, b, (((1,), (1,)), ((), ())), preferred_element_type=f32)


class Place:
    def __init__(self, flips=None):
        self.face, self.tile = lax.axis_index(FACE), lax.axis_index(TILE)
        self.odd_face, self.odd_tile = self.face % 2, self.tile % 2
        self.flips = flips

    def flags(self, side):
        faces, tiles = self.flips.shape
        face = (self.face + side) % faces
        return [self.flips[face, (self.tile + step) % tiles] for step in (tiles - 1, 0, 1)]


def fine_turns(place, count):
    lane = lanes(count)
    turns = []
    for side in range(2):
        left, own, right = place.flags(side)
        block = jnp.where(own == 1, 127 - lane, lane)
        strip = jnp.where(
            lane < 64,
            jnp.where((lane < SLOT) & (right == 1), SLOT - 1 - lane, lane),
            jnp.where((lane >= 128 - SLOT) & (left == 1), 255 - SLOT - lane, lane),
        )
        turns.append((block, strip))
    return turns


def coarse_turns(place, count):
    lane = lanes(count)
    turns = []
    for side in range(2):
        left, own, right = place.flags(side)
        index = jnp.where((lane < 64) & (own == 1), 63 - lane, lane)
        index = jnp.where((lane >= 64) & (lane < 64 + SLOT) & (right == 1), 127 + SLOT - lane, index)
        index = jnp.where((lane >= 128 - SLOT) & (left == 1), 255 - SLOT - lane, index)
        turns.append(index)
    return turns


def vertical(rows, row, height, top, bottom):
    if row == 0:
        upper = pick(rows[-1], top)
    elif row == height:
        upper = pick(rows[height - 1], bottom)
    else:
        upper = rows[row - 1]
    if row == -1:
        lower = pick(rows[0], top)
    elif row == height - 1:
        lower = pick(rows[height], bottom)
    else:
        lower = rows[row + 1]
    return upper + lower


def fine_lap(block, strip, row, turns, with_strip):
    (top, top_strip), (bottom, bottom_strip) = turns
    lane = lanes(block[row].shape[0])
    first, last = lane == 0, lane == 127
    b_right, s_right = roll(block[row], 1), roll(strip[row], 1)
    b_left, s_left = roll(block[row], -1), roll(strip[row], -1)
    side = jnp.where(first, s_right, b_right) + jnp.where(last, s_left, b_left)
    out = -0.25 * (vertical(block, row, ROWS, top, bottom) + side)
    if not with_strip:
        return out
    side = jnp.where(first, b_right, s_right) + jnp.where(last, b_left, s_left)
    return out, -0.25 * (vertical(strip, row, ROWS, top_strip, bottom_strip) + side)


def coarse_laps(rows, low, high, turns, around, ref):
    count = rows[low].shape[0]
    for n, row in enumerate(range(low, high)):
        side_by_side(ref, slice(count * n, count * (n + 1)), rows[row])
    sides = dot(ref[0 : count * (high - low)], around)
    return {
        row: sides[count * n : count * (n + 1)] - 0.25 * vertical(rows, row, CROWS, *turns)
        for n, row in enumerate(range(low, high))
    }


def grid(rows, columns):
    return (lax.broadcasted_iota(jnp.int32, (rows, columns), axis) for axis in range(2))


def ring(length, copies=1):
    i, j = grid(length * copies, length)
    step = (i - j + length) % length
    return jnp.where((step == 1) | (step == length - 1), -0.25, 0.0).astype(bf16)


def side_by_side(ref, at, value):
    high, low = halves(value)
    width = value.shape[1]
    ref[at, :width], ref[at, width:] = high, low


def end_index(count, stride=1, width=COLS):
    j = lanes(count) % SLOT
    return jnp.where(j < STRIP, j, width - SLOT + j) * stride


def fine_strip(left, right, place):
    group, slot = place // PER, place % PER
    lane = lanes(left[group].shape[0])
    return jnp.where(
        lane < 64, roll(right[group], -SLOT * slot), roll(left[group], 128 - SLOT - SLOT * slot)
    )


def coarse_row(block, left, right, slot):
    lane = lanes(block.shape[0])
    strip = jnp.where(
        lane < 96, roll(right, 64 - SLOT * slot), roll(left, 128 - SLOT - SLOT * slot)
    )
    return jnp.where(lane < 64, block, strip)


def groups(count):
    return -(-count // PER)


def put_slots(out_refs, filled, count):
    lane = lanes(filled[0].shape[0])
    for group in range(groups(count)):
        value = filled[group * PER]
        for n in range(group * PER + 1, min(count, group * PER + PER)):
            value = jnp.where(lane // SLOT == n % PER, filled[n], value)
        for out_ref in out_refs:
            out_ref[group] = value


def before(far, near, odd):
    return jnp.where(odd == 1, near, far)


def after(far, near, odd):
    return jnp.where(odd == 1, far, near)


def fine_rows(far_ref, near_ref, own_ref, odd):
    rows = {}
    for row in range(-UP0, ROWS + UP0):
        if row < 0:
            rows[row] = before(far_ref[UP0 + row], near_ref[UP0 + row], odd)
        elif row < ROWS:
            rows[row] = own_ref[row]
        else:
            rows[row] = after(far_ref[row - ROWS], near_ref[row - ROWS], odd)
    return rows


def rows_kernel(maps_ref, own_ref, far_ref, near_ref, t_ref):
    here = Place()
    t_ref[...] = maps_ref[...].astype(f32)
    rows = [t_ref[pl.ds(row, CI, stride=ROWS), :] for row in range(ROWS)]
    for row in range(ROWS):
        own_ref[row] = rows[row]
    for row in range(UP0):
        first, last = rows[row], rows[ROWS - UP0 + row]
        far_ref[row] = before(first, last, here.odd_face)
        near_ref[row] = after(first, last, here.odd_face)


def both_strips(far_ref, near_ref, odd):
    count = far_ref.shape[0]
    left = [before(far_ref[n], near_ref[n], odd) for n in range(count)]
    return left, [after(far_ref[n], near_ref[n], odd) for n in range(count)]


def ends_kernel(far_ref, near_ref, own_ref, *out_refs):
    index = end_index(CI)
    rows = fine_rows(far_ref, near_ref, own_ref, Place().odd_face)
    put_slots(out_refs, [pick(rows[row], index) for row in sorted(rows)], len(rows))


def fine_kernel(
    flips, far_ref, near_ref, own_ref, far0_ref, near0_ref, w_ref,
    x1_ref, sig_ref, terms_ref, ends_ref, ends_copy_ref, t_ref, x_ref, y_ref, a_ref,
):
    here = Place(flips)
    turns = fine_turns(here, CI)
    block = fine_rows(far_ref, near_ref, own_ref, here.odd_face)
    left, right = both_strips(far0_ref, near0_ref, here.odd_tile)
    strip = {row: fine_strip(left, right, row + UP0) for row in block}
    around = ring(256)
    for n, row in enumerate(sorted(block)):
        x_ref[CI * n : CI * (n + 1), :128] = block[row].astype(bf16)
        x_ref[CI * n : CI * (n + 1), 128:] = strip[row].astype(bf16)
    sides = dot(x_ref[...], around)
    (top, top_strip), (bottom, bottom_strip) = turns
    first, split = {}, {}
    for n, row in enumerate(range(1 - UP0, ROWS + UP0 - 1)):
        side = sides[CI * (n + 1) : CI * (n + 2)]
        first[row] = side[:, :128] - 0.25 * vertical(block, row, ROWS, top, bottom)
        other = side[:, 128:] - 0.25 * vertical(strip, row, ROWS, top_strip, bottom_strip)
        split[row] = halves(first[row])
        at = slice(CI * n, CI * (n + 1))
        y_ref[at, :128], y_ref[at, 256:384] = split[row]
        y_ref[at, 128:256], y_ref[at, 384:] = halves(other)
    around = around[:, :128]
    sides = dot(y_ref[:, :256], around) + dot(y_ref[:, 256:], around)
    low, high = -2 * UP1, ROWS + 2 * UP1
    for n, row in enumerate(range(low, high)):
        lap = sides[CI * (n + 1) : CI * (n + 2)] - 0.25 * vertical(first, row, ROWS, top, bottom)
        at = pl.ds(n * 128, 128)
        zero = block[row].astype(bf16)
        one, one_low = split[row]
        two, two_low = halves(2.0 * lap - block[row])
        for k, part in enumerate((zero, one, two, jnp.zeros_like(zero), one_low, two_low)):
            t_ref[CI * k : CI * (k + 1), at] = part
    own = pl.ds(-low * 128, ROWS * 128)
    terms_ref[: 3 * CI] = t_ref[: 3 * CI, own]
    terms_ref[3 * CI :] = t_ref[4 * CI :, own]
    weights = w_ref[...]
    for crow in range(-UP1, CROWS + UP1):
        place = crow + UP1
        at = slice(256 * place, 256 * (place + 1))
        pre = dot_halves(weights, t_ref[: 3 * CI, at], t_ref[3 * CI :, at])
        decay = jnp.exp(-jnp.abs(pre))
        act = jnp.maximum(pre, 0.0) + jnp.log1p(decay)
        if -1 <= crow <= CROWS:
            inverse = 1.0 / (1.0 + decay)
            sig = jnp.where(pre >= 0, inverse, decay * inverse)
            sig_ref[2 * (crow + 1)] = sig[:, :128]
            sig_ref[2 * (crow + 1) + 1] = sig[:, 128:]
        side_by_side(a_ref, slice(CA * place, CA * (place + 1)), act[:, :128] + act[:, 128:])
    i, j = grid(256, 256)
    slot = j % SLOT
    end = jnp.where(slot < STRIP, slot, CCOLS - SLOT + slot)
    column = jnp.where(j < 128, j, end)
    means = dot(a_ref[...], jnp.where(i % 128 // 2 == column, 0.25, 0.0).astype(bf16))
    filled = []
    for place in range(CROWS + 2 * UP1):
        value = means[CA * place : CA * (place + 1)]
        x1_ref[place] = value[:, :128]
        filled.append(value[:, 128:])
    put_slots((ends_ref, ends_copy_ref), filled, len(filled))


def coarse_kernel(
    flips, x1_ref, far_ref, near_ref, w_ref, feat_ref, sig_ref, t_ref, z_ref
):
    here = Place(flips)
    turns = coarse_turns(here, CA)
    lane = lanes(CA)
    left, right = both_strips(far_ref, near_ref, here.odd_tile)
    rows = {}
    for row in range(-UP1, CROWS + UP1):
        place = row + UP1
        rows[row] = coarse_row(
            x1_ref[place], left[place // PER], right[place // PER], place % PER
        )
    around = ring(128, 2)
    first = coarse_laps(rows, 1 - UP1, CROWS + UP1 - 1, turns, around, z_ref)
    second = coarse_laps(first, -UP2, CROWS + UP2, turns, around, z_ref)
    second = {row: 2.0 * second[row] - rows[row] for row in second}
    for q, (a, b) in enumerate(PAIRS):
        at = pl.ds(q * 128, 128)
        for k, term in enumerate((rows, first, second)):
            packed = jnp.where(lane < 64, term[a], roll(term[b], 64))
            high, low = halves(packed)
            for m in range(MAPS):
                chans = slice(CH0 * m, CH0 * (m + 1))
                t_ref[m, CH0 * k : CH0 * (k + 1), at] = high[chans]
                t_ref[m, CH0 * (3 + k) : CH0 * (4 + k), at] = low[chans]
    weights = w_ref[...].T
    own = OWN * 128
    sums = []
    for m in range(MAPS):
        pre = dot_halves(weights, t_ref[m, : ORDER * CH0], t_ref[m, ORDER * CH0 :])
        decay = jnp.exp(-jnp.abs(pre))
        inverse = 1.0 / (1.0 + decay)
        sig = jnp.where(pre >= 0, inverse, decay * inverse)
        act = jnp.maximum(pre[:, :own], 0.0) + jnp.log1p(decay[:, :own])
        sums.append(sum(act[:, 128 * q : 128 * (q + 1)] for q in range(OWN)))
        for q in range(len(PAIRS)):
            sig_ref[q, CH1 * m : CH1 * (m + 1)] = sig[:, 128 * q : 128 * (q + 1)]
    total = jnp.sum(jnp.concatenate(sums, axis=0).T, axis=0, keepdims=True)
    feat_ref[...] = jnp.broadcast_to(total, feat_ref.shape)


def gram_kernel(sig_ref, t_ref, ends_ref, ends_copy_ref, gram_ref, s_ref):
    j = lanes(CB) % SLOT
    column = jnp.where(j < STRIP, j, CCOLS - SLOT + j)
    index = jnp.where(lanes(CB) // SLOT % 2 == 0, column, 64 + column)
    ends = jnp.zeros((CB, 128), f32)
    for q in range(len(PAIRS)):
        value = sig_ref[q]
        ends = jnp.where(lanes(CB) // (2 * SLOT) == q, pick(value, index), ends)
        if q < OWN:
            s_ref[:CB, 128 * q : 128 * (q + 1)], s_ref[CB:, 128 * q : 128 * (q + 1)] = halves(value)
    ends = jnp.where(lanes(CB // 2) < 64, ends[: CB // 2], roll(ends[CB // 2 :], 64))
    ends_ref[...] = ends
    ends_copy_ref[...] = ends
    grams = [jnp.zeros((CH0, 128), f32) for _ in range(ORDER)]
    for m in range(MAPS):
        both = dot_nt(t_ref[m, :, : OWN * 128], s_ref[...])
        for k in range(ORDER):
            high = both[CH0 * k : CH0 * (k + 1)]
            low = both[CH0 * (3 + k) : CH0 * (4 + k)]
            value = high[:, :CB] + high[:, CB:] + low[:, :CB]
            grams[k] = jnp.where(lanes(CH0) // CH1 == m, value, grams[k])
    for k in range(ORDER):
        gram_ref[k] = grams[k]


def split_kernel(
    sig1_ref, far_ref, near_ref, shift_ref, labels_ref, out_ref, s_ref, head_ref
):
    here = Place()
    left = before(far_ref[...], near_ref[...], here.odd_tile)
    right = after(far_ref[...], near_ref[...], here.odd_tile)
    left, right = (jnp.concatenate([side, roll(side, 64)], axis=0) for side in (left, right))
    for n, row in enumerate(range(-UP2, CROWS + UP2)):
        q, half = WHERE[row]
        value = coarse_row(roll(sig1_ref[q], 64 * half), left, right, 2 * q + half)
        high, low = halves(value)
        at = pl.ds(n * 128, 128)
        for m in range(MAPS):
            chans = slice(CH1 * m, CH1 * (m + 1))
            s_ref[m, :CH1, at] = high[chans]
            s_ref[m, CH1:, at] = low[chans]
    head_ref[0] = shift_ref[...]
    head_ref[1] = labels_ref[...]
    head_ref[2] = jnp.broadcast_to(out_ref[...], (8, 128))


def back_kernel(
    flips, feat_ref, head_ref, fw_ref, w1_ref, s_ref, gram_ref, sig0_ref, terms_ref,
    logits_ref, grads_ref, d_ref, z_ref,
    *, pooled,
):
    here = Place(flips)
    features = jnp.sum(feat_ref[...], axis=0, keepdims=True) * (1.0 / pooled)
    row8 = lax.broadcasted_iota(jnp.int32, (8, 128), 0)
    apart = jnp.where(lanes(8) // CH1 == row8, jnp.broadcast_to(features, (8, 128)), 0.0)
    fw = jnp.concatenate([fw_ref[...]] * MAPS, axis=0)
    shift, labels, out = head_ref[0], head_ref[1], head_ref[2]
    hidden = jnp.tanh(
        jnp.dot(apart, fw, precision=exact, preferred_element_type=f32) + shift
    )
    logits = jnp.sum(hidden * out, axis=1, keepdims=True)
    logits_ref[...] = jnp.broadcast_to(logits, (8, 128))
    decay = jnp.exp(-jnp.abs(logits))
    dlogit = jnp.where(logits >= 0, 1.0, decay) / (1.0 + decay) - labels
    dhidden = dlogit * out * (1.0 - hidden * hidden)
    dhidden = jnp.concatenate(
        [jnp.broadcast_to(dhidden[m : m + 1], (CH1, 128)) for m in range(MAPS)], axis=0
    )
    dcol = jnp.sum(fw * dhidden, axis=1, keepdims=True) * (1.0 / pooled)
    dfull = jnp.broadcast_to(dcol, (CB, 128))
    drow = jnp.broadcast_to(dfull.T[:1], (CH0, 128))
    coarse = []
    for k in range(ORDER):
        value = gram_ref[k] * drow
        value = value + roll(value, 64)
        coarse.append(value + roll(value, 32))
    weighted = w1_ref[...] * jnp.broadcast_to(drow[:1], w1_ref.shape)
    lane = lanes(w1_ref.shape[0])
    parts = []
    for m in range(MAPS):
        weights = jnp.where(lane // CH1 == m, weighted, 0.0)
        weights = weights + roll(weights, 64)
        high, low = halves(weights + roll(weights, 32))
        parts.append(dot(high[:, : 2 * CH1], s_ref[m]) + dot(low[:, :CH1], s_ref[m, :CH1]))

    def term(k, low, high):
        rows = {}
        for row in range(low, high):
            at = slice(128 * (row + UP2), 128 * (row + UP2 + 1))
            rows[row] = jnp.concatenate([part[CH0 * k : CH0 * (k + 1), at] for part in parts], axis=0)
        return rows

    turns = coarse_turns(here, CA)
    around = ring(128, 2)
    g0 = term(0, -1, CROWS + 1)
    g1 = term(1, 1 - UP2, CROWS + UP2 - 1)
    g2 = term(2, -UP2, CROWS + UP2)
    inner = coarse_laps(g2, 1 - UP2, CROWS + UP2 - 1, turns, around, z_ref)
    inner = {row: g1[row] + 2.0 * inner[row] for row in g1}
    outer = coarse_laps(inner, -1, CROWS + 1, turns, around, z_ref)
    for n, crow in enumerate(range(-1, CROWS + 1)):
        at = slice(CA * n, CA * (n + 1))
        side_by_side(z_ref, at, g0[crow] - g2[crow] + outer[crow])
    i, j = grid(256, 128)
    doubled = jnp.where(i % 128 == j // 2, 0.25, 0.0).astype(bf16)
    spread = dot(z_ref[0 : CA * (CROWS + 2)], doubled)
    for n in range(ROWS + 4):
        value = spread[CA * (n // 2) : CA * (n // 2 + 1)]
        high, low = halves(value * sig0_ref[n])
        at = pl.ds(n * 128, 128)
        d_ref[:CA, at] = high
        d_ref[CA:, at] = low
    both = dot_nt(terms_ref[...], d_ref[:, 2 * 128 : (2 + ROWS) * 128])
    lane = lanes(CI)
    row16 = lax.broadcasted_iota(jnp.int32, (CI, 128), 0)
    same = lane % CA // CH0 == row16 // BINS
    fine = []
    for k in range(ORDER):
        value = jnp.where(same, both[CI * k : CI * (k + 1)], 0.0)
        if k:
            low = both[CI * (2 + k) : CI * (3 + k)]
            value = value + jnp.where(same & (lane < CA), low, 0.0)
        for shift in (64, 32, 16):
            value = value + roll(value, shift)
        for shift in (8, 4):
            value = value + pltpu.roll(value, shift, 0)
        fine.append(value)
    value = jnp.where(row16 // BINS == 0, fine[0], jnp.where(row16 // BINS == 1, fine[1], fine[2]))
    for k in range(ORDER):
        value = jnp.where(lane // CH1 == k, coarse[k], value)
    for n in range(grads_ref.shape[0] // CI):
        grads_ref[CI * n : CI * (n + 1)] = value


def terms_kernel(d_ref, w0_ref, g_ref, ends_ref, ends_copy_ref):
    weights = w0_ref[...]
    index = end_index(2 * CI)
    filled = []
    for n in range(0, ROWS + 4, 2):
        at = slice(128 * n, 128 * (n + 2))
        value = dot_halves(weights, d_ref[:CA, at], d_ref[CA:, at])
        for step in range(2):
            part = value[:, 128 * step : 128 * (step + 1)]
            g_ref[n + step] = part
            filled.append(pick(part[CI:], index))
    put_slots((ends_ref, ends_copy_ref), filled, len(filled))


def saliency_kernel(flips, g_ref, far_ref, near_ref, out_ref, *, pixels):
    here = Place(flips)
    turns = fine_turns(here, CI)
    left, right = both_strips(far_ref, near_ref, here.odd_tile)
    g0, g1, g2, s1, s2 = {}, {}, {}, {}, {}
    for row in range(-2, ROWS + 2):
        value = g_ref[row + 2]
        g0[row], g1[row], g2[row] = (value[CI * k : CI * (k + 1)] for k in range(3))
        strip = fine_strip(left, right, row + 2)
        s1[row], s2[row] = strip[:CI], strip[CI:]
    inner, inner_strip = {}, {}
    for row in range(-1, ROWS + 1):
        value, strip = fine_lap(g2, s2, row, turns, True)
        inner[row] = g1[row] + 2.0 * value
        inner_strip[row] = s1[row] + 2.0 * strip
    for row in range(ROWS):
        outer = fine_lap(inner, inner_strip, row, turns, False)
        out_ref[pl.ds(row, CI, stride=ROWS), :] = (g0[row] - g2[row] + outer) * pixels


def again_kernel(in_ref, out_ref):
    value = in_ref[0:CI]
    for n in range(1, in_ref.shape[0] // CI):
        value = value + in_ref[CI * n : CI * (n + 1)]
    for n in range(out_ref.shape[0] // CI):
        out_ref[CI * n : CI * (n + 1)] = value


def row_again_kernel(in_ref, out_ref):
    out_ref[...] = jnp.broadcast_to(jnp.sum(in_ref[...], axis=0, keepdims=True), out_ref.shape)


def last_kernel(in_ref, fine_ref, coarse_ref, tmp_ref):
    value = in_ref[0:CI]
    for n in range(1, in_ref.shape[0] // CI):
        value = value + in_ref[CI * n : CI * (n + 1)]
    for k in range(ORDER):
        coarse_ref[k] = roll(value, -CH1 * k)[:, :CH1]
    tmp_ref[...] = roll(value, -ORDER * CH1)
    for k in range(ORDER):
        fine_ref[k] = tmp_ref[BINS * k : BINS * (k + 1), :CH0]


def call(kernel, outs, *args, smem=0, scratch=()):
    in_specs = [
        pl.BlockSpec(memory_space=pltpu.SMEM if n < smem else pltpu.VMEM) for n in range(len(args))
    ]
    return pl.pallas_call(
        kernel,
        out_shape=outs,
        in_specs=in_specs,
        out_specs=jax.tree.map(lambda _: pl.BlockSpec(memory_space=pltpu.VMEM), outs),
        scratch_shapes=list(scratch),
        compiler_params=pltpu.CompilerParams(vmem_limit_bytes=32 * 2**20),
    )(*args)


def shape(*dims, dtype=f32):
    return jax.ShapeDtypeStruct(dims, dtype)


def exchange(axis, far_value, near_value):
    count = lax.axis_size(axis)
    far = [(n, (n + (1 if n % 2 else count - 1)) % count) for n in range(count)]
    near = [(n, n + (1 if n % 2 == 0 else -1)) for n in range(count)]
    return lax.ppermute(far_value, axis, far), lax.ppermute(near_value, axis, near)


def share(rows, axes):
    return lax.all_to_all(rows, axes, 0, 0, tiled=True)


def on_device(
    maps, params, labels, edge_flip,
    fine_weight, coarse_weight, feature_weight, param_weight, out_weight,
):
    faces, tiles = lax.axis_size(FACE), lax.axis_size(TILE)
    eye = jnp.eye(MAPS, dtype=f32)
    fine = jnp.einsum("kio,mn->monki", fine_weight, eye)
    fine = fine.transpose(0, 1, 3, 2, 4).reshape(CA, ORDER * CI)
    coarse = coarse_weight.reshape(ORDER * CH0, CH1)
    coarse_backward = jnp.concatenate([coarse] * MAPS, axis=1)
    pad = [(0, 8 - MAPS), (0, 0)]
    shift = jnp.dot(jnp.pad(params, pad), param_weight, precision=exact)
    labels8 = jnp.broadcast_to(jnp.pad(labels.astype(f32)[:, None], pad), (8, 128))

    trade = shape(UP0, CI, COLS)
    own, far, near = call(
        rows_kernel, (shape(ROWS, CI, COLS), trade, trade), maps.reshape(CI * ROWS, COLS),
        scratch=[pltpu.VMEM((CI * ROWS, COLS), f32)],
    )
    far, near = exchange(FACE, far, near)
    trade = shape(groups(ROWS + 2 * UP0), CI, 128)
    far0, near0 = call(ends_kernel, (trade, trade), far, near, own)
    far0, near0 = exchange(TILE, far0, near0)
    crows = CROWS + 2 * UP1
    trade = shape(groups(crows), CA, 128)
    x1, sig0, terms0, far1, near1 = call(
        fine_kernel,
        (
            shape(crows, CA, 128),
            shape(ROWS + 4, CA, 128),
            shape(5 * CI, ROWS * 128, dtype=bf16),
            trade,
            trade,
        ),
        edge_flip, far, near, own, far0, near0, fine,
        smem=1,
        scratch=[
            pltpu.VMEM((6 * CI, 2 * crows * 128), bf16),
            pltpu.VMEM(((ROWS + 2 * UP0) * CI, 256), bf16),
            pltpu.VMEM(((ROWS + 2 * UP0 - 2) * CI, 512), bf16),
            pltpu.VMEM((crows * CA, 256), bf16),
        ],
    )
    far1, near1 = exchange(TILE, far1, near1)
    feats, sig1, terms1 = call(
        coarse_kernel,
        (
            shape(lax.axis_size(FIRST), CB),
            shape(len(PAIRS), CB, 128),
            shape(MAPS, 2 * ORDER * CH0, len(PAIRS) * 128, dtype=bf16),
        ),
        edge_flip, x1, far1, near1, coarse,
        smem=1,
        scratch=[pltpu.VMEM((crows * CA, 256), bf16)],
    )
    feats = share(feats, FIRST)
    feats = call(row_again_kernel, shape(lax.axis_size(SECOND), CB), feats)
    trade = shape(CB // 2, 128)
    far2, near2, grams = call(
        gram_kernel, (trade, trade, shape(ORDER, CH0, 128)), sig1, terms1,
        scratch=[pltpu.VMEM((2 * CB, OWN * 128), bf16)],
    )
    feats = share(feats, SECOND)
    far2, near2 = exchange(TILE, far2, near2)
    pooled = CROWS * faces * CCOLS * tiles
    split1, head = call(
        split_kernel,
        (shape(MAPS, 2 * CH1, (CROWS + 2 * UP2) * 128, dtype=bf16), shape(3, 8, 128)),
        sig1, far2, near2, shift, labels8, out_weight[None],
    )
    logits, grads, dpre0 = call(
        lambda *refs: back_kernel(*refs, pooled=pooled),
        (
            shape(8, 128),
            shape(lax.axis_size(PLANE) * CI, 128),
            shape(2 * CA, (ROWS + 4) * 128, dtype=bf16),
        ),
        edge_flip, feats, head, feature_weight, coarse_backward, split1, grams, sig0, terms0,
        smem=1,
        scratch=[pltpu.VMEM(((CROWS + 2 * UP2) * CA, 256), bf16)],
    )
    grads = share(grads, PLANE)
    trade = shape(groups(ROWS + 4), 2 * CI, 128)
    g, far3, near3 = call(
        terms_kernel, (shape(ROWS + 4, ORDER * CI, 128), trade, trade), dpre0, fine.T
    )
    far3, near3 = exchange(TILE, far3, near3)
    grads = call(again_kernel, shape(lax.axis_size("z") * CI, 128), grads)
    grads = share(grads, "z")
    pixels = float(ROWS * faces * COLS * tiles)
    saliency = call(
        lambda *refs: saliency_kernel(*refs, pixels=pixels),
        shape(CI * ROWS, COLS), edge_flip, g, far3, near3,
        smem=1,
    )
    grad_f, grad_c = call(
        last_kernel, (shape(*fine_weight.shape), shape(*coarse_weight.shape)), grads,
        scratch=[pltpu.VMEM((CI, 128), f32)],
    )
    return (logits[:MAPS, 0], saliency.reshape(maps.shape), grad_f, grad_c)


def solution(mesh):
    faces, tiles = mesh.devices.shape
    sizes = (faces // 2, 2, tiles // 4, 2, 2)
    fine_mesh = jax.sharding.Mesh(mesh.devices.reshape(sizes), ("x", "y_lo", "z", "y_hi", "core"))
    tiled = P(None, None, FACE, TILE)
    return jax.shard_map(
        on_device,
        mesh=fine_mesh,
        in_specs=(tiled, P(), P(), P(), P(), P(), P(), P(), P()),
        out_specs=(P(), tiled, P(), P()),
        check_vma=False,
    )
```
